32 devices in a mesh: lists: 16 (over z, y, x), users: 2 (over core).
Axes of the slice: x: 2, y: 2, z: 4, core: 2. Of those that a mesh axis runs over, the one named last changes fastest.
Arguments:
- user_vectors: bfloat16 [64, 512], P('lists'), may hold values from -6 to 6
- probe_lists: int32 [64, 32], P('lists'), may hold values from 0 to 15, as said below
- list_items: bfloat16 [16, 4096, 512], P('lists', 'users'), may hold values from -6 to 6
- candidate_ids: int32 [16, 512], P('lists'), may hold values from 0 to 65535, as said below
- history: bfloat16 [16, 256, 512], P('lists', 'users'), may hold values from -6 to 6
- history_lengths: int32 [16], P('lists'), may hold values from 1 to 256, as said below
- query_weight: bfloat16 [512, 512], replicated, may hold values from -4 to 4
- key_value_weight: bfloat16 [512, 1024], replicated, may hold values from -4 to 4
- out_weight: bfloat16 [512, 512], replicated, may hold values from -3 to 3
Outputs:
- list_scores: bfloat16 [64, 32, 4096], P('lists', None, 'users')
- ranked: bfloat16 [16, 512, 512], P('lists', 'users')
The draws below stay inside these ranges and needn't reach their ends.
Inputs may be any that keep to these rules, and one draw needn't show every extreme that they name: `probe_lists`: among the probes of the 4 users of one index of lists, no list occurs more than 24 times, and some list exactly 24 times. `candidate_ids`: item i lies in list i // 4096. Among the candidates of the 1 users of one index of lists, at most 48 lie in the same group of 1 lists (list) and the same group of 2048 slots (slot // 2048), and some such pair of groups holds exactly 48. `history_lengths`: the first ranked user has 256 valid events.
All inputs are finite; a program needn't handle non-finite values.
Results may differ from the reference program's by a relative error of at most 0.018.
Values may be sent and summed in bfloat16 or wider, within the bound.
No kernel may reach another device: no remote copies, remote signals or barrier semaphores. Data moves between devices by JAX's collectives and lax.ppermute only.
A program may use at most 128 MiB of HBM per device.

```python
import jax
import jax.numpy as jnp
from jax import lax

D = 512
HEADS = 8
LIST_DEV = 1
ITEMS_LIST = 4096
USER_DEV = 4
PROBES = 32
RANK_DEV = 1
CANDS = 512
LISTS = 16
ITEMS_LOC = 2048
USERS = 64
RANK_USERS = 16
HIST = 256
CAP_L = 24
CAP2 = 48


def capped_bins(key, blocks, count, bins, most):

    def one_block(block_key):
        hot_key, rest_key, order_key = jax.random.split(block_key, 3)
        hot = jax.random.randint(hot_key, (), 0, bins)
        stock = jnp.arange(bins * most, dtype=jnp.int32) // most
        others = jax.random.permutation(rest_key, stock[most:])
        chosen = jnp.concatenate([stock[:most], others[:count - most]])
        chosen = jax.random.permutation(order_key, chosen)
        return (chosen + hot) % bins
    return jax.vmap(one_block)(jax.random.split(key, blocks))


def shared_row(key):
    return jnp.clip(jax.random.normal(key, (D,), jnp.float32), -4.0, 4.0)


def draw_probe_lists(key, part):
    key = jax.random.fold_in(key, 11)
    chosen = capped_bins(key, USERS // USER_DEV, USER_DEV * PROBES, LISTS, CAP_L)
    return chosen.reshape(USERS, PROBES).astype(jnp.int32)


def draw_candidate_ids(key, part):
    key = jax.random.fold_in(key, 23)
    owner_key, list_key, slot_key = jax.random.split(key, 3)
    columns = ITEMS_LIST // ITEMS_LOC
    owners = capped_bins(owner_key, RANK_USERS // RANK_DEV, RANK_DEV * CANDS, LISTS // LIST_DEV * columns, CAP2)
    owners = owners.reshape(RANK_USERS, CANDS)
    row_owner = owners // columns
    col_owner = owners % columns
    sub_list = jax.random.randint(list_key, (RANK_USERS, CANDS), 0, LIST_DEV)
    sub_slot = jax.random.randint(slot_key, (RANK_USERS, CANDS), 0, ITEMS_LOC)
    list_id = row_owner * LIST_DEV + sub_list
    slot_id = col_owner * ITEMS_LOC + sub_slot
    return (list_id * ITEMS_LIST + slot_id).astype(jnp.int32)


def draw_history_lengths(key, part):
    key = jax.random.fold_in(key, 37)
    lengths = jax.random.randint(key, (RANK_USERS,), 1, HIST + 1)
    return lengths.at[0].set(HIST).astype(jnp.int32)


def draw_list_items(key, part):
    key = jax.random.fold_in(key, 53)
    shape = (LISTS, ITEMS_LIST, D)
    values = jnp.clip(jax.random.normal(key, shape, jnp.float32), -6.0, 6.0)
    return values.astype(jnp.bfloat16)


def draw_history(key, part):
    key = jax.random.fold_in(key, 59)
    shape = (RANK_USERS, HIST, D)
    values = jnp.clip(jax.random.normal(key, shape, jnp.float32), -6.0, 6.0)
    return values.astype(jnp.bfloat16)


def draw_query_weight(key, part):
    row = shared_row(key)
    key = jax.random.fold_in(key, 41)
    first = (jnp.arange(D, dtype=jnp.int32) == 0)[:, None]
    rest = jax.random.normal(key, (D, D), jnp.float32) * D ** (-0.5)
    lead = row * D ** (-0.5)
    return jnp.where(first, lead[None, :], rest).astype(jnp.bfloat16)


def draw_key_value_weight(key, part):
    key = jax.random.fold_in(key, 43)
    rest_key = jax.random.fold_in(key, 0)
    values = jax.random.normal(rest_key, (D, 2 * D), jnp.float32) * D ** (-0.5)
    return values.astype(jnp.bfloat16)


def block_levels(own_key, shape, pieces, low, top_value):
    def one(axis_at, shards_of):
        heights = jax.random.uniform(jax.random.fold_in(jax.random.fold_in(own_key, 6), axis_at), (shards_of,), jnp.float32, low / len(pieces), top_value / len(pieces))
        return jnp.repeat(jnp.exp(heights), shape[axis_at] // shards_of).reshape((-1,) + (1,) * (len(shape) - axis_at - 1))

    level = one(*pieces[0])
    for cut in pieces[1:]:
        level = level * one(*cut)
    return level


def normal_values(stream_key, extent, deviation, bound, pieces=(), kind=jnp.bfloat16):
    result = deviation * jax.random.normal(stream_key, extent, jnp.float32)
    if pieces:
        result = result * block_levels(stream_key, extent, pieces, -0.22, 0.18)
    return jnp.clip(result, -bound, bound).astype(kind)


def setup_inputs(seed: int = 0) -> dict:
    seeds = jax.random.split(jax.random.key(seed), 10)
    user_vectors = normal_values(seeds[0], (USERS, D), 1.0, 6.0, ((0, 16),))
    probe_lists = draw_probe_lists(jax.random.fold_in(seeds[9], 71), 0)
    list_items = draw_list_items(jax.random.fold_in(seeds[9], 71), 0)
    candidate_ids = draw_candidate_ids(jax.random.fold_in(seeds[9], 71), 0)
    history = draw_history(jax.random.fold_in(seeds[9], 71), 0)
    history_lengths = draw_history_lengths(jax.random.fold_in(seeds[9], 71), 0)
    query_weight = draw_query_weight(jax.random.fold_in(seeds[9], 71), 0)
    key_value_weight = draw_key_value_weight(jax.random.fold_in(seeds[9], 71), 0)
    out_weight = normal_values(seeds[8], (D, D), 0.5, 3.0)
    return {"user_vectors": user_vectors, "probe_lists": probe_lists, "list_items": list_items, "candidate_ids": candidate_ids, "history": history, "history_lengths": history_lengths, "query_weight": query_weight, "key_value_weight": key_value_weight, "out_weight": out_weight}


def reference(user_vectors, probe_lists, list_items, candidate_ids, history, history_lengths, query_weight, key_value_weight, out_weight):
    width = list_items.shape[2]
    scale = width ** -0.5

    def score_user(packed):
        vector, probes = packed
        blocks = list_items[probes].reshape(-1, width)
        scores = jnp.dot(blocks, vector[:, None], preferred_element_type=jnp.float32)[:, 0]
        return (scores * scale).reshape(probes.shape[0], -1).astype(jnp.bfloat16)

    list_scores = lax.map(score_user, (user_vectors, probe_lists))

    flat_items = list_items.reshape(-1, width)
    head_dim = width // HEADS

    def rank_user(packed):
        ids, events, length = packed
        rows = flat_items[ids]
        queries = (jnp.dot(rows, query_weight, preferred_element_type=jnp.float32) * head_dim ** -0.5).astype(jnp.bfloat16)
        queries = queries.reshape(-1, HEADS, head_dim).astype(jnp.float32)
        pairs = jnp.dot(events, key_value_weight, preferred_element_type=jnp.float32).astype(jnp.bfloat16)
        pairs = pairs.reshape(-1, 2, HEADS, head_dim).astype(jnp.float32)
        scores = jnp.einsum("chd,ehd->che", queries, pairs[:, 0], precision=lax.Precision.HIGHEST)
        valid = (jnp.arange(events.shape[0], dtype=jnp.int32) < length)[None, None, :]
        scores = jnp.where(valid, scores, jnp.float32(-1e30))
        top = jnp.max(scores, axis=-1)
        exponentials = jnp.where(valid, jnp.exp(scores - top[..., None]), jnp.float32(0.0))
        total = jnp.sum(exponentials, axis=-1)
        probs = lax.optimization_barrier(exponentials.astype(jnp.bfloat16)).astype(jnp.float32)
        mixed = jnp.einsum("che,ehd->chd", probs, pairs[:, 1], precision=lax.Precision.HIGHEST)
        attended = (mixed / total[..., None]).reshape(-1, width).astype(jnp.bfloat16)
        return jnp.dot(attended, out_weight, preferred_element_type=jnp.float32).astype(jnp.bfloat16)

    ranked = lax.map(rank_user, (candidate_ids, history, history_lengths))
    return list_scores, ranked
```

```python
import functools

import jax
import jax.numpy as jnp
from jax import lax
from jax.experimental import pallas as pl
from jax.experimental.pallas import tpu as pltpu
from jax.sharding import PartitionSpec as P

HEADS = 8
BASE = 256
LANES = 128
ROW_TILE = 16
VMEM_BYTES = 28 * 1024 * 1024
ALL_VMEM_BYTES = 62 * 1024 * 1024


def round_up(value, step):
    return (value + step - 1) // step * step


def picks(index, count):
    place = lax.broadcasted_iota(jnp.int32, (index.shape[0], count), 1)
    return jnp.where(index == place, 1.0, 0.0).astype(jnp.bfloat16)


def pack_kernel(digits, ids_ref, vectors_ref, pack_ref):
    width = vectors_ref.shape[1]
    vectors = vectors_ref[...].astype(jnp.float32)
    ids = ids_ref[...]
    spans = [slice(start, start + LANES) for start in range(0, width, LANES)]
    rows = [vectors[:, span] for span in spans]
    for digit in range(digits):
        value = ((ids >> (8 * digit)) & (BASE - 1)).astype(jnp.float32)
        rows += [value[:, span] for span in spans]
    count = sum(row.shape[0] for row in rows)
    if pack_ref.shape[1] > count:
        rows.append(jnp.zeros((pack_ref.shape[1] - count, LANES), jnp.float32))
    pack_ref[...] = jnp.broadcast_to(jnp.concatenate(rows, axis=0).astype(jnp.bfloat16)[None], pack_ref.shape)


def earlier(count):
    row = lax.broadcasted_iota(jnp.int32, (count, count), 0)
    column = lax.broadcasted_iota(jnp.int32, (count, count), 1)
    return jnp.where(row < column, 1.0, 0.0).astype(jnp.bfloat16)


def items_kernel(items_hbm, items_ref, sems):
    part = items_ref.shape[0] // sems.shape[0]
    loads = []
    for p in range(sems.shape[0]):
        rows = pl.ds(p * part, part)
        loads.append(pltpu.make_async_copy(items_hbm.at[rows], items_ref.at[rows], sems.at[p]))
        loads[-1].start()
    for load in loads:
        load.wait()


def slot_kernel(n_lists, items_loc, n_users, block, col_ref, ids_ref, probes_ref, slot_ref, probe_ref):
    ids = ids_ref[...]
    cands = ids.shape[1]
    bins = ids // items_loc
    mine = bins % n_users == col_ref[0]
    owner = bins // n_users
    lists = lax.broadcasted_iota(jnp.int32, (n_lists, cands), 0)
    hot = jnp.where((lists == owner) & mine, 1.0, 0.0)
    before = jnp.dot(hot.astype(jnp.bfloat16), earlier(cands), preferred_element_type=jnp.float32)
    rank = jnp.sum(before * hot, axis=0, keepdims=True)
    slot = jnp.where(mine, owner.astype(jnp.float32) * block + rank, -1.0)
    slot_ref[...] = jnp.broadcast_to(slot, slot_ref.shape)
    probes = probes_ref[...].astype(jnp.float32)
    flat = jnp.concatenate([probes[u : u + 1] for u in range(probes.shape[0])], axis=1)
    probe_ref[...] = jnp.broadcast_to(flat, probe_ref.shape)


def pairs_kernel(n_parts, *refs):
    parts, (weight_ref, query_ref, keys_ref, values_ref, turned_ref) = refs[:n_parts], refs[n_parts:]
    events = jnp.concatenate([part[...] for part in parts], axis=0)
    pairs = jnp.dot(events, weight_ref[...], preferred_element_type=jnp.float32)
    heads, _, head_dim = keys_ref.shape
    width = heads * head_dim
    for h in range(heads):
        keys_ref[h] = pairs[:, h * head_dim : (h + 1) * head_dim].astype(jnp.bfloat16)
    values_ref[...] = jnp.transpose(pairs[:, width:]).astype(jnp.bfloat16)
    turned_ref[...] = jnp.transpose(query_ref[...].astype(jnp.float32)).astype(jnp.bfloat16)


def owner_kernel(n_lists, user_dev, digits, cap, scale, base_ref, gathered_ref, items_ref, *refs):
    out_hbm, out_ref, out_sems = refs
    pack_rows = gathered_ref.shape[0] // n_lists
    items_loc, width = items_ref.shape
    spans = width // LANES
    entry = lax.broadcasted_iota(jnp.int32, ((user_dev + digits) * n_lists, 1), 0)
    asker, field = entry % n_lists, entry // n_lists
    unpacked = []
    for span in range(spans):
        line = jnp.where(field < user_dev, span * user_dev + field, (user_dev + field - user_dev) * spans + span)
        unpacked.append(
            jnp.dot(
                picks(asker * pack_rows + line, n_lists * pack_rows),
                gathered_ref[...],
                preferred_element_type=jnp.float32,
            )
        )
    unpacked = jnp.concatenate(unpacked, axis=1)
    ids = jnp.zeros((n_lists, width), jnp.float32)
    for digit in range(digits):
        ids = ids + unpacked[(user_dev + digit) * n_lists : (user_dev + digit + 1) * n_lists] * float(BASE**digit)
    local = ids - base_ref[0].astype(jnp.float32)
    mine = (local >= 0.0) & (local < items_loc)
    hot = jnp.where(mine, 1.0, 0.0).astype(jnp.bfloat16)
    rank = jnp.dot(hot, earlier(width), preferred_element_type=jnp.float32)
    rank = jnp.where(mine, rank, -1.0)
    place = lax.broadcasted_iota(jnp.int32, (cap, width), 0).astype(jnp.float32)
    index = []
    for r in range(n_lists):
        picked = jnp.where(rank[r : r + 1] == place, local[r : r + 1], 0.0)
        index.append(jnp.sum(picked, axis=1, keepdims=True).astype(jnp.int32))
    scores = lax.dot_general(
        unpacked[: user_dev * n_lists].astype(jnp.bfloat16),
        items_ref[...],
        (((1,), (1,)), ((), ())),
        preferred_element_type=jnp.float32,
    )
    scores = (scores * scale).astype(jnp.bfloat16)
    pieces = items_loc // width
    stacked = jnp.concatenate(
        [scores[:, piece * width : (piece + 1) * width] for piece in range(pieces)], axis=0
    )
    kept = out_ref.shape[1] - cap
    entry = lax.broadcasted_iota(jnp.int32, (n_lists * kept, 1), 0)
    wanted = jnp.where(entry % kept < pieces * user_dev, entry % kept * n_lists + entry // kept, -1)
    spread = jnp.dot(
        picks(wanted, stacked.shape[0]), stacked, preferred_element_type=jnp.float32
    ).astype(jnp.bfloat16)
    out_ref[:, cap:, :] = spread.reshape(n_lists, kept, width)
    step = max(1, 256 // cap)
    sends = []
    for number, first in enumerate(range(0, n_lists, step)):
        last = min(n_lists, first + step)
        rows = jnp.dot(
            picks(jnp.concatenate(index[first:last], axis=0), items_loc),
            items_ref[...],
            preferred_element_type=jnp.float32,
        ).astype(jnp.bfloat16)
        out_ref[first:last, :cap, :] = rows.reshape(last - first, cap, width)
        send = pltpu.make_async_copy(out_ref.at[first:last], out_hbm.at[first:last], out_sems.at[number])
        send.start()
        sends.append(send)
    for send in sends:
        send.wait()


def place_kernel(n_users, col_ref, slot_ref, fetched_ref, own_ref, *rest):
    sent_refs, scratch = rest[:-1], rest[-1]
    n_lists, block, width = fetched_ref.shape
    rows = n_lists * block
    share = own_ref.shape[0]
    slot = jnp.transpose(slot_ref[...])[:, :1].astype(jnp.int32)
    scratch[...] = jnp.dot(
        picks(slot, rows), fetched_ref[...].reshape(rows, width), preferred_element_type=jnp.float32
    ).astype(jnp.bfloat16)
    for shift, ref in enumerate((own_ref, *sent_refs)):
        start = (col_ref[0] + shift) % n_users * share
        ref[...] = scratch[pl.ds(pl.multiple_of(start, share), share), :]


def attend_kernel(n_parts, col_ref, length_ref, *refs):
    parts, (keys_ref, values_ref, turned_ref, out_weight_ref, out_ref) = refs[:n_parts], refs[n_parts:]
    heads, events, head_dim = keys_ref.shape
    hist_dev = events // n_parts
    rows = parts[0][...]
    for part in parts[1:]:
        rows = rows + part[...]
    queries = lax.dot_general(
        turned_ref[...], rows, (((1,), (1,)), ((), ())), preferred_element_type=jnp.float32
    )
    queries = (queries * head_dim ** (-0.5)).astype(jnp.bfloat16)
    event = lax.broadcasted_iota(jnp.int32, (events, 1), 0)
    piece = event // hist_dev
    position = (col_ref[0] - piece + n_parts) % n_parts * hist_dev + event % hist_dev
    valid = position < length_ref[0]
    mixed = []
    for h in range(heads):
        span = slice(h * head_dim, (h + 1) * head_dim)
        scores = jnp.dot(keys_ref[h], queries[span], preferred_element_type=jnp.float32)
        scores = jnp.where(valid, scores, -1e30)
        exponentials = jnp.exp(scores - jnp.max(scores, axis=0, keepdims=True))
        total = jnp.sum(exponentials, axis=0, keepdims=True)
        head = jnp.dot(values_ref[span, :], exponentials.astype(jnp.bfloat16), preferred_element_type=jnp.float32)
        mixed.append(head / total)
    attended = jnp.transpose(jnp.concatenate(mixed, axis=0)).astype(jnp.bfloat16)
    out_ref[...] = jnp.dot(attended, out_weight_ref[...], preferred_element_type=jnp.float32).astype(jnp.bfloat16)


def expand_kernel(user_dev, pieces, cap, probes_ref, fetched_ref, out_ref):
    n_lists, block, width = fetched_ref.shape
    kept = block - cap
    rows = n_lists * kept
    returned = fetched_ref[:, cap:, :].reshape(rows, width)
    count = out_ref.shape[0]
    probe = jnp.transpose(probes_ref[...])[:, :1].astype(jnp.int32)
    user = lax.broadcasted_iota(jnp.int32, (count, 1), 0) // (count // user_dev)
    for piece in range(pieces):
        wanted = probe * kept + piece * user_dev + user
        out_ref[:, piece * width : (piece + 1) * width] = jnp.dot(
            picks(wanted, rows), returned, preferred_element_type=jnp.float32
        ).astype(jnp.bfloat16)


SMEM = pl.BlockSpec(memory_space=pltpu.SMEM)
VMEM = pl.BlockSpec(memory_space=pltpu.VMEM)
HBM = pl.BlockSpec(memory_space=pltpu.HBM)
PARAMS = pltpu.CompilerParams(vmem_limit_bytes=VMEM_BYTES)


def shards(
    user_vectors,
    probe_lists,
    list_items,
    candidate_ids,
    history,
    history_lengths,
    query_weight,
    key_value_weight,
    out_weight,
):
    n_lists = lax.axis_size("lists")
    n_users = lax.axis_size("users")
    _, items_loc, width = list_items.shape
    user_dev, probes = probe_lists.shape
    _, cands = candidate_ids.shape
    bf16 = jnp.bfloat16
    cap = max(2, 3 * cands // (n_lists * n_users))
    cap = round_up(cap, ROW_TILE)
    kept = round_up(items_loc // width * user_dev, ROW_TILE)
    share = cands // n_users
    pieces = items_loc // width
    digits = 1
    while BASE**digits < n_lists * n_users * items_loc:
        digits += 1
    pack_rows = round_up((user_dev + digits) * (width // LANES), 8)
    line = lax.axis_index("lists").astype(jnp.int32)
    col = lax.axis_index("users").astype(jnp.int32)
    col_arg = col.reshape(1)
    base_arg = ((line * n_users + col) * items_loc).reshape(1)

    flat_items = list_items.reshape(items_loc, width)
    pack = pl.pallas_call(
        functools.partial(pack_kernel, digits),
        out_shape=jax.ShapeDtypeStruct((n_lists, pack_rows, LANES), bf16),
        in_specs=[VMEM, VMEM],
        out_specs=VMEM,
        compiler_params=pltpu.CompilerParams(vmem_limit_bytes=ALL_VMEM_BYTES),
    )(candidate_ids, user_vectors)
    gathered = lax.all_to_all(pack, "lists", split_axis=0, concat_axis=0, tiled=True)
    gathered = gathered.reshape(n_lists * pack_rows, LANES)

    items = pl.pallas_call(
        items_kernel,
        out_shape=jax.ShapeDtypeStruct((items_loc, width), bf16),
        in_specs=[HBM],
        out_specs=VMEM,
        scratch_shapes=[pltpu.SemaphoreType.DMA((4,))],
        compiler_params=PARAMS,
    )(flat_items)
    gathered, items = lax.optimization_barrier((gathered, items))

    slot, probe_row = pl.pallas_call(
        functools.partial(slot_kernel, n_lists, items_loc, n_users, cap + kept),
        out_shape=(
            jax.ShapeDtypeStruct((8, cands), jnp.float32),
            jax.ShapeDtypeStruct((8, user_dev * probes), jnp.float32),
        ),
        in_specs=[SMEM, VMEM, VMEM],
        out_specs=(VMEM, VMEM),
        compiler_params=PARAMS,
    )(col_arg, candidate_ids, probe_lists)

    events = history.reshape(-1, width)
    hist = [events]
    for shift in range(1, n_users):
        hist.append(lax.ppermute(events, "users", [(i, (i + shift) % n_users) for i in range(n_users)]))
    total_events = n_users * events.shape[0]
    keys, values, turned = pl.pallas_call(
        functools.partial(pairs_kernel, n_users),
        out_shape=(
            jax.ShapeDtypeStruct((HEADS, total_events, width // HEADS), bf16),
            jax.ShapeDtypeStruct((width, total_events), bf16),
            jax.ShapeDtypeStruct((width, width), bf16),
        ),
        in_specs=[VMEM] * (n_users + 2),
        out_specs=(VMEM, VMEM, VMEM),
        compiler_params=PARAMS,
    )(*hist, key_value_weight, query_weight)

    step = max(1, 256 // cap)
    answers = pl.pallas_call(
        functools.partial(owner_kernel, n_lists, user_dev, digits, cap, width ** (-0.5)),
        out_shape=jax.ShapeDtypeStruct((n_lists, cap + kept, width), bf16),
        in_specs=[SMEM, VMEM, VMEM],
        out_specs=pl.BlockSpec(memory_space=pl.ANY),
        scratch_shapes=[
            pltpu.VMEM((n_lists, cap + kept, width), bf16),
            pltpu.SemaphoreType.DMA((-(-n_lists // step),)),
        ],
        compiler_params=PARAMS,
    )(base_arg, gathered, items)
    fetched = lax.all_to_all(answers, "lists", split_axis=0, concat_axis=0, tiled=True)
    fetched, slot, probe_row, keys, values, turned = lax.optimization_barrier(
        (fetched, slot, probe_row, keys, values, turned)
    )

    placed = pl.pallas_call(
        functools.partial(place_kernel, n_users),
        out_shape=tuple(jax.ShapeDtypeStruct((share, width), bf16) for _ in range(n_users)),
        in_specs=[SMEM, VMEM, VMEM],
        out_specs=tuple(VMEM for _ in range(n_users)),
        scratch_shapes=[pltpu.VMEM((cands, width), bf16)],
        compiler_params=PARAMS,
    )(col_arg, slot, fetched)
    parts = [placed[0]]
    for shift in range(1, n_users):
        parts.append(
            lax.ppermute(placed[shift], "users", [(i, (i + shift) % n_users) for i in range(n_users)])
        )
    ranked = pl.pallas_call(
        functools.partial(attend_kernel, n_users),
        out_shape=jax.ShapeDtypeStruct((share, width), bf16),
        in_specs=[SMEM, SMEM] + [VMEM] * (n_users + 4),
        out_specs=VMEM,
        compiler_params=PARAMS,
    )(col_arg, history_lengths, *parts, keys, values, turned, out_weight)

    list_scores = pl.pallas_call(
        functools.partial(expand_kernel, user_dev, pieces, cap),
        out_shape=jax.ShapeDtypeStruct((user_dev * probes, items_loc), bf16),
        in_specs=[VMEM, VMEM],
        out_specs=VMEM,
        compiler_params=PARAMS,
    )(probe_row, fetched)
    return (list_scores.reshape(user_dev, probes, items_loc), ranked.reshape(1, share, width))


def solution(mesh):
    placed = (
        P("lists", None),
        P("lists", None),
        P("lists", "users", None),
        P("lists", None),
        P("lists", "users", None),
        P("lists"),
        P(),
        P(),
        P(),
    )
    return jax.shard_map(
        shards,
        mesh=mesh,
        in_specs=placed,
        out_specs=(P("lists", None, "users"), P("lists", "users", None)),
        check_vma=False,
    )
```

```python
import functools

import jax
import jax.numpy as jnp
from jax import lax
from jax.experimental import pallas as pl
from jax.experimental.pallas import tpu as pltpu
from jax.sharding import PartitionSpec as P

HEADS = 8
BASE = 256
LANES = 128
ROW_TILE = 16
VMEM_BYTES = 28 * 1024 * 1024
ALL_VMEM_BYTES = 62 * 1024 * 1024


def round_up(value, step):
    return (value + step - 1) // step * step


def picks(index, count):
    place = lax.broadcasted_iota(jnp.int32, (index.shape[0], count), 1)
    return jnp.where(index == place, 1.0, 0.0).astype(jnp.bfloat16)


def pack_kernel(digits, ids_ref, vectors_ref, pack_ref):
    width = vectors_ref.shape[1]
    vectors = vectors_ref[...].astype(jnp.float32)
    ids = ids_ref[...]
    spans = [slice(start, start + LANES) for start in range(0, width, LANES)]
    rows = [vectors[:, span] for span in spans]
    for digit in range(digits):
        value = ((ids >> (8 * digit)) & (BASE - 1)).astype(jnp.float32)
        rows += [value[:, span] for span in spans]
    count = sum(row.shape[0] for row in rows)
    if pack_ref.shape[1] > count:
        rows.append(jnp.zeros((pack_ref.shape[1] - count, LANES), jnp.float32))
    pack_ref[...] = jnp.broadcast_to(jnp.concatenate(rows, axis=0).astype(jnp.bfloat16)[None], pack_ref.shape)


def earlier(count):
    row = lax.broadcasted_iota(jnp.int32, (count, count), 0)
    column = lax.broadcasted_iota(jnp.int32, (count, count), 1)
    return jnp.where(row < column, 1.0, 0.0).astype(jnp.bfloat16)


def items_kernel(items_hbm, items_ref, sems):
    part = items_ref.shape[0] // sems.shape[0]
    loads = []
    for p in range(sems.shape[0]):
        rows = pl.ds(p * part, part)
        loads.append(pltpu.make_async_copy(items_hbm.at[rows], items_ref.at[rows], sems.at[p]))
        loads[-1].start()
    for load in loads:
        load.wait()


def unpack(gathered_ref, n_lists, user_dev, digits, turn):
    pack_rows = gathered_ref.shape[0] // n_lists
    spans = pack_rows // (user_dev + digits)
    entry = lax.broadcasted_iota(jnp.int32, ((user_dev + digits) * n_lists, 1), 0)
    asker, field = (entry % n_lists) ^ turn, entry // n_lists
    fields = jnp.concatenate(
        [
            jnp.dot(
                picks(
                    asker * pack_rows
                    + jnp.where(field < user_dev, span * user_dev + field, field * spans + span),
                    n_lists * pack_rows,
                ),
                gathered_ref[...],
                preferred_element_type=jnp.float32,
            )
            for span in range(spans)
        ],
        axis=1,
    )
    ids = jnp.zeros((n_lists, fields.shape[1]), jnp.float32)
    for digit in range(digits):
        ids = ids + fields[(user_dev + digit) * n_lists : (user_dev + digit + 1) * n_lists] * float(BASE**digit)
    return fields[: user_dev * n_lists], ids


def asked(ids, base, items_loc, first, count):
    local = ids - base
    mine = (local >= 0.0) & (local < items_loc)
    hot = jnp.where(mine, 1.0, 0.0).astype(jnp.bfloat16)
    rank = jnp.dot(hot, earlier(ids.shape[1]), preferred_element_type=jnp.float32)
    rank = jnp.where(mine, rank, -1.0)
    place = lax.broadcasted_iota(jnp.int32, (count, ids.shape[1]), 0).astype(jnp.float32) + float(first)
    index = []
    for r in range(ids.shape[0]):
        picked = jnp.where(rank[r : r + 1] == place, local[r : r + 1] + 1.0, 0.0)
        index.append(jnp.sum(picked, axis=1, keepdims=True).astype(jnp.int32) - 1)
    return index


def slot_kernel(n_lists, items_loc, n_users, block, place_ref, ids_ref, slot_ref):
    ids = ids_ref[...]
    cands = ids.shape[1]
    bins = ids // items_loc
    mine = bins % n_users == place_ref[1]
    owner = bins // n_users
    lists = lax.broadcasted_iota(jnp.int32, (n_lists, cands), 0)
    hot = jnp.where((lists == owner) & mine, 1.0, 0.0)
    before = jnp.dot(hot.astype(jnp.bfloat16), earlier(cands), preferred_element_type=jnp.float32)
    rank = jnp.sum(before * hot, axis=0, keepdims=True)
    slot = owner.astype(jnp.float32) * block + rank
    slot_ref[...] = jnp.broadcast_to(jnp.where(mine, slot, -1.0), slot_ref.shape)


def pairs_kernel(n_parts, place_ref, length_ref, *refs):
    parts, (weight_ref, query_ref, keys_ref, values_ref, turned_ref) = refs[:n_parts], refs[n_parts:]
    history = jnp.concatenate([part[...] for part in parts], axis=0)
    pairs = jnp.dot(history, weight_ref[...], preferred_element_type=jnp.float32)
    heads, events, features = keys_ref.shape
    head_dim = features - ROW_TILE
    width = heads * head_dim
    hist_dev = events // n_parts
    event = lax.broadcasted_iota(jnp.int32, (events, ROW_TILE), 0)
    feature = lax.broadcasted_iota(jnp.int32, (events, ROW_TILE), 1)
    position = (place_ref[1] - event // hist_dev + n_parts) % n_parts * hist_dev + event % hist_dev
    mask = jnp.where((position >= length_ref[0]) & (feature == 0), -1e30, 0.0)
    for h in range(heads):
        keys = pairs[:, h * head_dim : (h + 1) * head_dim]
        keys_ref[h] = jnp.concatenate([keys, mask], axis=1).astype(jnp.bfloat16)
    values_ref[...] = jnp.transpose(pairs[:, width:]).astype(jnp.bfloat16)
    turned_ref[...] = jnp.transpose(query_ref[...].astype(jnp.float32)).astype(jnp.bfloat16)


def owner_kernel(n_lists, n_users, user_dev, digits, cap, scale, place_ref, gathered_ref, items_ref, *refs):
    out_hbm, out_ref, out_sems = refs
    items_loc, width = items_ref.shape
    vectors, ids = unpack(gathered_ref, n_lists, user_dev, digits, 0)
    base = ((place_ref[0] * n_users + place_ref[1]) * items_loc).astype(jnp.float32)
    index = asked(ids, base, items_loc, 0, cap)
    scores = lax.dot_general(
        vectors.astype(jnp.bfloat16),
        items_ref[...],
        (((1,), (1,)), ((), ())),
        preferred_element_type=jnp.float32,
    )
    scores = (scores * scale).astype(jnp.bfloat16)
    pieces = items_loc // width
    stacked = jnp.concatenate(
        [scores[:, piece * width : (piece + 1) * width] for piece in range(pieces)], axis=0
    )
    kept = out_ref.shape[1] - cap
    entry = lax.broadcasted_iota(jnp.int32, (n_lists * kept, 1), 0)
    wanted = jnp.where(entry % kept < pieces * user_dev, entry % kept * n_lists + entry // kept, -1)
    spread = jnp.dot(
        picks(wanted, stacked.shape[0]), stacked, preferred_element_type=jnp.float32
    ).astype(jnp.bfloat16)
    out_ref[:, cap:, :] = spread.reshape(n_lists, kept, width)
    step = max(1, 256 // cap)
    sends = []
    for number, first in enumerate(range(0, n_lists, step)):
        last = min(n_lists, first + step)
        rows = jnp.dot(
            picks(jnp.concatenate(index[first:last], axis=0), items_loc),
            items_ref[...],
            preferred_element_type=jnp.float32,
        ).astype(jnp.bfloat16)
        out_ref[first:last, :cap, :] = rows.reshape(last - first, cap, width)
        send = pltpu.make_async_copy(out_ref.at[first:last], out_hbm.at[first:last], out_sems.at[number])
        send.start()
        sends.append(send)
    for send in sends:
        send.wait()


def place_kernel(n_users, place_ref, slot_ref, fetched_ref, *refs):
    share_refs, scratch = refs[:-1], refs[-1]
    n_lists, block, width = fetched_ref.shape
    fetched = fetched_ref[...].reshape(n_lists * block, width)
    share = share_refs[0].shape[0]
    slot = jnp.transpose(slot_ref[...])[:, :1].astype(jnp.int32)
    scratch[...] = jnp.dot(
        picks(slot, fetched.shape[0]), fetched, preferred_element_type=jnp.float32
    ).astype(jnp.bfloat16)
    for shift, ref in enumerate(share_refs):
        start = (place_ref[1] + shift) % n_users * share
        ref[...] = scratch[pl.ds(pl.multiple_of(start, share), share), :]


def attend_kernel(n_parts, *refs):
    parts, (keys_ref, values_ref, turned_ref, out_weight_ref, out_ref) = refs[:n_parts], refs[n_parts:]
    heads, events, features = keys_ref.shape
    head_dim = features - ROW_TILE
    rows = parts[0][...]
    for part in parts[1:]:
        rows = rows + part[...]
    queries = lax.dot_general(
        turned_ref[...], rows, (((1,), (1,)), ((), ())), preferred_element_type=jnp.float32
    )
    queries = (queries * head_dim ** (-0.5)).astype(jnp.bfloat16)
    feature = lax.broadcasted_iota(jnp.int32, (ROW_TILE, rows.shape[0]), 0)
    one = jnp.where(feature == 0, 1.0, 0.0).astype(jnp.bfloat16)

    def score(h):
        query = jnp.concatenate([queries[h * head_dim : (h + 1) * head_dim], one], axis=0)
        return jnp.dot(keys_ref[h], query, preferred_element_type=jnp.float32)

    ahead = [score(h) for h in range(min(2, heads))]
    mixed = []
    for h in range(heads):
        if h + 2 < heads:
            ahead.append(score(h + 2))
        exponentials = jnp.exp(ahead[h] - jnp.max(ahead[h], axis=0, keepdims=True))
        total = jnp.sum(exponentials, axis=0, keepdims=True)
        span = slice(h * head_dim, (h + 1) * head_dim)
        head = jnp.dot(values_ref[span, :], exponentials.astype(jnp.bfloat16), preferred_element_type=jnp.float32)
        mixed.append(head / total)
    attended = jnp.transpose(jnp.concatenate(mixed, axis=0)).astype(jnp.bfloat16)
    out_ref[...] = jnp.dot(attended, out_weight_ref[...], preferred_element_type=jnp.float32).astype(jnp.bfloat16)


def expand_kernel(user_dev, pieces, cap, probes_ref, fetched_ref, out_hbm, out_ref, sems):
    n_lists, block, width = fetched_ref.shape
    kept = block - cap
    rows = n_lists * kept
    returned = fetched_ref[:, cap:, :].reshape(rows, width)
    count = out_ref.shape[0]
    probes = probes_ref[...].astype(jnp.float32)
    flat = jnp.concatenate([probes[u : u + 1] for u in range(user_dev)], axis=1)
    probe = jnp.transpose(jnp.broadcast_to(flat, (8, count)))[:, :1].astype(jnp.int32)
    user = lax.broadcasted_iota(jnp.int32, (count, 1), 0) // (count // user_dev)
    sends = []
    for piece in range(pieces):
        wanted = probe * kept + piece * user_dev + user
        span = pl.ds(piece * width, width)
        out_ref[:, span] = jnp.dot(picks(wanted, rows), returned, preferred_element_type=jnp.float32).astype(
            jnp.bfloat16
        )
        sends.append(pltpu.make_async_copy(out_ref.at[:, span], out_hbm.at[:, span], sems.at[piece]))
        sends[-1].start()
    for send in sends:
        send.wait()


SMEM = pl.BlockSpec(memory_space=pltpu.SMEM)
VMEM = pl.BlockSpec(memory_space=pltpu.VMEM)
HBM = pl.BlockSpec(memory_space=pltpu.HBM)
PARAMS = pltpu.CompilerParams(vmem_limit_bytes=VMEM_BYTES)


def shards(
    user_vectors,
    probe_lists,
    list_items,
    candidate_ids,
    history,
    history_lengths,
    query_weight,
    key_value_weight,
    out_weight,
):
    n_lists = lax.axis_size("lists")
    n_users = lax.axis_size("users")
    _, items_loc, width = list_items.shape
    user_dev, probes = probe_lists.shape
    _, cands = candidate_ids.shape
    bf16 = jnp.bfloat16
    cap = max(2, 3 * cands // (n_lists * n_users))
    cap = round_up(cap, ROW_TILE)
    kept = round_up(items_loc // width * user_dev, ROW_TILE)
    share = cands // n_users
    pieces = items_loc // width
    digits = 1
    while BASE**digits < n_lists * n_users * items_loc:
        digits += 1
    pack_rows = round_up((user_dev + digits) * (width // LANES), 8)
    line = lax.axis_index("lists").astype(jnp.int32)
    col = lax.axis_index("users").astype(jnp.int32)
    place_arg = jnp.stack([line, col])
    block = cap + kept

    flat_items = list_items.reshape(items_loc, width)
    pack = pl.pallas_call(
        functools.partial(pack_kernel, digits),
        out_shape=jax.ShapeDtypeStruct((n_lists, pack_rows, LANES), bf16),
        in_specs=[VMEM, VMEM],
        out_specs=VMEM,
        compiler_params=pltpu.CompilerParams(vmem_limit_bytes=ALL_VMEM_BYTES),
    )(candidate_ids, user_vectors)
    gathered = lax.all_to_all(pack, "lists", split_axis=0, concat_axis=0, tiled=True)
    gathered = gathered.reshape(n_lists * pack_rows, LANES)

    items = pl.pallas_call(
        items_kernel,
        out_shape=jax.ShapeDtypeStruct((items_loc, width), bf16),
        in_specs=[HBM],
        out_specs=VMEM,
        scratch_shapes=[pltpu.SemaphoreType.DMA((4,))],
        compiler_params=PARAMS,
    )(flat_items)
    gathered, items = lax.optimization_barrier((gathered, items))

    events = history.reshape(-1, width)
    hist = [events]
    for shift in range(1, n_users):
        hist.append(lax.ppermute(events, "users", [(i, (i + shift) % n_users) for i in range(n_users)]))
    total_events = n_users * events.shape[0]
    keys, values, turned = pl.pallas_call(
        functools.partial(pairs_kernel, n_users),
        out_shape=(
            jax.ShapeDtypeStruct((HEADS, total_events, width // HEADS + ROW_TILE), bf16),
            jax.ShapeDtypeStruct((width, total_events), bf16),
            jax.ShapeDtypeStruct((width, width), bf16),
        ),
        in_specs=[SMEM, SMEM] + [VMEM] * (n_users + 2),
        out_specs=(VMEM, VMEM, VMEM),
        compiler_params=PARAMS,
    )(place_arg, history_lengths, *hist, key_value_weight, query_weight)

    step = max(1, 256 // cap)
    answers = pl.pallas_call(
        functools.partial(owner_kernel, n_lists, n_users, user_dev, digits, cap, width ** (-0.5)),
        out_shape=jax.ShapeDtypeStruct((n_lists, block, width), bf16),
        in_specs=[SMEM, VMEM, VMEM],
        out_specs=pl.BlockSpec(memory_space=pl.ANY),
        scratch_shapes=[
            pltpu.VMEM((n_lists, block, width), bf16),
            pltpu.SemaphoreType.DMA((-(-n_lists // step),)),
        ],
        compiler_params=PARAMS,
    )(place_arg, gathered, items)
    fetched = lax.all_to_all(answers, "lists", split_axis=0, concat_axis=0, tiled=True)

    slot = pl.pallas_call(
        functools.partial(slot_kernel, n_lists, items_loc, n_users, block),
        out_shape=jax.ShapeDtypeStruct((8, cands), jnp.float32),
        in_specs=[SMEM, VMEM],
        out_specs=VMEM,
        compiler_params=PARAMS,
    )(place_arg, candidate_ids)
    fetched, slot, keys, values, turned = lax.optimization_barrier((fetched, slot, keys, values, turned))

    placed = pl.pallas_call(
        functools.partial(place_kernel, n_users),
        out_shape=tuple(jax.ShapeDtypeStruct((share, width), bf16) for _ in range(n_users)),
        in_specs=[SMEM, VMEM, VMEM],
        out_specs=tuple(VMEM for _ in range(n_users)),
        scratch_shapes=[pltpu.VMEM((cands, width), bf16)],
        compiler_params=PARAMS,
    )(place_arg, slot, fetched)
    parts = [placed[0]]
    for shift in range(1, n_users):
        parts.append(
            lax.ppermute(placed[shift], "users", [(i, (i + shift) % n_users) for i in range(n_users)])
        )
    ranked = pl.pallas_call(
        functools.partial(attend_kernel, n_users),
        out_shape=jax.ShapeDtypeStruct((share, width), bf16),
        in_specs=[VMEM] * (n_users + 4),
        out_specs=VMEM,
        compiler_params=PARAMS,
    )(*parts, keys, values, turned, out_weight)

    list_scores = pl.pallas_call(
        functools.partial(expand_kernel, user_dev, pieces, cap),
        out_shape=jax.ShapeDtypeStruct((user_dev * probes, items_loc), bf16),
        in_specs=[VMEM, VMEM],
        out_specs=pl.BlockSpec(memory_space=pl.ANY),
        scratch_shapes=[
            pltpu.VMEM((user_dev * probes, items_loc), bf16),
            pltpu.SemaphoreType.DMA((pieces,)),
        ],
        compiler_params=PARAMS,
    )(probe_lists, fetched)
    return (list_scores.reshape(user_dev, probes, items_loc), ranked.reshape(1, share, width))


def solution(mesh):
    placed = (
        P("lists", None),
        P("lists", None),
        P("lists", "users", None),
        P("lists", None),
        P("lists", "users", None),
        P("lists"),
        P(),
        P(),
        P(),
    )
    return jax.shard_map(
        shards,
        mesh=mesh,
        in_specs=placed,
        out_specs=(P("lists", None, "users"), P("lists", "users", None)),
        check_vma=False,
    )
```

```python
import functools

import jax
import jax.numpy as jnp
from jax import lax
from jax.experimental import pallas as pl
from jax.experimental.pallas import tpu as pltpu
from jax.sharding import PartitionSpec as P

HEADS = 8
BASE = 256
LANES = 128
ROW_TILE = 16
VMEM_BYTES = 28 * 1024 * 1024
ALL_VMEM_BYTES = 62 * 1024 * 1024


def round_up(value, step):
    return (value + step - 1) // step * step


def picks(index, count):
    place = lax.broadcasted_iota(jnp.int32, (index.shape[0], count), 1)
    return jnp.where(index == place, 1.0, 0.0).astype(jnp.bfloat16)


def pack_kernel(digits, ids_ref, vectors_ref, pack_ref):
    width = vectors_ref.shape[1]
    vectors = vectors_ref[...].astype(jnp.float32)
    ids = ids_ref[...]
    spans = [slice(start, start + LANES) for start in range(0, width, LANES)]
    rows = [vectors[:, span] for span in spans]
    for digit in range(digits):
        value = ((ids >> (8 * digit)) & (BASE - 1)).astype(jnp.float32)
        rows += [value[:, span] for span in spans]
    count = sum(row.shape[0] for row in rows)
    if pack_ref.shape[1] > count:
        rows.append(jnp.zeros((pack_ref.shape[1] - count, LANES), jnp.float32))
    pack_ref[...] = jnp.broadcast_to(jnp.concatenate(rows, axis=0).astype(jnp.bfloat16)[None], pack_ref.shape)


def earlier(count):
    row = lax.broadcasted_iota(jnp.int32, (count, count), 0)
    column = lax.broadcasted_iota(jnp.int32, (count, count), 1)
    return jnp.where(row < column, 1.0, 0.0).astype(jnp.bfloat16)


def unpack(gathered_ref, n_lists, user_dev, digits, turn):
    pack_rows = gathered_ref.shape[0] // n_lists
    spans = pack_rows // (user_dev + digits)
    entry = lax.broadcasted_iota(jnp.int32, ((user_dev + digits) * n_lists, 1), 0)
    asker, field = (entry % n_lists) ^ turn, entry // n_lists
    fields = jnp.concatenate(
        [
            jnp.dot(
                picks(
                    asker * pack_rows
                    + jnp.where(field < user_dev, span * user_dev + field, field * spans + span),
                    n_lists * pack_rows,
                ),
                gathered_ref[...],
                preferred_element_type=jnp.float32,
            )
            for span in range(spans)
        ],
        axis=1,
    )
    ids = jnp.zeros((n_lists, fields.shape[1]), jnp.float32)
    for digit in range(digits):
        ids = ids + fields[(user_dev + digit) * n_lists : (user_dev + digit + 1) * n_lists] * float(BASE**digit)
    return fields[: user_dev * n_lists], ids


def asked(ids, base, items_loc, first, count):
    local = ids - base
    mine = (local >= 0.0) & (local < items_loc)
    hot = jnp.where(mine, 1.0, 0.0).astype(jnp.bfloat16)
    rank = jnp.dot(hot, earlier(ids.shape[1]), preferred_element_type=jnp.float32)
    rank = jnp.where(mine, rank, -1.0)
    place = lax.broadcasted_iota(jnp.int32, (count, ids.shape[1]), 0).astype(jnp.float32) + float(first)
    index = []
    for r in range(ids.shape[0]):
        picked = jnp.where(rank[r : r + 1] == place, local[r : r + 1] + 1.0, 0.0)
        index.append(jnp.sum(picked, axis=1, keepdims=True).astype(jnp.int32) - 1)
    return index


def early_kernel(n_lists, n_users, block, col_ref, ids_ref, probes_ref, items_hbm, known_ref, items_ref, sems):
    items_loc = items_ref.shape[0]
    part = items_loc // sems.shape[0]
    loads = []
    for p in range(sems.shape[0]):
        span = pl.ds(p * part, part)
        loads.append(pltpu.make_async_copy(items_hbm.at[span], items_ref.at[span], sems.at[p]))
        loads[-1].start()
    ids = ids_ref[...]
    cands = ids.shape[1]
    bins = ids // items_loc
    mine = bins % n_users == col_ref[0]
    owner = bins // n_users
    lists = lax.broadcasted_iota(jnp.int32, (n_lists, cands), 0)
    hot = jnp.where((lists == owner) & mine, 1.0, 0.0)
    before = jnp.dot(hot.astype(jnp.bfloat16), earlier(cands), preferred_element_type=jnp.float32)
    rank = jnp.sum(before * hot, axis=0, keepdims=True)
    slot = jnp.where(mine, owner.astype(jnp.float32) * block + rank, -1.0)
    probes = probes_ref[...].astype(jnp.float32)
    known = jnp.concatenate([slot] + [probes[u : u + 1] for u in range(probes.shape[0])], axis=1)
    known_ref[...] = jnp.broadcast_to(known, known_ref.shape)
    for load in loads:
        load.wait()


def pairs_kernel(n_parts, col_ref, length_ref, *refs):
    parts, (weight_ref, query_ref, keys_ref, values_ref, turned_ref) = refs[:n_parts], refs[n_parts:]
    history = jnp.concatenate([part[...] for part in parts], axis=0)
    pairs = jnp.dot(history, weight_ref[...], preferred_element_type=jnp.float32)
    heads, events, features = keys_ref.shape
    head_dim = features - ROW_TILE
    width = heads * head_dim
    hist_dev = events // n_parts
    event = lax.broadcasted_iota(jnp.int32, (events, ROW_TILE), 0)
    feature = lax.broadcasted_iota(jnp.int32, (events, ROW_TILE), 1)
    position = (col_ref[0] - event // hist_dev + n_parts) % n_parts * hist_dev + event % hist_dev
    mask = jnp.where((position >= length_ref[0]) & (feature == 0), -1e30, 0.0)
    for h in range(heads):
        keys = pairs[:, h * head_dim : (h + 1) * head_dim]
        keys_ref[h] = jnp.concatenate([keys, mask], axis=1).astype(jnp.bfloat16)
    values_ref[...] = jnp.transpose(pairs[:, width:]).astype(jnp.bfloat16)
    turned_ref[...] = jnp.transpose(query_ref[...].astype(jnp.float32)).astype(jnp.bfloat16)


def owner_kernel(n_lists, user_dev, digits, cap, scale, base_ref, gathered_ref, items_ref, *refs):
    out_hbm, out_ref, out_sems = refs
    items_loc, width = items_ref.shape
    vectors, ids = unpack(gathered_ref, n_lists, user_dev, digits, 0)
    index = asked(ids, base_ref[0].astype(jnp.float32), items_loc, 0, cap)
    scores = lax.dot_general(
        vectors.astype(jnp.bfloat16),
        items_ref[...],
        (((1,), (1,)), ((), ())),
        preferred_element_type=jnp.float32,
    )
    scores = (scores * scale).astype(jnp.bfloat16)
    pieces = items_loc // width
    stacked = jnp.concatenate(
        [scores[:, piece * width : (piece + 1) * width] for piece in range(pieces)], axis=0
    )
    kept = out_ref.shape[1] - cap
    entry = lax.broadcasted_iota(jnp.int32, (n_lists * kept, 1), 0)
    wanted = jnp.where(entry % kept < pieces * user_dev, entry % kept * n_lists + entry // kept, -1)
    spread = jnp.dot(
        picks(wanted, stacked.shape[0]), stacked, preferred_element_type=jnp.float32
    ).astype(jnp.bfloat16)
    out_ref[:, cap:, :] = spread.reshape(n_lists, kept, width)
    step = max(1, 256 // cap)
    sends = []
    for number, first in enumerate(range(0, n_lists, step)):
        last = min(n_lists, first + step)
        rows = jnp.dot(
            picks(jnp.concatenate(index[first:last], axis=0), items_loc),
            items_ref[...],
            preferred_element_type=jnp.float32,
        ).astype(jnp.bfloat16)
        out_ref[first:last, :cap, :] = rows.reshape(last - first, cap, width)
        send = pltpu.make_async_copy(out_ref.at[first:last], out_hbm.at[first:last], out_sems.at[number])
        send.start()
        sends.append(send)
    for send in sends:
        send.wait()


def place_kernel(n_users, col_ref, known_ref, fetched_ref, *refs):
    share_refs, scratch = refs[:-1], refs[-1]
    n_lists, block, width = fetched_ref.shape
    fetched = fetched_ref[...].reshape(n_lists * block, width)
    share = share_refs[0].shape[0]
    slot = jnp.transpose(known_ref[:, : share * n_users])[:, :1].astype(jnp.int32)
    scratch[...] = jnp.dot(
        picks(slot, fetched.shape[0]), fetched, preferred_element_type=jnp.float32
    ).astype(jnp.bfloat16)
    for shift, ref in enumerate(share_refs):
        start = (col_ref[0] + shift) % n_users * share
        ref[...] = scratch[pl.ds(pl.multiple_of(start, share), share), :]


def attend_kernel(n_parts, *refs):
    parts, (keys_ref, values_ref, turned_ref, out_weight_ref, out_ref) = refs[:n_parts], refs[n_parts:]
    heads, events, features = keys_ref.shape
    head_dim = features - ROW_TILE
    rows = parts[0][...]
    for part in parts[1:]:
        rows = rows + part[...]
    queries = lax.dot_general(
        turned_ref[...], rows, (((1,), (1,)), ((), ())), preferred_element_type=jnp.float32
    )
    queries = (queries * head_dim ** (-0.5)).astype(jnp.bfloat16)
    feature = lax.broadcasted_iota(jnp.int32, (ROW_TILE, rows.shape[0]), 0)
    one = jnp.where(feature == 0, 1.0, 0.0).astype(jnp.bfloat16)

    def score(h):
        query = jnp.concatenate([queries[h * head_dim : (h + 1) * head_dim], one], axis=0)
        return jnp.dot(keys_ref[h], query, preferred_element_type=jnp.float32)

    ahead = [score(h) for h in range(min(2, heads))]
    mixed = []
    for h in range(heads):
        if h + 2 < heads:
            ahead.append(score(h + 2))
        exponentials = jnp.exp(ahead[h] - jnp.max(ahead[h], axis=0, keepdims=True))
        total = jnp.sum(exponentials, axis=0, keepdims=True)
        span = slice(h * head_dim, (h + 1) * head_dim)
        head = jnp.dot(values_ref[span, :], exponentials.astype(jnp.bfloat16), preferred_element_type=jnp.float32)
        mixed.append(head / total)
    attended = jnp.transpose(jnp.concatenate(mixed, axis=0)).astype(jnp.bfloat16)
    out_ref[...] = jnp.dot(attended, out_weight_ref[...], preferred_element_type=jnp.float32).astype(jnp.bfloat16)


def expand_kernel(user_dev, pieces, cap, known_ref, fetched_ref, out_hbm, out_ref, sems):
    n_lists, block, width = fetched_ref.shape
    kept = block - cap
    rows = n_lists * kept
    returned = fetched_ref[:, cap:, :].reshape(rows, width)
    count = out_ref.shape[0]
    first = known_ref.shape[1] - count
    probe = jnp.transpose(known_ref[:, first:])[:, :1].astype(jnp.int32)
    user = lax.broadcasted_iota(jnp.int32, (count, 1), 0) // (count // user_dev)
    sends = []
    for piece in range(pieces):
        wanted = probe * kept + piece * user_dev + user
        span = pl.ds(piece * width, width)
        out_ref[:, span] = jnp.dot(picks(wanted, rows), returned, preferred_element_type=jnp.float32).astype(
            jnp.bfloat16
        )
        sends.append(pltpu.make_async_copy(out_ref.at[:, span], out_hbm.at[:, span], sems.at[piece]))
        sends[-1].start()
    for send in sends:
        send.wait()


SMEM = pl.BlockSpec(memory_space=pltpu.SMEM)
VMEM = pl.BlockSpec(memory_space=pltpu.VMEM)
HBM = pl.BlockSpec(memory_space=pltpu.HBM)
PARAMS = pltpu.CompilerParams(vmem_limit_bytes=VMEM_BYTES)


def shards(
    user_vectors,
    probe_lists,
    list_items,
    candidate_ids,
    history,
    history_lengths,
    query_weight,
    key_value_weight,
    out_weight,
):
    n_lists = lax.axis_size("lists")
    n_users = lax.axis_size("users")
    _, items_loc, width = list_items.shape
    user_dev, probes = probe_lists.shape
    _, cands = candidate_ids.shape
    bf16 = jnp.bfloat16
    cap = max(2, 3 * cands // (n_lists * n_users))
    cap = round_up(cap, ROW_TILE)
    kept = round_up(items_loc // width * user_dev, ROW_TILE)
    share = cands // n_users
    pieces = items_loc // width
    digits = 1
    while BASE**digits < n_lists * n_users * items_loc:
        digits += 1
    pack_rows = round_up((user_dev + digits) * (width // LANES), 8)
    line = lax.axis_index("lists").astype(jnp.int32)
    col = lax.axis_index("users").astype(jnp.int32)
    col_arg = col.reshape(1)
    base_arg = ((line * n_users + col) * items_loc).reshape(1)
    block = cap + kept

    flat_items = list_items.reshape(items_loc, width)
    pack = pl.pallas_call(
        functools.partial(pack_kernel, digits),
        out_shape=jax.ShapeDtypeStruct((n_lists, pack_rows, LANES), bf16),
        in_specs=[VMEM, VMEM],
        out_specs=VMEM,
        compiler_params=pltpu.CompilerParams(vmem_limit_bytes=ALL_VMEM_BYTES),
    )(candidate_ids, user_vectors)
    gathered = lax.all_to_all(pack, "lists", split_axis=0, concat_axis=0, tiled=True)
    gathered = gathered.reshape(n_lists * pack_rows, LANES)

    known, items = pl.pallas_call(
        functools.partial(early_kernel, n_lists, n_users, block),
        out_shape=(
            jax.ShapeDtypeStruct((8, cands + user_dev * probes), jnp.float32),
            jax.ShapeDtypeStruct((items_loc, width), bf16),
        ),
        in_specs=[SMEM, VMEM, VMEM, HBM],
        out_specs=(VMEM, VMEM),
        scratch_shapes=[pltpu.SemaphoreType.DMA((4,))],
        compiler_params=PARAMS,
    )(col_arg, candidate_ids, probe_lists, flat_items)
    gathered, known, items = lax.optimization_barrier((gathered, known, items))

    events = history.reshape(-1, width)
    hist = [events]
    for shift in range(1, n_users):
        hist.append(lax.ppermute(events, "users", [(i, (i + shift) % n_users) for i in range(n_users)]))
    total_events = n_users * events.shape[0]
    keys, values, turned = pl.pallas_call(
        functools.partial(pairs_kernel, n_users),
        out_shape=(
            jax.ShapeDtypeStruct((HEADS, total_events, width // HEADS + ROW_TILE), bf16),
            jax.ShapeDtypeStruct((width, total_events), bf16),
            jax.ShapeDtypeStruct((width, width), bf16),
        ),
        in_specs=[SMEM, SMEM] + [VMEM] * (n_users + 2),
        out_specs=(VMEM, VMEM, VMEM),
        compiler_params=PARAMS,
    )(col_arg, history_lengths, *hist, key_value_weight, query_weight)

    step = max(1, 256 // cap)
    answers = pl.pallas_call(
        functools.partial(owner_kernel, n_lists, user_dev, digits, cap, width ** (-0.5)),
        out_shape=jax.ShapeDtypeStruct((n_lists, block, width), bf16),
        in_specs=[SMEM, VMEM, VMEM],
        out_specs=pl.BlockSpec(memory_space=pl.ANY),
        scratch_shapes=[
            pltpu.VMEM((n_lists, block, width), bf16),
            pltpu.SemaphoreType.DMA((-(-n_lists // step),)),
        ],
        compiler_params=PARAMS,
    )(base_arg, gathered, items)
    fetched = lax.all_to_all(answers, "lists", split_axis=0, concat_axis=0, tiled=True)

    fetched, keys, values, turned = lax.optimization_barrier((fetched, keys, values, turned))

    placed = pl.pallas_call(
        functools.partial(place_kernel, n_users),
        out_shape=tuple(jax.ShapeDtypeStruct((share, width), bf16) for _ in range(n_users)),
        in_specs=[SMEM, VMEM, VMEM],
        out_specs=tuple(VMEM for _ in range(n_users)),
        scratch_shapes=[pltpu.VMEM((cands, width), bf16)],
        compiler_params=PARAMS,
    )(col_arg, known, fetched)
    parts = [placed[0]]
    for shift in range(1, n_users):
        parts.append(
            lax.ppermute(placed[shift], "users", [(i, (i + shift) % n_users) for i in range(n_users)])
        )
    ranked = pl.pallas_call(
        functools.partial(attend_kernel, n_users),
        out_shape=jax.ShapeDtypeStruct((share, width), bf16),
        in_specs=[VMEM] * (n_users + 4),
        out_specs=VMEM,
        compiler_params=PARAMS,
    )(*parts, keys, values, turned, out_weight)

    list_scores = pl.pallas_call(
        functools.partial(expand_kernel, user_dev, pieces, cap),
        out_shape=jax.ShapeDtypeStruct((user_dev * probes, items_loc), bf16),
        in_specs=[VMEM, VMEM],
        out_specs=pl.BlockSpec(memory_space=pl.ANY),
        scratch_shapes=[
            pltpu.VMEM((user_dev * probes, items_loc), bf16),
            pltpu.SemaphoreType.DMA((pieces,)),
        ],
        compiler_params=PARAMS,
    )(known, fetched)
    return (list_scores.reshape(user_dev, probes, items_loc), ranked.reshape(1, share, width))


def solution(mesh):
    placed = (
        P("lists", None),
        P("lists", None),
        P("lists", "users", None),
        P("lists", None),
        P("lists", "users", None),
        P("lists"),
        P(),
        P(),
        P(),
    )
    return jax.shard_map(
        shards,
        mesh=mesh,
        in_specs=placed,
        out_specs=(P("lists", None, "users"), P("lists", "users", None)),
        check_vma=False,
    )
```

```python
import functools

import jax
import jax.numpy as jnp
from jax import lax
from jax.experimental import pallas as pl
from jax.experimental.pallas import tpu as pltpu
from jax.sharding import PartitionSpec as P

HEADS = 8
BASE = 256
LANES = 128
ROW_TILE = 16
VMEM_BYTES = 28 * 1024 * 1024
ALL_VMEM_BYTES = 62 * 1024 * 1024


def round_up(value, step):
    return (value + step - 1) // step * step


def picks(index, count):
    place = lax.broadcasted_iota(jnp.int32, (index.shape[0], count), 1)
    return jnp.where(index == place, 1.0, 0.0).astype(jnp.bfloat16)


def pack_kernel(digits, ids_ref, vectors_ref, pack_ref):
    width = vectors_ref.shape[1]
    vectors = vectors_ref[...].astype(jnp.float32)
    ids = ids_ref[...]
    spans = [slice(start, start + LANES) for start in range(0, width, LANES)]
    rows = [vectors[:, span] for span in spans]
    for digit in range(digits):
        value = ((ids >> (8 * digit)) & (BASE - 1)).astype(jnp.float32)
        rows += [value[:, span] for span in spans]
    count = sum(row.shape[0] for row in rows)
    if pack_ref.shape[0] > count:
        rows.append(jnp.zeros((pack_ref.shape[0] - count, LANES), jnp.float32))
    pack_ref[...] = jnp.concatenate(rows, axis=0).astype(jnp.bfloat16)


def earlier(count):
    row = lax.broadcasted_iota(jnp.int32, (count, count), 0)
    column = lax.broadcasted_iota(jnp.int32, (count, count), 1)
    return jnp.where(row < column, 1.0, 0.0).astype(jnp.bfloat16)


def unpack(gathered_ref, n_lists, user_dev, digits, turn):
    pack_rows = gathered_ref.shape[0] // n_lists
    spans = pack_rows // (user_dev + digits)
    entry = lax.broadcasted_iota(jnp.int32, ((user_dev + digits) * n_lists, 1), 0)
    asker, field = (entry % n_lists) ^ turn, entry // n_lists
    fields = jnp.concatenate(
        [
            jnp.dot(
                picks(
                    asker * pack_rows
                    + jnp.where(field < user_dev, span * user_dev + field, field * spans + span),
                    n_lists * pack_rows,
                ),
                gathered_ref[...],
                preferred_element_type=jnp.float32,
            )
            for span in range(spans)
        ],
        axis=1,
    )
    ids = jnp.zeros((n_lists, fields.shape[1]), jnp.float32)
    for digit in range(digits):
        ids = ids + fields[(user_dev + digit) * n_lists : (user_dev + digit + 1) * n_lists] * float(BASE**digit)
    return fields[: user_dev * n_lists], ids


def asked(ids, base, items_loc, first, count):
    local = ids - base
    mine = (local >= 0.0) & (local < items_loc)
    hot = jnp.where(mine, 1.0, 0.0).astype(jnp.bfloat16)
    rank = jnp.dot(hot, earlier(ids.shape[1]), preferred_element_type=jnp.float32)
    rank = jnp.where(mine, rank, -1.0)
    place = lax.broadcasted_iota(jnp.int32, (count, ids.shape[1]), 0).astype(jnp.float32) + float(first)
    index = []
    for r in range(ids.shape[0]):
        picked = jnp.where(rank[r : r + 1] == place, local[r : r + 1] + 1.0, 0.0)
        index.append(jnp.sum(picked, axis=1, keepdims=True).astype(jnp.int32) - 1)
    return index


def items_kernel(items_hbm, after_ref, items_ref, sems):
    part = items_ref.shape[0] // sems.shape[0]
    loads = []
    for p in range(sems.shape[0]):
        span = pl.ds(p * part, part)
        loads.append(pltpu.make_async_copy(items_hbm.at[span], items_ref.at[span], sems.at[p]))
        loads[-1].start()
    for load in loads:
        load.wait()


def slot_kernel(
    n_lists, items_loc, n_users, block, col_ref, ids_ref, probes_ref, after_ref, slot_ref, probe_ref
):
    ids = ids_ref[...]
    cands = ids.shape[1]
    bins = ids // items_loc
    mine = bins % n_users == col_ref[0]
    owner = bins // n_users
    lists = lax.broadcasted_iota(jnp.int32, (n_lists, cands), 0)
    hot = jnp.where((lists == owner) & mine, 1.0, 0.0)
    before = jnp.dot(hot.astype(jnp.bfloat16), earlier(cands), preferred_element_type=jnp.float32)
    rank = jnp.sum(before * hot, axis=0, keepdims=True)
    slot = jnp.where(mine, owner.astype(jnp.float32) * block + rank, -1.0)
    slot_ref[...] = jnp.broadcast_to(slot, slot_ref.shape)
    probes = probes_ref[...].astype(jnp.float32)
    flat = jnp.concatenate([probes[u : u + 1] for u in range(probes.shape[0])], axis=1)
    probe_ref[...] = jnp.broadcast_to(flat, probe_ref.shape)


def pairs_kernel(n_parts, col_ref, length_ref, after_ref, *refs):
    parts, (weight_ref, query_ref, keys_ref, values_ref, turned_ref) = refs[:n_parts], refs[n_parts:]
    history = jnp.concatenate([part[...] for part in parts], axis=0)
    pairs = jnp.dot(history, weight_ref[...], preferred_element_type=jnp.float32)
    heads, events, features = keys_ref.shape
    head_dim = features - ROW_TILE
    width = heads * head_dim
    hist_dev = events // n_parts
    event = lax.broadcasted_iota(jnp.int32, (events, ROW_TILE), 0)
    feature = lax.broadcasted_iota(jnp.int32, (events, ROW_TILE), 1)
    position = (col_ref[0] - event // hist_dev + n_parts) % n_parts * hist_dev + event % hist_dev
    mask = jnp.where((position >= length_ref[0]) & (feature == 0), -1e30, 0.0)
    for h in range(heads):
        keys = pairs[:, h * head_dim : (h + 1) * head_dim]
        keys_ref[h] = jnp.concatenate([keys, mask], axis=1).astype(jnp.bfloat16)
    values_ref[...] = jnp.transpose(pairs[:, width:]).astype(jnp.bfloat16)
    turned_ref[...] = jnp.transpose(query_ref[...].astype(jnp.float32)).astype(jnp.bfloat16)


def owner_kernel(n_lists, user_dev, digits, cap, scale, line_ref, base_ref, gathered_ref, items_ref, *refs):
    out_hbm, out_ref, out_sems = refs
    items_loc, width = items_ref.shape
    vectors, ids = unpack(gathered_ref, n_lists, user_dev, digits, line_ref[0])
    scores = lax.dot_general(
        vectors.astype(jnp.bfloat16),
        items_ref[...],
        (((1,), (1,)), ((), ())),
        preferred_element_type=jnp.float32,
    )
    scores = (scores * scale).astype(jnp.bfloat16)
    index = asked(ids, base_ref[0].astype(jnp.float32), items_loc, 0, cap)
    pieces = items_loc // width
    stacked = jnp.concatenate(
        [scores[:, piece * width : (piece + 1) * width] for piece in range(pieces)], axis=0
    )
    kept = out_ref.shape[1] - cap
    entry = lax.broadcasted_iota(jnp.int32, (n_lists * kept, 1), 0)
    wanted = jnp.where(entry % kept < pieces * user_dev, entry % kept * n_lists + entry // kept, -1)
    spread = jnp.dot(
        picks(wanted, stacked.shape[0]), stacked, preferred_element_type=jnp.float32
    ).astype(jnp.bfloat16)
    out_ref[:, cap:, :] = spread.reshape(n_lists, kept, width)
    step = max(1, 256 // cap)
    sends = []
    for number, first in enumerate(range(0, n_lists, step)):
        last = min(n_lists, first + step)
        rows = jnp.dot(
            picks(jnp.concatenate(index[first:last], axis=0), items_loc),
            items_ref[...],
            preferred_element_type=jnp.float32,
        ).astype(jnp.bfloat16)
        out_ref[first:last, :cap, :] = rows.reshape(last - first, cap, width)
        send = pltpu.make_async_copy(out_ref.at[first:last], out_hbm.at[first:last], out_sems.at[number])
        send.start()
        sends.append(send)
    for send in sends:
        send.wait()


def place_kernel(n_users, col_ref, slot_ref, fetched_ref, *refs):
    share_refs, scratch = refs[:-1], refs[-1]
    n_lists, block, width = fetched_ref.shape
    fetched = fetched_ref[...].reshape(n_lists * block, width)
    share = share_refs[0].shape[0]
    slot = jnp.transpose(slot_ref[...])[:, :1].astype(jnp.int32)
    scratch[...] = jnp.dot(
        picks(slot, fetched.shape[0]), fetched, preferred_element_type=jnp.float32
    ).astype(jnp.bfloat16)
    for shift, ref in enumerate(share_refs):
        start = (col_ref[0] + shift) % n_users * share
        ref[...] = scratch[pl.ds(pl.multiple_of(start, share), share), :]


def attend_kernel(n_parts, *refs):
    parts, (keys_ref, values_ref, turned_ref, out_weight_ref, out_ref) = refs[:n_parts], refs[n_parts:]
    heads, events, features = keys_ref.shape
    head_dim = features - ROW_TILE
    rows = parts[0][...]
    for part in parts[1:]:
        rows = rows + part[...]
    queries = lax.dot_general(
        turned_ref[...], rows, (((1,), (1,)), ((), ())), preferred_element_type=jnp.float32
    )
    queries = (queries * head_dim ** (-0.5)).astype(jnp.bfloat16)
    feature = lax.broadcasted_iota(jnp.int32, (ROW_TILE, rows.shape[0]), 0)
    one = jnp.where(feature == 0, 1.0, 0.0).astype(jnp.bfloat16)

    def score(h):
        query = jnp.concatenate([queries[h * head_dim : (h + 1) * head_dim], one], axis=0)
        return jnp.dot(keys_ref[h], query, preferred_element_type=jnp.float32)

    ahead = [score(h) for h in range(min(2, heads))]
    mixed = []
    for h in range(heads):
        if h + 2 < heads:
            ahead.append(score(h + 2))
        exponentials = jnp.exp(ahead[h] - jnp.max(ahead[h], axis=0, keepdims=True))
        total = jnp.sum(exponentials, axis=0, keepdims=True)
        span = slice(h * head_dim, (h + 1) * head_dim)
        head = jnp.dot(values_ref[span, :], exponentials.astype(jnp.bfloat16), preferred_element_type=jnp.float32)
        mixed.append(head / total)
    attended = jnp.transpose(jnp.concatenate(mixed, axis=0)).astype(jnp.bfloat16)
    out_ref[...] = jnp.dot(attended, out_weight_ref[...], preferred_element_type=jnp.float32).astype(jnp.bfloat16)


def expand_kernel(user_dev, pieces, cap, probe_ref, fetched_ref, out_hbm, out_ref, sems):
    n_lists, block, width = fetched_ref.shape
    kept = block - cap
    rows = n_lists * kept
    returned = fetched_ref[:, cap:, :].reshape(rows, width)
    count = out_ref.shape[0]
    probe = jnp.transpose(probe_ref[...])[:, :1].astype(jnp.int32)
    user = lax.broadcasted_iota(jnp.int32, (count, 1), 0) // (count // user_dev)
    sends = []
    for piece in range(pieces):
        wanted = probe * kept + piece * user_dev + user
        span = pl.ds(piece * width, width)
        out_ref[:, span] = jnp.dot(picks(wanted, rows), returned, preferred_element_type=jnp.float32).astype(
            jnp.bfloat16
        )
        sends.append(pltpu.make_async_copy(out_ref.at[:, span], out_hbm.at[:, span], sems.at[piece]))
        sends[-1].start()
    for send in sends:
        send.wait()


SMEM = pl.BlockSpec(memory_space=pltpu.SMEM)
VMEM = pl.BlockSpec(memory_space=pltpu.VMEM)
HBM = pl.BlockSpec(memory_space=pltpu.HBM)
PARAMS = pltpu.CompilerParams(vmem_limit_bytes=VMEM_BYTES)


def shards(
    user_vectors,
    probe_lists,
    list_items,
    candidate_ids,
    history,
    history_lengths,
    query_weight,
    key_value_weight,
    out_weight,
):
    n_lists = lax.axis_size("lists")
    n_users = lax.axis_size("users")
    _, items_loc, width = list_items.shape
    user_dev, probes = probe_lists.shape
    _, cands = candidate_ids.shape
    bf16 = jnp.bfloat16
    cap = max(2, 3 * cands // (n_lists * n_users))
    cap = round_up(cap, ROW_TILE)
    kept = round_up(items_loc // width * user_dev, ROW_TILE)
    share = cands // n_users
    pieces = items_loc // width
    digits = 1
    while BASE**digits < n_lists * n_users * items_loc:
        digits += 1
    pack_rows = round_up((user_dev + digits) * (width // LANES), 8)
    line = lax.axis_index("lists").astype(jnp.int32)
    col = lax.axis_index("users").astype(jnp.int32)
    line_arg = line.reshape(1)
    col_arg = col.reshape(1)
    base_arg = ((line * n_users + col) * items_loc).reshape(1)
    block = cap + kept

    flat_items = list_items.reshape(items_loc, width)
    pack = pl.pallas_call(
        functools.partial(pack_kernel, digits),
        out_shape=jax.ShapeDtypeStruct((pack_rows, LANES), bf16),
        in_specs=[VMEM, VMEM],
        out_specs=VMEM,
        compiler_params=pltpu.CompilerParams(vmem_limit_bytes=ALL_VMEM_BYTES),
    )(candidate_ids, user_vectors)
    gathered, reach = pack, 1
    while reach < n_lists:
        ahead = gathered
        came = lax.ppermute(gathered, "lists", [(i, i ^ reach) for i in range(n_lists)])
        gathered, reach = jnp.concatenate([gathered, came], axis=0), reach * 2

    items = pl.pallas_call(
        items_kernel,
        out_shape=jax.ShapeDtypeStruct((items_loc, width), bf16),
        in_specs=[HBM, pl.BlockSpec(memory_space=pl.ANY)],
        out_specs=VMEM,
        scratch_shapes=[pltpu.SemaphoreType.DMA((4,))],
        compiler_params=PARAMS,
    )(flat_items, ahead)

    events = history.reshape(-1, width)
    hist = [events]
    for shift in range(1, n_users):
        hist.append(lax.ppermute(events, "users", [(i, (i + shift) % n_users) for i in range(n_users)]))
    total_events = n_users * events.shape[0]
    step = max(1, 256 // cap)
    answers = pl.pallas_call(
        functools.partial(owner_kernel, n_lists, user_dev, digits, cap, width ** (-0.5)),
        out_shape=jax.ShapeDtypeStruct((n_lists, block, width), bf16),
        in_specs=[SMEM, SMEM, VMEM, VMEM],
        out_specs=pl.BlockSpec(memory_space=pl.ANY),
        scratch_shapes=[
            pltpu.VMEM((n_lists, block, width), bf16),
            pltpu.SemaphoreType.DMA((-(-n_lists // step),)),
        ],
        compiler_params=PARAMS,
    )(line_arg, base_arg, gathered, items)
    fetched = lax.all_to_all(answers, "lists", split_axis=0, concat_axis=0, tiled=True)
    slot, probe_row = pl.pallas_call(
        functools.partial(slot_kernel, n_lists, items_loc, n_users, block),
        out_shape=(
            jax.ShapeDtypeStruct((8, cands), jnp.float32),
            jax.ShapeDtypeStruct((8, user_dev * probes), jnp.float32),
        ),
        in_specs=[SMEM, VMEM, VMEM, pl.BlockSpec(memory_space=pl.ANY)],
        out_specs=(VMEM, VMEM),
        compiler_params=PARAMS,
    )(col_arg, candidate_ids, probe_lists, answers)

    keys, values, turned = pl.pallas_call(
        functools.partial(pairs_kernel, n_users),
        out_shape=(
            jax.ShapeDtypeStruct((HEADS, total_events, width // HEADS + ROW_TILE), bf16),
            jax.ShapeDtypeStruct((width, total_events), bf16),
            jax.ShapeDtypeStruct((width, width), bf16),
        ),
        in_specs=[SMEM, SMEM, pl.BlockSpec(memory_space=pl.ANY)] + [VMEM] * (n_users + 2),
        out_specs=(VMEM, VMEM, VMEM),
        compiler_params=PARAMS,
    )(col_arg, history_lengths, answers, *hist, key_value_weight, query_weight)

    fetched, slot, probe_row, keys, values, turned = lax.optimization_barrier(
        (fetched, slot, probe_row, keys, values, turned)
    )

    placed = pl.pallas_call(
        functools.partial(place_kernel, n_users),
        out_shape=tuple(jax.ShapeDtypeStruct((share, width), bf16) for _ in range(n_users)),
        in_specs=[SMEM, VMEM, VMEM],
        out_specs=tuple(VMEM for _ in range(n_users)),
        scratch_shapes=[pltpu.VMEM((cands, width), bf16)],
        compiler_params=PARAMS,
    )(col_arg, slot, fetched)
    parts = [placed[0]]
    for shift in range(1, n_users):
        parts.append(
            lax.ppermute(placed[shift], "users", [(i, (i + shift) % n_users) for i in range(n_users)])
        )
    ranked = pl.pallas_call(
        functools.partial(attend_kernel, n_users),
        out_shape=jax.ShapeDtypeStruct((share, width), bf16),
        in_specs=[VMEM] * (n_users + 4),
        out_specs=VMEM,
        compiler_params=PARAMS,
    )(*parts, keys, values, turned, out_weight)

    list_scores = pl.pallas_call(
        functools.partial(expand_kernel, user_dev, pieces, cap),
        out_shape=jax.ShapeDtypeStruct((user_dev * probes, items_loc), bf16),
        in_specs=[VMEM, VMEM],
        out_specs=pl.BlockSpec(memory_space=pl.ANY),
        scratch_shapes=[
            pltpu.VMEM((user_dev * probes, items_loc), bf16),
            pltpu.SemaphoreType.DMA((pieces,)),
        ],
        compiler_params=PARAMS,
    )(probe_row, fetched)
    return (list_scores.reshape(user_dev, probes, items_loc), ranked.reshape(1, share, width))


def solution(mesh):
    placed = (
        P("lists", None),
        P("lists", None),
        P("lists", "users", None),
        P("lists", None),
        P("lists", "users", None),
        P("lists"),
        P(),
        P(),
        P(),
    )
    return jax.shard_map(
        shards,
        mesh=mesh,
        in_specs=placed,
        out_specs=(P("lists", None, "users"), P("lists", "users", None)),
        check_vma=False,
    )
```

```python
import functools

import jax
import jax.numpy as jnp
from jax import lax
from jax.experimental import pallas as pl
from jax.experimental.pallas import tpu as pltpu
from jax.sharding import PartitionSpec as P

HEADS = 8
BASE = 256
LANES = 128
ROW_TILE = 16
VMEM_BYTES = 28 * 1024 * 1024
ALL_VMEM_BYTES = 62 * 1024 * 1024


def round_up(value, step):
    return (value + step - 1) // step * step


def picks(index, count):
    place = lax.broadcasted_iota(jnp.int32, (index.shape[0], count), 1)
    return jnp.where(index == place, 1.0, 0.0).astype(jnp.bfloat16)


def pack_kernel(digits, ids_ref, vectors_ref, pack_ref):
    width = vectors_ref.shape[1]
    vectors = vectors_ref[...].astype(jnp.float32)
    ids = ids_ref[...]
    spans = [slice(start, start + LANES) for start in range(0, width, LANES)]
    rows = [vectors[:, span] for span in spans]
    for digit in range(digits):
        value = ((ids >> (8 * digit)) & (BASE - 1)).astype(jnp.float32)
        rows += [value[:, span] for span in spans]
    count = sum(row.shape[0] for row in rows)
    if pack_ref.shape[1] > count:
        rows.append(jnp.zeros((pack_ref.shape[1] - count, LANES), jnp.float32))
    pack_ref[...] = jnp.broadcast_to(jnp.concatenate(rows, axis=0).astype(jnp.bfloat16)[None], pack_ref.shape)


def earlier(count):
    row = lax.broadcasted_iota(jnp.int32, (count, count), 0)
    column = lax.broadcasted_iota(jnp.int32, (count, count), 1)
    return jnp.where(row < column, 1.0, 0.0).astype(jnp.bfloat16)


def unpack(gathered_ref, n_lists, user_dev, digits, turn):
    pack_rows = gathered_ref.shape[0] // n_lists
    spans = pack_rows // (user_dev + digits)
    entry = lax.broadcasted_iota(jnp.int32, ((user_dev + digits) * n_lists, 1), 0)
    asker, field = (entry % n_lists) ^ turn, entry // n_lists
    fields = jnp.concatenate(
        [
            jnp.dot(
                picks(
                    asker * pack_rows
                    + jnp.where(field < user_dev, span * user_dev + field, field * spans + span),
                    n_lists * pack_rows,
                ),
                gathered_ref[...],
                preferred_element_type=jnp.float32,
            )
            for span in range(spans)
        ],
        axis=1,
    )
    ids = jnp.zeros((n_lists, fields.shape[1]), jnp.float32)
    for digit in range(digits):
        ids = ids + fields[(user_dev + digit) * n_lists : (user_dev + digit + 1) * n_lists] * float(BASE**digit)
    return fields[: user_dev * n_lists], ids


def asked(ids, base, items_loc, first, count):
    local = ids - base
    mine = (local >= 0.0) & (local < items_loc)
    hot = jnp.where(mine, 1.0, 0.0).astype(jnp.bfloat16)
    rank = jnp.dot(hot, earlier(ids.shape[1]), preferred_element_type=jnp.float32)
    rank = jnp.where(mine, rank, -1.0)
    place = lax.broadcasted_iota(jnp.int32, (count, ids.shape[1]), 0).astype(jnp.float32) + float(first)
    index = []
    for r in range(ids.shape[0]):
        picked = jnp.where(rank[r : r + 1] == place, local[r : r + 1] + 1.0, 0.0)
        index.append(jnp.sum(picked, axis=1, keepdims=True).astype(jnp.int32) - 1)
    return index


def position(index, count):
    half = max(1, count // 2)
    return index % half * 2 + index // half if count > 1 else index


def items_kernel(items_hbm, items_ref, sems):
    part = items_ref.shape[0] // sems.shape[0]
    loads = []
    for p in range(sems.shape[0]):
        span = pl.ds(p * part, part)
        loads.append(pltpu.make_async_copy(items_hbm.at[span], items_ref.at[span], sems.at[p]))
        loads[-1].start()
    for load in loads:
        load.wait()


def known_kernel(n_lists, items_loc, n_users, block, col_ref, ids_ref, probes_ref, known_ref, order_ref):
    ids = ids_ref[...]
    cands = ids.shape[1]
    bins = ids // items_loc
    mine = bins % n_users == col_ref[0]
    owner = bins // n_users
    lists = lax.broadcasted_iota(jnp.int32, (n_lists, cands), 0)
    hot = jnp.where((lists == owner) & mine, 1.0, 0.0)
    before = jnp.dot(hot.astype(jnp.bfloat16), earlier(cands), preferred_element_type=jnp.float32)
    rank = jnp.sum(before * hot, axis=0, keepdims=True)
    slot = jnp.where(mine, position(owner, n_lists).astype(jnp.float32) * block + rank, -1.0)
    probes = position(probes_ref[...], n_lists).astype(jnp.float32)
    flat = jnp.concatenate([probes[u : u + 1] for u in range(probes.shape[0])], axis=1)
    if flat.shape[1] < cands:
        flat = jnp.concatenate([flat, jnp.zeros((1, cands - flat.shape[1]), jnp.float32)], axis=1)
    row = lax.broadcasted_iota(jnp.int32, known_ref.shape, 0)
    known_ref[...] = jnp.where(row == 0, slot, flat)
    order_ref[...] = jnp.zeros_like(order_ref)


def pairs_kernel(n_parts, col_ref, length_ref, *refs):
    parts, (weight_ref, query_ref, keys_ref, values_ref, turned_ref) = refs[:n_parts], refs[n_parts:]
    history = jnp.concatenate([part[...] for part in parts], axis=0)
    pairs = jnp.dot(history, weight_ref[...], preferred_element_type=jnp.float32)
    heads, events, features = keys_ref.shape
    head_dim = features - ROW_TILE
    width = heads * head_dim
    hist_dev = events // n_parts
    event = lax.broadcasted_iota(jnp.int32, (events, ROW_TILE), 0)
    feature = lax.broadcasted_iota(jnp.int32, (events, ROW_TILE), 1)
    position = (col_ref[0] - event // hist_dev + n_parts) % n_parts * hist_dev + event % hist_dev
    mask = jnp.where((position >= length_ref[0]) & (feature == 0), -1e30, 0.0)
    for h in range(heads):
        keys = pairs[:, h * head_dim : (h + 1) * head_dim]
        keys_ref[h] = jnp.concatenate([keys, mask], axis=1).astype(jnp.bfloat16)
    values_ref[...] = jnp.transpose(pairs[:, width:]).astype(jnp.bfloat16)
    turned_ref[...] = jnp.transpose(query_ref[...].astype(jnp.float32)).astype(jnp.bfloat16)


def owner_kernel(n_lists, user_dev, digits, cap, scale, base_ref, gathered_ref, items_ref, *refs):
    out_hbm, out_ref, out_sems = refs
    items_loc, width = items_ref.shape
    vectors, ids = unpack(gathered_ref, n_lists, user_dev, digits, 0)
    index = asked(ids, base_ref[0].astype(jnp.float32), items_loc, 0, cap)
    scores = lax.dot_general(
        vectors.astype(jnp.bfloat16),
        items_ref[...],
        (((1,), (1,)), ((), ())),
        preferred_element_type=jnp.float32,
    )
    scores = (scores * scale).astype(jnp.bfloat16)
    pieces = items_loc // width
    stacked = jnp.concatenate(
        [scores[:, piece * width : (piece + 1) * width] for piece in range(pieces)], axis=0
    )
    kept = out_ref.shape[1] - cap
    entry = lax.broadcasted_iota(jnp.int32, (n_lists * kept, 1), 0)
    wanted = jnp.where(entry % kept < pieces * user_dev, entry % kept * n_lists + entry // kept, -1)
    spread = jnp.dot(
        picks(wanted, stacked.shape[0]), stacked, preferred_element_type=jnp.float32
    ).astype(jnp.bfloat16)
    out_ref[:, cap:, :] = spread.reshape(n_lists, kept, width)
    step = max(1, 256 // cap)
    sends = []
    for number, first in enumerate(range(0, n_lists, step)):
        last = min(n_lists, first + step)
        rows = jnp.dot(
            picks(jnp.concatenate(index[first:last], axis=0), items_loc),
            items_ref[...],
            preferred_element_type=jnp.float32,
        ).astype(jnp.bfloat16)
        out_ref[first:last, :cap, :] = rows.reshape(last - first, cap, width)
        send = pltpu.make_async_copy(out_ref.at[first:last], out_hbm.at[first:last], out_sems.at[number])
        send.start()
        sends.append(send)
    for send in sends:
        send.wait()


def place_kernel(n_users, col_ref, known_ref, fetched_ref, *refs):
    share_refs, scratch = refs[:-1], refs[-1]
    n_lists, block, width = fetched_ref.shape
    fetched = fetched_ref[...].reshape(n_lists * block, width)
    share = share_refs[0].shape[0]
    slot = jnp.transpose(known_ref[...])[:, :1].astype(jnp.int32)
    scratch[...] = jnp.dot(
        picks(slot, fetched.shape[0]), fetched, preferred_element_type=jnp.float32
    ).astype(jnp.bfloat16)
    for shift, ref in enumerate(share_refs):
        start = (col_ref[0] + shift) % n_users * share
        ref[...] = scratch[pl.ds(pl.multiple_of(start, share), share), :]


def attend_kernel(n_parts, *refs):
    parts, (keys_ref, values_ref, turned_ref, out_weight_ref, out_ref) = refs[:n_parts], refs[n_parts:]
    heads, events, features = keys_ref.shape
    head_dim = features - ROW_TILE
    rows = parts[0][...]
    for part in parts[1:]:
        rows = rows + part[...]
    queries = lax.dot_general(
        turned_ref[...], rows, (((1,), (1,)), ((), ())), preferred_element_type=jnp.float32
    )
    queries = (queries * head_dim ** (-0.5)).astype(jnp.bfloat16)
    feature = lax.broadcasted_iota(jnp.int32, (ROW_TILE, rows.shape[0]), 0)
    one = jnp.where(feature == 0, 1.0, 0.0).astype(jnp.bfloat16)

    def score(h):
        query = jnp.concatenate([queries[h * head_dim : (h + 1) * head_dim], one], axis=0)
        return jnp.dot(keys_ref[h], query, preferred_element_type=jnp.float32)

    ahead = [score(h) for h in range(min(2, heads))]
    mixed = []
    for h in range(heads):
        if h + 2 < heads:
            ahead.append(score(h + 2))
        exponentials = jnp.exp(ahead[h] - jnp.max(ahead[h], axis=0, keepdims=True))
        total = jnp.sum(exponentials, axis=0, keepdims=True)
        span = slice(h * head_dim, (h + 1) * head_dim)
        head = jnp.dot(values_ref[span, :], exponentials.astype(jnp.bfloat16), preferred_element_type=jnp.float32)
        mixed.append(head / total)
    attended = jnp.transpose(jnp.concatenate(mixed, axis=0)).astype(jnp.bfloat16)
    out_ref[...] = jnp.dot(attended, out_weight_ref[...], preferred_element_type=jnp.float32).astype(jnp.bfloat16)


def expand_kernel(user_dev, pieces, cap, known_ref, order_ref, fetched_ref, out_hbm, out_ref, sems):
    n_lists, block, width = fetched_ref.shape
    kept = block - cap
    rows = n_lists * kept
    returned = fetched_ref[:, cap:, :].reshape(rows, width)
    count = out_ref.shape[0]
    probe = jnp.transpose(known_ref[:, :count])[:, 1:2].astype(jnp.int32)
    user = lax.broadcasted_iota(jnp.int32, (count, 1), 0) // (count // user_dev)
    sends = []
    for piece in range(pieces):
        wanted = probe * kept + piece * user_dev + user
        span = pl.ds(piece * width, width)
        out_ref[:, span] = jnp.dot(picks(wanted, rows), returned, preferred_element_type=jnp.float32).astype(
            jnp.bfloat16
        )
        sends.append(pltpu.make_async_copy(out_ref.at[:, span], out_hbm.at[:, span], sems.at[piece]))
        sends[-1].start()
    for send in sends:
        send.wait()


SMEM = pl.BlockSpec(memory_space=pltpu.SMEM)
VMEM = pl.BlockSpec(memory_space=pltpu.VMEM)
HBM = pl.BlockSpec(memory_space=pltpu.HBM)
PARAMS = pltpu.CompilerParams(vmem_limit_bytes=VMEM_BYTES)


def exchange(value):
    count = lax.axis_size("lists")
    group = sorted(range(count), key=lambda index: position(index, count))
    return lax.all_to_all(
        value, "lists", split_axis=0, concat_axis=0, axis_index_groups=[group], tiled=True
    )


def shards(
    user_vectors,
    probe_lists,
    list_items,
    candidate_ids,
    history,
    history_lengths,
    query_weight,
    key_value_weight,
    out_weight,
):
    n_lists = lax.axis_size("lists")
    n_users = lax.axis_size("users")
    _, items_loc, width = list_items.shape
    user_dev, probes = probe_lists.shape
    _, cands = candidate_ids.shape
    bf16 = jnp.bfloat16
    cap = max(2, 3 * cands // (n_lists * n_users))
    cap = round_up(cap, ROW_TILE)
    kept = round_up(items_loc // width * user_dev, ROW_TILE)
    share = cands // n_users
    pieces = items_loc // width
    digits = 1
    while BASE**digits < n_lists * n_users * items_loc:
        digits += 1
    pack_rows = round_up((user_dev + digits) * (width // LANES), 8)
    line = lax.axis_index("lists").astype(jnp.int32)
    col = lax.axis_index("users").astype(jnp.int32)
    col_arg = col.reshape(1)
    base_arg = ((line * n_users + col) * items_loc).reshape(1)
    block = cap + kept

    flat_items = list_items.reshape(items_loc, width)
    pack = pl.pallas_call(
        functools.partial(pack_kernel, digits),
        out_shape=jax.ShapeDtypeStruct((n_lists, pack_rows, LANES), bf16),
        in_specs=[VMEM, VMEM],
        out_specs=VMEM,
        compiler_params=pltpu.CompilerParams(vmem_limit_bytes=ALL_VMEM_BYTES),
    )(candidate_ids, user_vectors)
    gathered = exchange(pack)
    gathered = gathered.reshape(n_lists * pack_rows, LANES)

    items = pl.pallas_call(
        items_kernel,
        out_shape=jax.ShapeDtypeStruct((items_loc, width), bf16),
        in_specs=[HBM],
        out_specs=VMEM,
        scratch_shapes=[pltpu.SemaphoreType.DMA((4,))],
        compiler_params=PARAMS,
    )(flat_items)
    gathered, items = lax.optimization_barrier((gathered, items))

    known, order = pl.pallas_call(
        functools.partial(known_kernel, n_lists, items_loc, n_users, block),
        out_shape=(
            jax.ShapeDtypeStruct((8, cands), jnp.float32),
            jax.ShapeDtypeStruct((8, LANES), jnp.float32),
        ),
        in_specs=[SMEM, VMEM, VMEM],
        out_specs=(VMEM, VMEM),
        compiler_params=PARAMS,
    )(col_arg, candidate_ids, probe_lists)

    events = history.reshape(-1, width)
    hist = [events]
    for shift in range(1, n_users):
        hist.append(lax.ppermute(events, "users", [(i, (i + shift) % n_users) for i in range(n_users)]))
    total_events = n_users * events.shape[0]
    keys, values, turned = pl.pallas_call(
        functools.partial(pairs_kernel, n_users),
        out_shape=(
            jax.ShapeDtypeStruct((HEADS, total_events, width // HEADS + ROW_TILE), bf16),
            jax.ShapeDtypeStruct((width, total_events), bf16),
            jax.ShapeDtypeStruct((width, width), bf16),
        ),
        in_specs=[SMEM, SMEM] + [VMEM] * (n_users + 2),
        out_specs=(VMEM, VMEM, VMEM),
        compiler_params=PARAMS,
    )(col_arg, history_lengths, *hist, key_value_weight, query_weight)

    step = max(1, 256 // cap)
    answers = pl.pallas_call(
        functools.partial(owner_kernel, n_lists, user_dev, digits, cap, width ** (-0.5)),
        out_shape=jax.ShapeDtypeStruct((n_lists, block, width), bf16),
        in_specs=[SMEM, VMEM, VMEM],
        out_specs=pl.BlockSpec(memory_space=pl.ANY),
        scratch_shapes=[
            pltpu.VMEM((n_lists, block, width), bf16),
            pltpu.SemaphoreType.DMA((-(-n_lists // step),)),
        ],
        compiler_params=PARAMS,
    )(base_arg, gathered, items)
    fetched = exchange(answers)

    fetched, known, order, keys, values, turned = lax.optimization_barrier(
        (fetched, known, order, keys, values, turned)
    )

    placed = pl.pallas_call(
        functools.partial(place_kernel, n_users),
        out_shape=tuple(jax.ShapeDtypeStruct((share, width), bf16) for _ in range(n_users)),
        in_specs=[SMEM, VMEM, VMEM],
        out_specs=tuple(VMEM for _ in range(n_users)),
        scratch_shapes=[pltpu.VMEM((cands, width), bf16)],
        compiler_params=PARAMS,
    )(col_arg, known, fetched)
    parts = [placed[0]]
    for shift in range(1, n_users):
        parts.append(
            lax.ppermute(placed[shift], "users", [(i, (i + shift) % n_users) for i in range(n_users)])
        )
    ranked = pl.pallas_call(
        functools.partial(attend_kernel, n_users),
        out_shape=jax.ShapeDtypeStruct((share, width), bf16),
        in_specs=[VMEM] * (n_users + 4),
        out_specs=VMEM,
        compiler_params=PARAMS,
    )(*parts, keys, values, turned, out_weight)

    list_scores = pl.pallas_call(
        functools.partial(expand_kernel, user_dev, pieces, cap),
        out_shape=jax.ShapeDtypeStruct((user_dev * probes, items_loc), bf16),
        in_specs=[VMEM, pl.BlockSpec(memory_space=pl.ANY), VMEM],
        out_specs=pl.BlockSpec(memory_space=pl.ANY),
        scratch_shapes=[
            pltpu.VMEM((user_dev * probes, items_loc), bf16),
            pltpu.SemaphoreType.DMA((pieces,)),
        ],
        compiler_params=PARAMS,
    )(known, order, fetched)
    return (list_scores.reshape(user_dev, probes, items_loc), ranked.reshape(1, share, width))


def solution(mesh):
    placed = (
        P("lists", None),
        P("lists", None),
        P("lists", "users", None),
        P("lists", None),
        P("lists", "users", None),
        P("lists"),
        P(),
        P(),
        P(),
    )
    return jax.shard_map(
        shards,
        mesh=mesh,
        in_specs=placed,
        out_specs=(P("lists", None, "users"), P("lists", "users", None)),
        check_vma=False,
    )
```

```python
import functools

import jax
import jax.numpy as jnp
from jax import lax
from jax.experimental import pallas as pl
from jax.experimental.pallas import tpu as pltpu
from jax.sharding import PartitionSpec as P

HEADS = 8
BASE = 256
LANES = 128
ROW_TILE = 16
PROBE_ROWS = 1024
VMEM_BYTES = 28 * 1024 * 1024
ALL_VMEM_BYTES = 62 * 1024 * 1024


def round_up(value, step):
    return (value + step - 1) // step * step


def picks(index, count):
    place = lax.broadcasted_iota(jnp.int32, (index.shape[0], count), 1)
    return jnp.where(index == place, 1.0, 0.0).astype(jnp.bfloat16)


def pack_kernel(digits, ids_ref, vectors_ref, pack_ref):
    width = vectors_ref.shape[1]
    vectors = vectors_ref[...].astype(jnp.float32)
    ids = ids_ref[...]
    spans = [slice(start, start + LANES) for start in range(0, width, LANES)]
    rows = [vectors[:, span] for span in spans]
    for digit in range(digits):
        value = ((ids >> (8 * digit)) & (BASE - 1)).astype(jnp.float32)
        rows += [value[:, span] for span in spans]
    count = sum(row.shape[0] for row in rows)
    if pack_ref.shape[1] > count:
        rows.append(jnp.zeros((pack_ref.shape[1] - count, LANES), jnp.float32))
    pack_ref[...] = jnp.broadcast_to(jnp.concatenate(rows, axis=0).astype(jnp.bfloat16)[None], pack_ref.shape)


def earlier(count):
    row = lax.broadcasted_iota(jnp.int32, (count, count), 0)
    column = lax.broadcasted_iota(jnp.int32, (count, count), 1)
    return jnp.where(row < column, 1.0, 0.0).astype(jnp.bfloat16)


def unpack(gathered_ref, n_lists, user_dev, digits, turn):
    pack_rows = gathered_ref.shape[0] // n_lists
    spans = pack_rows // (user_dev + digits)
    entry = lax.broadcasted_iota(jnp.int32, ((user_dev + digits) * n_lists, 1), 0)
    asker, field = (entry % n_lists) ^ turn, entry // n_lists
    fields = jnp.concatenate(
        [
            jnp.dot(
                picks(
                    asker * pack_rows
                    + jnp.where(field < user_dev, span * user_dev + field, field * spans + span),
                    n_lists * pack_rows,
                ),
                gathered_ref[...],
                preferred_element_type=jnp.float32,
            )
            for span in range(spans)
        ],
        axis=1,
    )
    ids = jnp.zeros((n_lists, fields.shape[1]), jnp.float32)
    for digit in range(digits):
        ids = ids + fields[(user_dev + digit) * n_lists : (user_dev + digit + 1) * n_lists] * float(BASE**digit)
    return fields[: user_dev * n_lists], ids


def asked(ids, base, items_loc, first, count):
    local = ids - base
    mine = (local >= 0.0) & (local < items_loc)
    hot = jnp.where(mine, 1.0, 0.0).astype(jnp.bfloat16)
    rank = jnp.dot(hot, earlier(ids.shape[1]), preferred_element_type=jnp.float32)
    rank = jnp.where(mine, rank, -1.0)
    place = lax.broadcasted_iota(jnp.int32, (count, ids.shape[1]), 0).astype(jnp.float32) + float(first)
    index = []
    for r in range(ids.shape[0]):
        picked = jnp.where(rank[r : r + 1] == place, local[r : r + 1] + 1.0, 0.0)
        index.append(jnp.sum(picked, axis=1, keepdims=True).astype(jnp.int32) - 1)
    return index


def position(index, count):
    bits = count.bit_length() - 1
    if count != 1 << bits:
        return index
    place = index * 0
    for bit in range(bits):
        place = place | (((index >> bit) & 1) << (bits - 1 - bit))
    return place


def items_kernel(items_hbm, items_ref, sems):
    part = items_ref.shape[0] // sems.shape[0]
    loads = []
    for p in range(sems.shape[0]):
        span = pl.ds(p * part, part)
        loads.append(pltpu.make_async_copy(items_hbm.at[span], items_ref.at[span], sems.at[p]))
        loads[-1].start()
    for load in loads:
        load.wait()


def known_kernel(n_lists, items_loc, n_users, block, col_ref, ids_ref, probes_ref, slot_ref, probe_ref):
    ids = ids_ref[...]
    cands = ids.shape[1]
    bins = ids // items_loc
    mine = bins % n_users == col_ref[0]
    owner = bins // n_users
    lists = lax.broadcasted_iota(jnp.int32, (n_lists, cands), 0)
    hot = jnp.where((lists == owner) & mine, 1.0, 0.0)
    before = jnp.dot(hot.astype(jnp.bfloat16), earlier(cands), preferred_element_type=jnp.float32)
    rank = jnp.sum(before * hot, axis=0, keepdims=True)
    slot = jnp.where(mine, position(owner, n_lists).astype(jnp.float32) * block + rank, -1.0)
    probes = position(probes_ref[...], n_lists).astype(jnp.float32)
    flat = jnp.concatenate([probes[u : u + 1] for u in range(probes.shape[0])], axis=1)
    slot_ref[...] = jnp.broadcast_to(slot, slot_ref.shape)
    probe_ref[...] = jnp.broadcast_to(flat, probe_ref.shape)


def pairs_kernel(n_parts, col_ref, length_ref, *refs):
    parts, (weight_ref, query_ref, keys_ref, values_ref, turned_ref) = refs[:n_parts], refs[n_parts:]
    history = jnp.concatenate([part[...] for part in parts], axis=0)
    pairs = jnp.dot(history, weight_ref[...], preferred_element_type=jnp.float32)
    heads, events, features = keys_ref.shape
    head_dim = features - ROW_TILE
    width = heads * head_dim
    hist_dev = events // n_parts
    event = lax.broadcasted_iota(jnp.int32, (events, ROW_TILE), 0)
    feature = lax.broadcasted_iota(jnp.int32, (events, ROW_TILE), 1)
    position = (col_ref[0] - event // hist_dev + n_parts) % n_parts * hist_dev + event % hist_dev
    mask = jnp.where((position >= length_ref[0]) & (feature == 0), -1e30, 0.0)
    for h in range(heads):
        keys = pairs[:, h * head_dim : (h + 1) * head_dim]
        keys_ref[h] = jnp.concatenate([keys, mask], axis=1).astype(jnp.bfloat16)
    values_ref[...] = jnp.transpose(pairs[:, width:]).astype(jnp.bfloat16)
    turned_ref[...] = jnp.transpose(query_ref[...].astype(jnp.float32)).astype(jnp.bfloat16)


def owner_kernel(n_lists, user_dev, digits, cap, scale, base_ref, gathered_ref, items_ref, *refs):
    out_hbm, out_ref, out_sems = refs
    items_loc, width = items_ref.shape
    vectors, ids = unpack(gathered_ref, n_lists, user_dev, digits, 0)
    index = asked(ids, base_ref[0].astype(jnp.float32), items_loc, 0, cap)
    scores = lax.dot_general(
        vectors.astype(jnp.bfloat16),
        items_ref[...],
        (((1,), (1,)), ((), ())),
        preferred_element_type=jnp.float32,
    )
    scores = (scores * scale).astype(jnp.bfloat16)
    pieces = items_loc // width
    stacked = jnp.concatenate(
        [scores[:, piece * width : (piece + 1) * width] for piece in range(pieces)], axis=0
    )
    kept = out_ref.shape[1] - cap
    entry = lax.broadcasted_iota(jnp.int32, (n_lists * kept, 1), 0)
    wanted = jnp.where(entry % kept < pieces * user_dev, entry % kept * n_lists + entry // kept, -1)
    spread = jnp.dot(
        picks(wanted, stacked.shape[0]), stacked, preferred_element_type=jnp.float32
    ).astype(jnp.bfloat16)
    out_ref[:, cap:, :] = spread.reshape(n_lists, kept, width)
    step = max(1, 256 // cap)
    sends = []
    for number, first in enumerate(range(0, n_lists, step)):
        last = min(n_lists, first + step)
        rows = jnp.dot(
            picks(jnp.concatenate(index[first:last], axis=0), items_loc),
            items_ref[...],
            preferred_element_type=jnp.float32,
        ).astype(jnp.bfloat16)
        out_ref[first:last, :cap, :] = rows.reshape(last - first, cap, width)
        send = pltpu.make_async_copy(out_ref.at[first:last], out_hbm.at[first:last], out_sems.at[number])
        send.start()
        sends.append(send)
    for send in sends:
        send.wait()


def place_kernel(n_users, col_ref, slot_ref, fetched_ref, *refs):
    share_refs, scratch = refs[:-1], refs[-1]
    n_lists, block, width = fetched_ref.shape
    fetched = fetched_ref[...].reshape(n_lists * block, width)
    share = share_refs[0].shape[0]
    slot = jnp.transpose(slot_ref[...])[:, :1].astype(jnp.int32)
    scratch[...] = jnp.dot(
        picks(slot, fetched.shape[0]), fetched, preferred_element_type=jnp.float32
    ).astype(jnp.bfloat16)
    for shift, ref in enumerate(share_refs):
        start = (col_ref[0] + shift) % n_users * share
        ref[...] = scratch[pl.ds(pl.multiple_of(start, share), share), :]


def attend_kernel(n_parts, *refs):
    parts, (keys_ref, values_ref, turned_ref, out_weight_ref, out_ref) = refs[:n_parts], refs[n_parts:]
    heads, events, features = keys_ref.shape
    head_dim = features - ROW_TILE
    rows = parts[0][...]
    for part in parts[1:]:
        rows = rows + part[...]
    queries = lax.dot_general(
        turned_ref[...], rows, (((1,), (1,)), ((), ())), preferred_element_type=jnp.float32
    )
    queries = (queries * head_dim ** (-0.5)).astype(jnp.bfloat16)
    feature = lax.broadcasted_iota(jnp.int32, (ROW_TILE, rows.shape[0]), 0)
    one = jnp.where(feature == 0, 1.0, 0.0).astype(jnp.bfloat16)

    def score(h):
        query = jnp.concatenate([queries[h * head_dim : (h + 1) * head_dim], one], axis=0)
        return jnp.dot(keys_ref[h], query, preferred_element_type=jnp.float32)

    ahead = [score(h) for h in range(min(2, heads))]
    mixed = []
    for h in range(heads):
        if h + 2 < heads:
            ahead.append(score(h + 2))
        exponentials = jnp.exp(ahead[h] - jnp.max(ahead[h], axis=0, keepdims=True))
        total = jnp.sum(exponentials, axis=0, keepdims=True)
        span = slice(h * head_dim, (h + 1) * head_dim)
        head = jnp.dot(values_ref[span, :], exponentials.astype(jnp.bfloat16), preferred_element_type=jnp.float32)
        mixed.append(head / total)
    attended = jnp.transpose(jnp.concatenate(mixed, axis=0)).astype(jnp.bfloat16)
    out_ref[...] = jnp.dot(attended, out_weight_ref[...], preferred_element_type=jnp.float32).astype(jnp.bfloat16)


def expand_kernel(user_dev, pieces, cap, probe_ref, fetched_ref, out_hbm, out_ref, sems):
    n_lists, block, width = fetched_ref.shape
    kept = block - cap
    rows = n_lists * kept
    returned = fetched_ref[:, cap:, :].reshape(rows, width)
    count = out_ref.shape[0]
    probe = jnp.transpose(probe_ref[:8, :])[:, :1].astype(jnp.int32)
    user = lax.broadcasted_iota(jnp.int32, (count, 1), 0) // (count // user_dev)
    sends = []
    for piece in range(pieces):
        wanted = probe * kept + piece * user_dev + user
        span = pl.ds(piece * width, width)
        out_ref[:, span] = jnp.dot(picks(wanted, rows), returned, preferred_element_type=jnp.float32).astype(
            jnp.bfloat16
        )
        sends.append(pltpu.make_async_copy(out_ref.at[:, span], out_hbm.at[:, span], sems.at[piece]))
        sends[-1].start()
    for send in sends:
        send.wait()


SMEM = pl.BlockSpec(memory_space=pltpu.SMEM)
VMEM = pl.BlockSpec(memory_space=pltpu.VMEM)
HBM = pl.BlockSpec(memory_space=pltpu.HBM)
PARAMS = pltpu.CompilerParams(vmem_limit_bytes=VMEM_BYTES)


def exchange(value):
    count = lax.axis_size("lists")
    group = sorted(range(count), key=lambda index: position(index, count))
    return lax.all_to_all(
        value, "lists", split_axis=0, concat_axis=0, axis_index_groups=[group], tiled=True
    )


def shards(
    user_vectors,
    probe_lists,
    list_items,
    candidate_ids,
    history,
    history_lengths,
    query_weight,
    key_value_weight,
    out_weight,
):
    n_lists = lax.axis_size("lists")
    n_users = lax.axis_size("users")
    _, items_loc, width = list_items.shape
    user_dev, probes = probe_lists.shape
    _, cands = candidate_ids.shape
    bf16 = jnp.bfloat16
    cap = max(2, 3 * cands // (n_lists * n_users))
    cap = round_up(cap, ROW_TILE)
    kept = round_up(items_loc // width * user_dev, ROW_TILE)
    share = cands // n_users
    pieces = items_loc // width
    digits = 1
    while BASE**digits < n_lists * n_users * items_loc:
        digits += 1
    pack_rows = round_up((user_dev + digits) * (width // LANES), 8)
    line = lax.axis_index("lists").astype(jnp.int32)
    col = lax.axis_index("users").astype(jnp.int32)
    col_arg = col.reshape(1)
    base_arg = ((line * n_users + col) * items_loc).reshape(1)
    block = cap + kept

    flat_items = list_items.reshape(items_loc, width)
    pack = pl.pallas_call(
        functools.partial(pack_kernel, digits),
        out_shape=jax.ShapeDtypeStruct((n_lists, pack_rows, LANES), bf16),
        in_specs=[VMEM, VMEM],
        out_specs=VMEM,
        compiler_params=pltpu.CompilerParams(vmem_limit_bytes=ALL_VMEM_BYTES),
    )(candidate_ids, user_vectors)
    gathered = exchange(pack)
    gathered = gathered.reshape(n_lists * pack_rows, LANES)

    items = pl.pallas_call(
        items_kernel,
        out_shape=jax.ShapeDtypeStruct((items_loc, width), bf16),
        in_specs=[HBM],
        out_specs=VMEM,
        scratch_shapes=[pltpu.SemaphoreType.DMA((4,))],
        compiler_params=PARAMS,
    )(flat_items)
    gathered, items = lax.optimization_barrier((gathered, items))

    slot, probe_row = pl.pallas_call(
        functools.partial(known_kernel, n_lists, items_loc, n_users, block),
        out_shape=(
            jax.ShapeDtypeStruct((8, cands), jnp.float32),
            jax.ShapeDtypeStruct((PROBE_ROWS, user_dev * probes), jnp.float32),
        ),
        in_specs=[SMEM, VMEM, VMEM],
        out_specs=(VMEM, VMEM),
        compiler_params=PARAMS,
    )(col_arg, candidate_ids, probe_lists)

    events = history.reshape(-1, width)
    hist = [events]
    for shift in range(1, n_users):
        hist.append(lax.ppermute(events, "users", [(i, (i + shift) % n_users) for i in range(n_users)]))
    total_events = n_users * events.shape[0]
    keys, values, turned = pl.pallas_call(
        functools.partial(pairs_kernel, n_users),
        out_shape=(
            jax.ShapeDtypeStruct((HEADS, total_events, width // HEADS + ROW_TILE), bf16),
            jax.ShapeDtypeStruct((width, total_events), bf16),
            jax.ShapeDtypeStruct((width, width), bf16),
        ),
        in_specs=[SMEM, SMEM] + [VMEM] * (n_users + 2),
        out_specs=(VMEM, VMEM, VMEM),
        compiler_params=PARAMS,
    )(col_arg, history_lengths, *hist, key_value_weight, query_weight)

    step = max(1, 256 // cap)
    answers = pl.pallas_call(
        functools.partial(owner_kernel, n_lists, user_dev, digits, cap, width ** (-0.5)),
        out_shape=jax.ShapeDtypeStruct((n_lists, block, width), bf16),
        in_specs=[SMEM, VMEM, VMEM],
        out_specs=pl.BlockSpec(memory_space=pl.ANY),
        scratch_shapes=[
            pltpu.VMEM((n_lists, block, width), bf16),
            pltpu.SemaphoreType.DMA((-(-n_lists // step),)),
        ],
        compiler_params=PARAMS,
    )(base_arg, gathered, items)
    fetched = exchange(answers)

    fetched, slot, probe_row, keys, values, turned = lax.optimization_barrier(
        (fetched, slot, probe_row, keys, values, turned)
    )

    placed = pl.pallas_call(
        functools.partial(place_kernel, n_users),
        out_shape=tuple(jax.ShapeDtypeStruct((share, width), bf16) for _ in range(n_users)),
        in_specs=[SMEM, VMEM, VMEM],
        out_specs=tuple(VMEM for _ in range(n_users)),
        scratch_shapes=[pltpu.VMEM((cands, width), bf16)],
        compiler_params=PARAMS,
    )(col_arg, slot, fetched)
    parts = [placed[0]]
    for shift in range(1, n_users):
        parts.append(
            lax.ppermute(placed[shift], "users", [(i, (i + shift) % n_users) for i in range(n_users)])
        )
    ranked = pl.pallas_call(
        functools.partial(attend_kernel, n_users),
        out_shape=jax.ShapeDtypeStruct((share, width), bf16),
        in_specs=[VMEM] * (n_users + 4),
        out_specs=VMEM,
        compiler_params=PARAMS,
    )(*parts, keys, values, turned, out_weight)

    list_scores = pl.pallas_call(
        functools.partial(expand_kernel, user_dev, pieces, cap),
        out_shape=jax.ShapeDtypeStruct((user_dev * probes, items_loc), bf16),
        in_specs=[VMEM, VMEM],
        out_specs=pl.BlockSpec(memory_space=pl.ANY),
        scratch_shapes=[
            pltpu.VMEM((user_dev * probes, items_loc), bf16),
            pltpu.SemaphoreType.DMA((pieces,)),
        ],
        compiler_params=PARAMS,
    )(probe_row, fetched)
    return (list_scores.reshape(user_dev, probes, items_loc), ranked.reshape(1, share, width))


def solution(mesh):
    placed = (
        P("lists", None),
        P("lists", None),
        P("lists", "users", None),
        P("lists", None),
        P("lists", "users", None),
        P("lists"),
        P(),
        P(),
        P(),
    )
    return jax.shard_map(
        shards,
        mesh=mesh,
        in_specs=placed,
        out_specs=(P("lists", None, "users"), P("lists", "users", None)),
        check_vma=False,
    )
```

```python
import functools

import jax
import jax.numpy as jnp
from jax import lax
from jax.experimental import pallas as pl
from jax.experimental.pallas import tpu as pltpu
from jax.sharding import PartitionSpec as P

HEADS = 8
BASE = 256
LANES = 128
ROW_TILE = 16
VMEM_BYTES = 28 * 1024 * 1024
ALL_VMEM_BYTES = 62 * 1024 * 1024


def round_up(value, step):
    return (value + step - 1) // step * step


def picks(index, count):
    place = lax.broadcasted_iota(jnp.int32, (index.shape[0], count), 1).astype(jnp.int16)
    one, zero = jnp.bfloat16(1.0), jnp.bfloat16(0.0)
    return jnp.where(index.astype(jnp.int16) == place, one, zero)


def pack_kernel(digits, ids_ref, vectors_ref, pack_ref):
    width = vectors_ref.shape[1]
    vectors = vectors_ref[...].astype(jnp.float32)
    ids = ids_ref[...]
    spans = [slice(start, start + LANES) for start in range(0, width, LANES)]
    rows = [vectors[:, span] for span in spans]
    for digit in range(digits):
        value = ((ids >> (8 * digit)) & (BASE - 1)).astype(jnp.float32)
        rows += [value[:, span] for span in spans]
    count = sum(row.shape[0] for row in rows)
    if pack_ref.shape[1] > count:
        rows.append(jnp.zeros((pack_ref.shape[1] - count, LANES), jnp.float32))
    pack_ref[...] = jnp.broadcast_to(jnp.concatenate(rows, axis=0).astype(jnp.bfloat16)[None], pack_ref.shape)


def earlier(count):
    row = lax.broadcasted_iota(jnp.int32, (count, count), 0)
    column = lax.broadcasted_iota(jnp.int32, (count, count), 1)
    return jnp.where(row < column, 1.0, 0.0).astype(jnp.bfloat16)


def unpack(gathered_ref, n_lists, user_dev, digits, turn):
    pack_rows = gathered_ref.shape[0] // n_lists
    spans = pack_rows // (user_dev + digits)
    entry = lax.broadcasted_iota(jnp.int32, ((user_dev + digits) * n_lists, 1), 0)
    asker, field = (entry % n_lists) ^ turn, entry // n_lists
    fields = jnp.concatenate(
        [
            jnp.dot(
                picks(
                    asker * pack_rows
                    + jnp.where(field < user_dev, span * user_dev + field, field * spans + span),
                    n_lists * pack_rows,
                ),
                gathered_ref[...],
                preferred_element_type=jnp.float32,
            )
            for span in range(spans)
        ],
        axis=1,
    )
    ids = jnp.zeros((n_lists, fields.shape[1]), jnp.float32)
    for digit in range(digits):
        ids = ids + fields[(user_dev + digit) * n_lists : (user_dev + digit + 1) * n_lists] * float(BASE**digit)
    return fields[: user_dev * n_lists], ids


def asked(ids, base, items_loc, first, count):
    local = ids - base
    mine = (local >= 0.0) & (local < items_loc)
    hot = jnp.where(mine, 1.0, 0.0).astype(jnp.bfloat16)
    rank = jnp.dot(hot, earlier(ids.shape[1]), preferred_element_type=jnp.float32)
    rank = jnp.where(mine, rank, -1.0)
    place = lax.broadcasted_iota(jnp.int32, (count, ids.shape[1]), 0).astype(jnp.float32) + float(first)
    index = []
    for r in range(ids.shape[0]):
        picked = jnp.where(rank[r : r + 1] == place, local[r : r + 1] + 1.0, 0.0)
        index.append(jnp.sum(picked, axis=1, keepdims=True).astype(jnp.int32) - 1)
    return index


def items_kernel(items_hbm, items_ref, sems):
    part = items_ref.shape[0] // sems.shape[0]
    loads = []
    for p in range(sems.shape[0]):
        span = pl.ds(p * part, part)
        loads.append(pltpu.make_async_copy(items_hbm.at[span], items_ref.at[span], sems.at[p]))
        loads[-1].start()
    for load in loads:
        load.wait()


def known_kernel(n_lists, items_loc, n_users, block, col_ref, ids_ref, probes_ref, known_ref):
    ids = ids_ref[...]
    cands = ids.shape[1]
    bins = ids // items_loc
    mine = bins % n_users == col_ref[0]
    owner = bins // n_users
    lists = lax.broadcasted_iota(jnp.int32, (n_lists, cands), 0)
    hot = jnp.where((lists == owner) & mine, 1.0, 0.0)
    before = jnp.dot(hot.astype(jnp.bfloat16), earlier(cands), preferred_element_type=jnp.float32)
    rank = jnp.sum(before * hot, axis=0, keepdims=True)
    slot = jnp.where(mine, owner.astype(jnp.float32) * block + rank, -1.0)
    probes = probes_ref[...].astype(jnp.float32)
    flat = jnp.concatenate([probes[u : u + 1] for u in range(probes.shape[0])], axis=1)
    if flat.shape[1] < cands:
        flat = jnp.concatenate([flat, jnp.zeros((1, cands - flat.shape[1]), jnp.float32)], axis=1)
    row = lax.broadcasted_iota(jnp.int32, known_ref.shape, 0)
    known_ref[...] = jnp.where(row == 0, slot, flat)


def pairs_kernel(n_parts, col_ref, length_ref, *refs):
    parts, (weight_ref, query_ref, keys_ref, values_ref, turned_ref) = refs[:n_parts], refs[n_parts:]
    history = jnp.concatenate([part[...] for part in parts], axis=0)
    pairs = jnp.dot(history, weight_ref[...], preferred_element_type=jnp.float32)
    heads, events, features = keys_ref.shape
    head_dim = features - ROW_TILE
    width = heads * head_dim
    hist_dev = events // n_parts
    event = lax.broadcasted_iota(jnp.int32, (events, ROW_TILE), 0)
    feature = lax.broadcasted_iota(jnp.int32, (events, ROW_TILE), 1)
    position = (col_ref[0] - event // hist_dev + n_parts) % n_parts * hist_dev + event % hist_dev
    mask = jnp.where((position >= length_ref[0]) & (feature == 0), -1e30, 0.0)
    for h in range(heads):
        keys = pairs[:, h * head_dim : (h + 1) * head_dim]
        keys_ref[h] = jnp.concatenate([keys, mask], axis=1).astype(jnp.bfloat16)
    values_ref[...] = jnp.transpose(pairs[:, width:]).astype(jnp.bfloat16)
    turned_ref[...] = jnp.transpose(query_ref[...].astype(jnp.float32)).astype(jnp.bfloat16)


def owner_kernel(n_lists, user_dev, digits, cap, scale, base_ref, gathered_ref, items_ref, *refs):
    out_hbm, out_ref, out_sems = refs
    items_loc, width = items_ref.shape
    vectors, ids = unpack(gathered_ref, n_lists, user_dev, digits, 0)
    index = asked(ids, base_ref[0].astype(jnp.float32), items_loc, 0, cap)
    scores = lax.dot_general(
        vectors.astype(jnp.bfloat16),
        items_ref[...],
        (((1,), (1,)), ((), ())),
        preferred_element_type=jnp.float32,
    )
    scores = (scores * scale).astype(jnp.bfloat16)
    pieces = items_loc // width
    stacked = jnp.concatenate(
        [scores[:, piece * width : (piece + 1) * width] for piece in range(pieces)], axis=0
    )
    kept = out_ref.shape[1] - cap
    entry = lax.broadcasted_iota(jnp.int32, (n_lists * kept, 1), 0)
    wanted = jnp.where(entry % kept < pieces * user_dev, entry % kept * n_lists + entry // kept, -1)
    spread = jnp.dot(
        picks(wanted, stacked.shape[0]), stacked, preferred_element_type=jnp.float32
    ).astype(jnp.bfloat16)
    out_ref[:, cap:, :] = spread.reshape(n_lists, kept, width)
    step = max(1, 256 // cap)
    sends = []
    for number, first in enumerate(range(0, n_lists, step)):
        last = min(n_lists, first + step)
        rows = jnp.dot(
            picks(jnp.concatenate(index[first:last], axis=0), items_loc),
            items_ref[...],
            preferred_element_type=jnp.float32,
        ).astype(jnp.bfloat16)
        out_ref[first:last, :cap, :] = rows.reshape(last - first, cap, width)
        send = pltpu.make_async_copy(out_ref.at[first:last], out_hbm.at[first:last], out_sems.at[number])
        send.start()
        sends.append(send)
    for send in sends:
        send.wait()


def place_kernel(n_users, col_ref, known_ref, fetched_ref, *refs):
    share_refs, scratch = refs[:-1], refs[-1]
    n_lists, block, width = fetched_ref.shape
    fetched = fetched_ref[...].reshape(n_lists * block, width)
    share = share_refs[0].shape[0]
    slot = jnp.transpose(known_ref[...])[:, :1].astype(jnp.int32)
    scratch[...] = jnp.dot(
        picks(slot, fetched.shape[0]), fetched, preferred_element_type=jnp.float32
    ).astype(jnp.bfloat16)
    for shift, ref in enumerate(share_refs):
        start = (col_ref[0] + shift) % n_users * share
        ref[...] = scratch[pl.ds(pl.multiple_of(start, share), share), :]


def attend_kernel(n_parts, *refs):
    parts, (keys_ref, values_ref, turned_ref, out_weight_ref, out_ref) = refs[:n_parts], refs[n_parts:]
    heads, events, features = keys_ref.shape
    head_dim = features - ROW_TILE
    rows = parts[0][...]
    for part in parts[1:]:
        rows = rows + part[...]
    queries = lax.dot_general(
        turned_ref[...], rows, (((1,), (1,)), ((), ())), preferred_element_type=jnp.float32
    )
    queries = (queries * head_dim ** (-0.5)).astype(jnp.bfloat16)
    feature = lax.broadcasted_iota(jnp.int32, (ROW_TILE, rows.shape[0]), 0)
    one = jnp.where(feature == 0, 1.0, 0.0).astype(jnp.bfloat16)

    def score(h):
        query = jnp.concatenate([queries[h * head_dim : (h + 1) * head_dim], one], axis=0)
        return jnp.dot(keys_ref[h], query, preferred_element_type=jnp.float32)

    ahead = [score(h) for h in range(min(2, heads))]
    mixed = []
    for h in range(heads):
        if h + 2 < heads:
            ahead.append(score(h + 2))
        exponentials = jnp.exp(ahead[h] - jnp.max(ahead[h], axis=0, keepdims=True))
        total = jnp.sum(exponentials, axis=0, keepdims=True)
        span = slice(h * head_dim, (h + 1) * head_dim)
        head = jnp.dot(values_ref[span, :], exponentials.astype(jnp.bfloat16), preferred_element_type=jnp.float32)
        mixed.append(head / total)
    attended = jnp.transpose(jnp.concatenate(mixed, axis=0)).astype(jnp.bfloat16)
    out_ref[...] = jnp.dot(attended, out_weight_ref[...], preferred_element_type=jnp.float32).astype(jnp.bfloat16)


def expand_kernel(user_dev, pieces, cap, known_ref, fetched_ref, out_hbm, out_ref, sems):
    n_lists, block, width = fetched_ref.shape
    kept = block - cap
    rows = n_lists * kept
    returned = fetched_ref[:, cap:, :].reshape(rows, width)
    count = out_ref.shape[0]
    probe = jnp.transpose(known_ref[:, :count])[:, 1:2].astype(jnp.int32)
    user = lax.broadcasted_iota(jnp.int32, (count, 1), 0) // (count // user_dev)
    sends = []
    for piece in range(pieces):
        wanted = probe * kept + piece * user_dev + user
        span = pl.ds(piece * width, width)
        out_ref[:, span] = jnp.dot(picks(wanted, rows), returned, preferred_element_type=jnp.float32).astype(
            jnp.bfloat16
        )
        sends.append(pltpu.make_async_copy(out_ref.at[:, span], out_hbm.at[:, span], sems.at[piece]))
        sends[-1].start()
    for send in sends:
        send.wait()


SMEM = pl.BlockSpec(memory_space=pltpu.SMEM)
VMEM = pl.BlockSpec(memory_space=pltpu.VMEM)
HBM = pl.BlockSpec(memory_space=pltpu.HBM)
PARAMS = pltpu.CompilerParams(vmem_limit_bytes=VMEM_BYTES)


def exchange(value):
    return lax.all_to_all(value, "lists", split_axis=0, concat_axis=0, tiled=True)


def shards(
    user_vectors,
    probe_lists,
    list_items,
    candidate_ids,
    history,
    history_lengths,
    query_weight,
    key_value_weight,
    out_weight,
):
    n_lists = lax.axis_size("lists")
    n_users = lax.axis_size("users")
    _, items_loc, width = list_items.shape
    user_dev, probes = probe_lists.shape
    _, cands = candidate_ids.shape
    bf16 = jnp.bfloat16
    cap = max(2, 3 * cands // (n_lists * n_users))
    cap = round_up(cap, ROW_TILE)
    kept = round_up(items_loc // width * user_dev, ROW_TILE)
    share = cands // n_users
    pieces = items_loc // width
    digits = 1
    while BASE**digits < n_lists * n_users * items_loc:
        digits += 1
    pack_rows = round_up((user_dev + digits) * (width // LANES), 8)
    line = lax.axis_index("lists").astype(jnp.int32)
    col = lax.axis_index("users").astype(jnp.int32)
    col_arg = col.reshape(1)
    base_arg = ((line * n_users + col) * items_loc).reshape(1)
    block = cap + kept

    flat_items = list_items.reshape(items_loc, width)
    pack = pl.pallas_call(
        functools.partial(pack_kernel, digits),
        out_shape=jax.ShapeDtypeStruct((n_lists, pack_rows, LANES), bf16),
        in_specs=[VMEM, VMEM],
        out_specs=VMEM,
        compiler_params=pltpu.CompilerParams(vmem_limit_bytes=ALL_VMEM_BYTES),
    )(candidate_ids, user_vectors)
    gathered = exchange(pack)
    gathered = gathered.reshape(n_lists * pack_rows, LANES)

    items = pl.pallas_call(
        items_kernel,
        out_shape=jax.ShapeDtypeStruct((items_loc, width), bf16),
        in_specs=[HBM],
        out_specs=VMEM,
        scratch_shapes=[pltpu.SemaphoreType.DMA((4,))],
        compiler_params=PARAMS,
    )(flat_items)
    gathered, items = lax.optimization_barrier((gathered, items))

    known = pl.pallas_call(
        functools.partial(known_kernel, n_lists, items_loc, n_users, block),
        out_shape=jax.ShapeDtypeStruct((8, cands), jnp.float32),
        in_specs=[SMEM, VMEM, VMEM],
        out_specs=VMEM,
        compiler_params=PARAMS,
    )(col_arg, candidate_ids, probe_lists)

    events = history.reshape(-1, width)
    hist = [events]
    for shift in range(1, n_users):
        hist.append(lax.ppermute(events, "users", [(i, (i + shift) % n_users) for i in range(n_users)]))
    total_events = n_users * events.shape[0]
    keys, values, turned = pl.pallas_call(
        functools.partial(pairs_kernel, n_users),
        out_shape=(
            jax.ShapeDtypeStruct((HEADS, total_events, width // HEADS + ROW_TILE), bf16),
            jax.ShapeDtypeStruct((width, total_events), bf16),
            jax.ShapeDtypeStruct((width, width), bf16),
        ),
        in_specs=[SMEM, SMEM] + [VMEM] * (n_users + 2),
        out_specs=(VMEM, VMEM, VMEM),
        compiler_params=PARAMS,
    )(col_arg, history_lengths, *hist, key_value_weight, query_weight)

    step = max(1, 256 // cap)
    answers = pl.pallas_call(
        functools.partial(owner_kernel, n_lists, user_dev, digits, cap, width ** (-0.5)),
        out_shape=jax.ShapeDtypeStruct((n_lists, block, width), bf16),
        in_specs=[SMEM, VMEM, VMEM],
        out_specs=pl.BlockSpec(memory_space=pl.ANY),
        scratch_shapes=[
            pltpu.VMEM((n_lists, block, width), bf16),
            pltpu.SemaphoreType.DMA((-(-n_lists // step),)),
        ],
        compiler_params=PARAMS,
    )(base_arg, gathered, items)
    fetched = exchange(answers)

    fetched, known, keys, values, turned = lax.optimization_barrier((fetched, known, keys, values, turned))

    placed = pl.pallas_call(
        functools.partial(place_kernel, n_users),
        out_shape=tuple(jax.ShapeDtypeStruct((share, width), bf16) for _ in range(n_users)),
        in_specs=[SMEM, VMEM, VMEM],
        out_specs=tuple(VMEM for _ in range(n_users)),
        scratch_shapes=[pltpu.VMEM((cands, width), bf16)],
        compiler_params=PARAMS,
    )(col_arg, known, fetched)
    parts = [placed[0]]
    for shift in range(1, n_users):
        parts.append(
            lax.ppermute(placed[shift], "users", [(i, (i + shift) % n_users) for i in range(n_users)])
        )
    ranked = pl.pallas_call(
        functools.partial(attend_kernel, n_users),
        out_shape=jax.ShapeDtypeStruct((share, width), bf16),
        in_specs=[VMEM] * (n_users + 4),
        out_specs=VMEM,
        compiler_params=PARAMS,
    )(*parts, keys, values, turned, out_weight)

    list_scores = pl.pallas_call(
        functools.partial(expand_kernel, user_dev, pieces, cap),
        out_shape=jax.ShapeDtypeStruct((user_dev * probes, items_loc), bf16),
        in_specs=[VMEM, VMEM],
        out_specs=pl.BlockSpec(memory_space=pl.ANY),
        scratch_shapes=[
            pltpu.VMEM((user_dev * probes, items_loc), bf16),
            pltpu.SemaphoreType.DMA((pieces,)),
        ],
        compiler_params=PARAMS,
    )(known, fetched)
    return (list_scores.reshape(user_dev, probes, items_loc), ranked.reshape(1, share, width))


def solution(mesh):
    placed = (
        P("lists", None),
        P("lists", None),
        P("lists", "users", None),
        P("lists", None),
        P("lists", "users", None),
        P("lists"),
        P(),
        P(),
        P(),
    )
    return jax.shard_map(
        shards,
        mesh=mesh,
        in_specs=placed,
        out_specs=(P("lists", None, "users"), P("lists", "users", None)),
        check_vma=False,
    )
```

```python
import functools

import jax
import jax.numpy as jnp
from jax import lax
from jax.experimental import pallas as pl
from jax.experimental.pallas import tpu as pltpu
from jax.sharding import PartitionSpec as P

HEADS = 8
BASE = 256
LANES = 128
ROW_TILE = 16
VMEM_BYTES = 28 * 1024 * 1024
ALL_VMEM_BYTES = 62 * 1024 * 1024


def round_up(value, step):
    return (value + step - 1) // step * step


def picks(index, count):
    place = lax.broadcasted_iota(jnp.int32, (index.shape[0], count), 1).astype(jnp.int16)
    one, zero = jnp.bfloat16(1.0), jnp.bfloat16(0.0)
    return jnp.where(index.astype(jnp.int16) == place, one, zero)


def pack_kernel(digits, ids_ref, vectors_ref, pack_ref):
    width = vectors_ref.shape[1]
    vectors = vectors_ref[...].astype(jnp.float32)
    ids = ids_ref[...]
    spans = [slice(start, start + LANES) for start in range(0, width, LANES)]
    rows = [vectors[:, span] for span in spans]
    for digit in range(digits):
        value = ((ids >> (8 * digit)) & (BASE - 1)).astype(jnp.float32)
        rows += [value[:, span] for span in spans]
    count = sum(row.shape[0] for row in rows)
    if pack_ref.shape[1] > count:
        rows.append(jnp.zeros((pack_ref.shape[1] - count, LANES), jnp.float32))
    pack_ref[...] = jnp.broadcast_to(jnp.concatenate(rows, axis=0).astype(jnp.bfloat16)[None], pack_ref.shape)


def earlier(count):
    row = lax.broadcasted_iota(jnp.int32, (count, count), 0)
    column = lax.broadcasted_iota(jnp.int32, (count, count), 1)
    return jnp.where(row < column, 1.0, 0.0).astype(jnp.bfloat16)


def unpack(gathered_ref, n_lists, user_dev, digits, turn):
    pack_rows = gathered_ref.shape[0] // n_lists
    spans = pack_rows // (user_dev + digits)
    entry = lax.broadcasted_iota(jnp.int32, ((user_dev + digits) * n_lists, 1), 0)
    asker, field = (entry % n_lists) ^ turn, entry // n_lists
    fields = jnp.concatenate(
        [
            jnp.dot(
                picks(
                    asker * pack_rows
                    + jnp.where(field < user_dev, span * user_dev + field, field * spans + span),
                    n_lists * pack_rows,
                ),
                gathered_ref[...],
                preferred_element_type=jnp.float32,
            )
            for span in range(spans)
        ],
        axis=1,
    )
    ids = jnp.zeros((n_lists, fields.shape[1]), jnp.float32)
    for digit in range(digits):
        ids = ids + fields[(user_dev + digit) * n_lists : (user_dev + digit + 1) * n_lists] * float(BASE**digit)
    return fields[: user_dev * n_lists], ids


def asked(ids, base, items_loc, first, count):
    local = ids - base
    mine = (local >= 0.0) & (local < items_loc)
    hot = jnp.where(mine, 1.0, 0.0).astype(jnp.bfloat16)
    rank = jnp.dot(hot, earlier(ids.shape[1]), preferred_element_type=jnp.float32)
    rank = jnp.where(mine, rank, -1.0)
    place = lax.broadcasted_iota(jnp.int32, (count, ids.shape[1]), 0).astype(jnp.float32) + float(first)
    index = []
    for r in range(ids.shape[0]):
        picked = jnp.where(rank[r : r + 1] == place, local[r : r + 1] + 1.0, 0.0)
        index.append(jnp.sum(picked, axis=1, keepdims=True).astype(jnp.int32) - 1)
    return index


def items_kernel(items_hbm, items_ref, sems):
    part = items_ref.shape[0] // sems.shape[0]
    loads = []
    for p in range(sems.shape[0]):
        span = pl.ds(p * part, part)
        loads.append(pltpu.make_async_copy(items_hbm.at[span], items_ref.at[span], sems.at[p]))
        loads[-1].start()
    for load in loads:
        load.wait()


def known_kernel(n_lists, items_loc, n_users, block, col_ref, ids_ref, probes_ref, known_ref):
    ids = ids_ref[...]
    cands = ids.shape[1]
    bins = ids // items_loc
    mine = bins % n_users == col_ref[0]
    owner = bins // n_users
    lists = lax.broadcasted_iota(jnp.int32, (n_lists, cands), 0)
    hot = jnp.where((lists == owner) & mine, 1.0, 0.0)
    before = jnp.dot(hot.astype(jnp.bfloat16), earlier(cands), preferred_element_type=jnp.float32)
    rank = jnp.sum(before * hot, axis=0, keepdims=True)
    slot = jnp.where(mine, owner.astype(jnp.float32) * block + rank, -1.0)
    probes = probes_ref[...].astype(jnp.float32)
    flat = jnp.concatenate([probes[u : u + 1] for u in range(probes.shape[0])], axis=1)
    if flat.shape[1] < cands:
        flat = jnp.concatenate([flat, jnp.zeros((1, cands - flat.shape[1]), jnp.float32)], axis=1)
    row = lax.broadcasted_iota(jnp.int32, known_ref.shape, 0)
    known_ref[...] = jnp.where(row == 0, slot, flat)


def pairs_kernel(n_parts, col_ref, length_ref, *refs):
    parts, (weight_ref, query_ref, keys_ref, values_ref, turned_ref) = refs[:n_parts], refs[n_parts:]
    history = jnp.concatenate([part[...] for part in parts], axis=0)
    pairs = jnp.dot(history, weight_ref[...], preferred_element_type=jnp.float32)
    heads, events, features = keys_ref.shape
    head_dim = features - ROW_TILE
    width = heads * head_dim
    hist_dev = events // n_parts
    event = lax.broadcasted_iota(jnp.int32, (events, ROW_TILE), 0)
    feature = lax.broadcasted_iota(jnp.int32, (events, ROW_TILE), 1)
    position = (col_ref[0] - event // hist_dev + n_parts) % n_parts * hist_dev + event % hist_dev
    mask = jnp.where((position >= length_ref[0]) & (feature == 0), -1e30, 0.0)
    for h in range(heads):
        keys = pairs[:, h * head_dim : (h + 1) * head_dim]
        keys_ref[h] = jnp.concatenate([keys, mask], axis=1).astype(jnp.bfloat16)
    values_ref[...] = jnp.transpose(pairs[:, width:]).astype(jnp.bfloat16)
    turned_ref[...] = jnp.transpose(query_ref[...].astype(jnp.float32)).astype(jnp.bfloat16)


def owner_kernel(n_lists, user_dev, digits, cap, scale, base_ref, gathered_ref, items_ref, *refs):
    out_hbm, out_ref, out_sems = refs
    items_loc, width = items_ref.shape
    vectors, ids = unpack(gathered_ref, n_lists, user_dev, digits, 0)
    index = asked(ids, base_ref[0].astype(jnp.float32), items_loc, 0, cap)
    scores = lax.dot_general(
        vectors.astype(jnp.bfloat16),
        items_ref[...],
        (((1,), (1,)), ((), ())),
        preferred_element_type=jnp.float32,
    )
    scores = (scores * scale).astype(jnp.bfloat16)
    pieces = items_loc // width
    stacked = jnp.concatenate(
        [scores[:, piece * width : (piece + 1) * width] for piece in range(pieces)], axis=0
    )
    kept = out_ref.shape[1] - cap
    entry = lax.broadcasted_iota(jnp.int32, (n_lists * kept, 1), 0)
    wanted = jnp.where(entry % kept < pieces * user_dev, entry % kept * n_lists + entry // kept, -1)
    spread = jnp.dot(
        picks(wanted, stacked.shape[0]), stacked, preferred_element_type=jnp.float32
    ).astype(jnp.bfloat16)
    out_ref[:, cap:, :] = spread.reshape(n_lists, kept, width)
    step = max(1, 384 // cap)
    sends = []
    for number, first in enumerate(range(0, n_lists, step)):
        last = min(n_lists, first + step)
        rows = jnp.dot(
            picks(jnp.concatenate(index[first:last], axis=0), items_loc),
            items_ref[...],
            preferred_element_type=jnp.float32,
        ).astype(jnp.bfloat16)
        out_ref[first:last, :cap, :] = rows.reshape(last - first, cap, width)
        send = pltpu.make_async_copy(out_ref.at[first:last], out_hbm.at[first:last], out_sems.at[number])
        send.start()
        sends.append(send)
    for send in sends:
        send.wait()


def placed(column, known_ref, slots, fetched_ref, out_ref):
    n_lists, block, width = fetched_ref.shape
    share = out_ref.shape[0]
    slots[...] = jnp.transpose(known_ref[...])
    start = pl.multiple_of(column * share, share)
    slot = slots[pl.ds(start, share), :][:, :1].astype(jnp.int32)
    out_ref[...] = jnp.dot(
        picks(slot, n_lists * block),
        fetched_ref[...].reshape(n_lists * block, width),
        preferred_element_type=jnp.float32,
    ).astype(jnp.bfloat16)


def place_kernel(n_users, col_ref, known_ref, fetched_ref, *refs):
    sent_refs, slots = refs[:-1], refs[-1]
    for shift, ref in enumerate(sent_refs):
        placed((col_ref[0] + shift + 1) % n_users, known_ref, slots, fetched_ref, ref)


def attend_kernel(n_parts, *refs):
    parts, (keys_ref, values_ref, turned_ref, out_weight_ref, out_ref) = refs[:n_parts], refs[n_parts:]
    heads, events, features = keys_ref.shape
    head_dim = features - ROW_TILE
    rows = parts[0][...]
    for part in parts[1:]:
        rows = rows + part[...]
    queries = lax.dot_general(
        turned_ref[...], rows, (((1,), (1,)), ((), ())), preferred_element_type=jnp.float32
    )
    queries = (queries * head_dim ** (-0.5)).astype(jnp.bfloat16)
    feature = lax.broadcasted_iota(jnp.int32, (ROW_TILE, rows.shape[0]), 0)
    one = jnp.where(feature == 0, 1.0, 0.0).astype(jnp.bfloat16)

    def score(h):
        query = jnp.concatenate([queries[h * head_dim : (h + 1) * head_dim], one], axis=0)
        return jnp.dot(keys_ref[h], query, preferred_element_type=jnp.float32)

    ahead = [score(h) for h in range(min(2, heads))]
    mixed = []
    for h in range(heads):
        if h + 2 < heads:
            ahead.append(score(h + 2))
        exponentials = jnp.exp(ahead[h] - jnp.max(ahead[h], axis=0, keepdims=True))
        total = jnp.sum(exponentials, axis=0, keepdims=True)
        span = slice(h * head_dim, (h + 1) * head_dim)
        head = jnp.dot(values_ref[span, :], exponentials.astype(jnp.bfloat16), preferred_element_type=jnp.float32)
        mixed.append(head / total)
    attended = jnp.transpose(jnp.concatenate(mixed, axis=0)).astype(jnp.bfloat16)
    out_ref[...] = jnp.dot(attended, out_weight_ref[...], preferred_element_type=jnp.float32).astype(jnp.bfloat16)


def expand_kernel(user_dev, pieces, cap, col_ref, known_ref, fetched_ref, out_hbm, own_ref, out_ref, slots, sems):
    n_lists, block, width = fetched_ref.shape
    kept = block - cap
    rows = n_lists * kept
    returned = fetched_ref[:, cap:, :].reshape(rows, width)
    count = out_ref.shape[0]
    probe = jnp.transpose(known_ref[:, :count])[:, 1:2].astype(jnp.int32)
    user = lax.broadcasted_iota(jnp.int32, (count, 1), 0) // (count // user_dev)
    sends = []
    for piece in range(pieces):
        wanted = probe * kept + piece * user_dev + user
        span = pl.ds(piece * width, width)
        out_ref[:, span] = jnp.dot(picks(wanted, rows), returned, preferred_element_type=jnp.float32).astype(
            jnp.bfloat16
        )
        sends.append(pltpu.make_async_copy(out_ref.at[:, span], out_hbm.at[:, span], sems.at[piece]))
        sends[-1].start()
    placed(col_ref[0], known_ref, slots, fetched_ref, own_ref)
    for send in sends:
        send.wait()


SMEM = pl.BlockSpec(memory_space=pltpu.SMEM)
VMEM = pl.BlockSpec(memory_space=pltpu.VMEM)
HBM = pl.BlockSpec(memory_space=pltpu.HBM)
PARAMS = pltpu.CompilerParams(vmem_limit_bytes=VMEM_BYTES)


def exchange(value):
    return lax.all_to_all(value, "lists", split_axis=0, concat_axis=0, tiled=True)


def shards(
    user_vectors,
    probe_lists,
    list_items,
    candidate_ids,
    history,
    history_lengths,
    query_weight,
    key_value_weight,
    out_weight,
):
    n_lists = lax.axis_size("lists")
    n_users = lax.axis_size("users")
    _, items_loc, width = list_items.shape
    user_dev, probes = probe_lists.shape
    _, cands = candidate_ids.shape
    bf16 = jnp.bfloat16
    cap = max(2, 3 * cands // (n_lists * n_users))
    cap = round_up(cap, ROW_TILE)
    kept = round_up(items_loc // width * user_dev, ROW_TILE)
    share = cands // n_users
    pieces = items_loc // width
    digits = 1
    while BASE**digits < n_lists * n_users * items_loc:
        digits += 1
    pack_rows = round_up((user_dev + digits) * (width // LANES), 8)
    line = lax.axis_index("lists").astype(jnp.int32)
    col = lax.axis_index("users").astype(jnp.int32)
    col_arg = col.reshape(1)
    base_arg = ((line * n_users + col) * items_loc).reshape(1)
    block = cap + kept

    flat_items = list_items.reshape(items_loc, width)
    pack = pl.pallas_call(
        functools.partial(pack_kernel, digits),
        out_shape=jax.ShapeDtypeStruct((n_lists, pack_rows, LANES), bf16),
        in_specs=[VMEM, VMEM],
        out_specs=VMEM,
        compiler_params=pltpu.CompilerParams(vmem_limit_bytes=ALL_VMEM_BYTES),
    )(candidate_ids, user_vectors)
    gathered = exchange(pack)
    gathered = gathered.reshape(n_lists * pack_rows, LANES)

    items = pl.pallas_call(
        items_kernel,
        out_shape=jax.ShapeDtypeStruct((items_loc, width), bf16),
        in_specs=[HBM],
        out_specs=VMEM,
        scratch_shapes=[pltpu.SemaphoreType.DMA((4,))],
        compiler_params=PARAMS,
    )(flat_items)
    gathered, items = lax.optimization_barrier((gathered, items))

    known = pl.pallas_call(
        functools.partial(known_kernel, n_lists, items_loc, n_users, block),
        out_shape=jax.ShapeDtypeStruct((8, cands), jnp.float32),
        in_specs=[SMEM, VMEM, VMEM],
        out_specs=VMEM,
        compiler_params=PARAMS,
    )(col_arg, candidate_ids, probe_lists)

    events = history.reshape(-1, width)
    hist = [events]
    for shift in range(1, n_users):
        hist.append(lax.ppermute(events, "users", [(i, (i + shift) % n_users) for i in range(n_users)]))
    total_events = n_users * events.shape[0]
    keys, values, turned = pl.pallas_call(
        functools.partial(pairs_kernel, n_users),
        out_shape=(
            jax.ShapeDtypeStruct((HEADS, total_events, width // HEADS + ROW_TILE), bf16),
            jax.ShapeDtypeStruct((width, total_events), bf16),
            jax.ShapeDtypeStruct((width, width), bf16),
        ),
        in_specs=[SMEM, SMEM] + [VMEM] * (n_users + 2),
        out_specs=(VMEM, VMEM, VMEM),
        compiler_params=PARAMS,
    )(col_arg, history_lengths, *hist, key_value_weight, query_weight)

    step = max(1, 384 // cap)
    answers = pl.pallas_call(
        functools.partial(owner_kernel, n_lists, user_dev, digits, cap, width ** (-0.5)),
        out_shape=jax.ShapeDtypeStruct((n_lists, block, width), bf16),
        in_specs=[SMEM, VMEM, VMEM],
        out_specs=pl.BlockSpec(memory_space=pl.ANY),
        scratch_shapes=[
            pltpu.VMEM((n_lists, block, width), bf16),
            pltpu.SemaphoreType.DMA((-(-n_lists // step),)),
        ],
        compiler_params=PARAMS,
    )(base_arg, gathered, items)
    fetched = exchange(answers)

    fetched, known, keys, values, turned = lax.optimization_barrier((fetched, known, keys, values, turned))

    sent = []
    if n_users > 1:
        sent = pl.pallas_call(
            functools.partial(place_kernel, n_users),
            out_shape=tuple(jax.ShapeDtypeStruct((share, width), bf16) for _ in range(n_users - 1)),
            in_specs=[SMEM, VMEM, VMEM],
            out_specs=tuple(VMEM for _ in range(n_users - 1)),
            scratch_shapes=[pltpu.VMEM((cands, 8), jnp.float32)],
            compiler_params=PARAMS,
        )(col_arg, known, fetched)
    parts = []
    for shift in range(1, n_users):
        parts.append(
            lax.ppermute(sent[shift - 1], "users", [(i, (i + shift) % n_users) for i in range(n_users)])
        )

    list_scores, own = pl.pallas_call(
        functools.partial(expand_kernel, user_dev, pieces, cap),
        out_shape=(
            jax.ShapeDtypeStruct((user_dev * probes, items_loc), bf16),
            jax.ShapeDtypeStruct((share, width), bf16),
        ),
        in_specs=[SMEM, VMEM, VMEM],
        out_specs=(pl.BlockSpec(memory_space=pl.ANY), VMEM),
        scratch_shapes=[
            pltpu.VMEM((user_dev * probes, items_loc), bf16),
            pltpu.VMEM((cands, 8), jnp.float32),
            pltpu.SemaphoreType.DMA((pieces,)),
        ],
        compiler_params=PARAMS,
    )(col_arg, known, fetched)
    ranked = pl.pallas_call(
        functools.partial(attend_kernel, n_users),
        out_shape=jax.ShapeDtypeStruct((share, width), bf16),
        in_specs=[VMEM] * (n_users + 4),
        out_specs=VMEM,
        compiler_params=PARAMS,
    )(own, *parts, keys, values, turned, out_weight)
    return (list_scores.reshape(user_dev, probes, items_loc), ranked.reshape(1, share, width))


def solution(mesh):
    placed = (
        P("lists", None),
        P("lists", None),
        P("lists", "users", None),
        P("lists", None),
        P("lists", "users", None),
        P("lists"),
        P(),
        P(),
        P(),
    )
    return jax.shard_map(
        shards,
        mesh=mesh,
        in_specs=placed,
        out_specs=(P("lists", None, "users"), P("lists", "users", None)),
        check_vma=False,
    )
```

```python
import functools

import jax
import jax.numpy as jnp
from jax import lax
from jax.experimental import pallas as pl
from jax.experimental.pallas import tpu as pltpu
from jax.sharding import PartitionSpec as P

HEADS = 8
BASE = 256
LANES = 128
ROW_TILE = 16
VMEM_BYTES = 28 * 1024 * 1024
ALL_VMEM_BYTES = 62 * 1024 * 1024


def round_up(value, step):
    return (value + step - 1) // step * step


def picks(index, count):
    place = lax.broadcasted_iota(jnp.int32, (index.shape[0], count), 1).astype(jnp.int16)
    one, zero = jnp.bfloat16(1.0), jnp.bfloat16(0.0)
    return jnp.where(index.astype(jnp.int16) == place, one, zero)


def pack_kernel(digits, ids_ref, vectors_ref, pack_ref):
    width = vectors_ref.shape[1]
    vectors = vectors_ref[...].astype(jnp.float32)
    ids = ids_ref[...]
    spans = [slice(start, start + LANES) for start in range(0, width, LANES)]
    rows = [vectors[:, span] for span in spans]
    for digit in range(digits):
        value = ((ids >> (8 * digit)) & (BASE - 1)).astype(jnp.float32)
        rows += [value[:, span] for span in spans]
    count = sum(row.shape[0] for row in rows)
    if pack_ref.shape[1] > count:
        rows.append(jnp.zeros((pack_ref.shape[1] - count, LANES), jnp.float32))
    pack_ref[...] = jnp.broadcast_to(jnp.concatenate(rows, axis=0).astype(jnp.bfloat16)[None], pack_ref.shape)


def earlier(count):
    row = lax.broadcasted_iota(jnp.int32, (count, count), 0)
    column = lax.broadcasted_iota(jnp.int32, (count, count), 1)
    return jnp.where(row < column, 1.0, 0.0).astype(jnp.bfloat16)


def unpack(wide, n_lists, user_dev, digits, spans):
    pack_rows = wide.shape[0] // n_lists

    def line(number):
        return wide[pl.ds(number, n_lists, stride=pack_rows), :]

    vectors = jnp.concatenate(
        [
            jnp.concatenate([line(span * user_dev + u) for span in range(spans)], axis=1)
            for u in range(user_dev)
        ],
        axis=0,
    )
    ids = []
    for span in range(spans):
        value = line(user_dev * spans + span)
        for digit in range(1, digits):
            value = value + line((user_dev + digit) * spans + span) * float(BASE**digit)
        ids.append(value)
    return vectors, ids


def asked(ids, base, items_loc, count):
    n_lists = ids[0].shape[0]
    local = jnp.concatenate([part - base for part in ids], axis=0)
    mine = (local >= 0.0) & (local < items_loc)
    hot = jnp.where(mine, 1.0, 0.0)
    rank = jnp.dot(hot.astype(jnp.bfloat16), earlier(LANES), preferred_element_type=jnp.float32)
    totals = jnp.sum(hot, axis=1, keepdims=True)
    before = jnp.zeros((n_lists, 1), jnp.float32)
    ranks, locals_ = [], []
    for span in range(len(ids)):
        rows = slice(span * n_lists, (span + 1) * n_lists)
        ranks.append(jnp.where(mine[rows], rank[rows] + before, -1.0))
        locals_.append(local[rows] + 1.0)
        before = before + totals[rows]
    rank, local = jnp.concatenate(ranks, axis=1), jnp.concatenate(locals_, axis=1)
    place = lax.broadcasted_iota(jnp.int32, (count, rank.shape[1]), 0).astype(jnp.float32)
    index = []
    for r in range(n_lists):
        picked = jnp.where(rank[r : r + 1] == place, local[r : r + 1], 0.0)
        index.append(jnp.sum(picked, axis=1, keepdims=True).astype(jnp.int32) - 1)
    return index


def items_kernel(items_hbm, items_ref, sems):
    part = items_ref.shape[0] // sems.shape[0]
    loads = []
    for p in range(sems.shape[0]):
        span = pl.ds(p * part, part)
        loads.append(pltpu.make_async_copy(items_hbm.at[span], items_ref.at[span], sems.at[p]))
        loads[-1].start()
    for load in loads:
        load.wait()


def known_kernel(n_lists, items_loc, n_users, block, col_ref, ids_ref, probes_ref, known_ref):
    ids = ids_ref[...]
    cands = ids.shape[1]
    bins = ids // items_loc
    mine = bins % n_users == col_ref[0]
    owner = bins // n_users
    lists = lax.broadcasted_iota(jnp.int32, (n_lists, cands), 0)
    hot = jnp.where((lists == owner) & mine, 1.0, 0.0)
    before = jnp.dot(hot.astype(jnp.bfloat16), earlier(cands), preferred_element_type=jnp.float32)
    rank = jnp.sum(before * hot, axis=0, keepdims=True)
    slot = jnp.where(mine, owner.astype(jnp.float32) * block + rank, -1.0)
    probes = probes_ref[...].astype(jnp.float32)
    flat = jnp.concatenate([probes[u : u + 1] for u in range(probes.shape[0])], axis=1)
    if flat.shape[1] < cands:
        flat = jnp.concatenate([flat, jnp.zeros((1, cands - flat.shape[1]), jnp.float32)], axis=1)
    row = lax.broadcasted_iota(jnp.int32, known_ref.shape, 0)
    known_ref[...] = jnp.where(row == 0, slot, flat)


def pairs_kernel(n_parts, col_ref, length_ref, *refs):
    parts, (weight_ref, query_ref, keys_ref, values_ref, turned_ref) = refs[:n_parts], refs[n_parts:]
    history = jnp.concatenate([part[...] for part in parts], axis=0)
    pairs = jnp.dot(history, weight_ref[...], preferred_element_type=jnp.float32)
    heads, events, features = keys_ref.shape
    head_dim = features - ROW_TILE
    width = heads * head_dim
    hist_dev = events // n_parts
    event = lax.broadcasted_iota(jnp.int32, (events, ROW_TILE), 0)
    feature = lax.broadcasted_iota(jnp.int32, (events, ROW_TILE), 1)
    position = (col_ref[0] - event // hist_dev + n_parts) % n_parts * hist_dev + event % hist_dev
    mask = jnp.where((position >= length_ref[0]) & (feature == 0), -1e30, 0.0)
    for h in range(heads):
        keys = pairs[:, h * head_dim : (h + 1) * head_dim]
        keys_ref[h] = jnp.concatenate([keys, mask], axis=1).astype(jnp.bfloat16)
    values_ref[...] = jnp.transpose(pairs[:, width:]).astype(jnp.bfloat16)
    turned_ref[...] = jnp.transpose(query_ref[...].astype(jnp.float32)).astype(jnp.bfloat16)


def owner_kernel(n_lists, user_dev, digits, cap, scale, base_ref, gathered_ref, items_ref, *refs):
    out_hbm, wide, out_ref, out_sems = refs
    items_loc, width = items_ref.shape
    wide[...] = gathered_ref[...].astype(jnp.float32)
    vectors, ids = unpack(wide, n_lists, user_dev, digits, width // LANES)
    index = asked(ids, base_ref[0].astype(jnp.float32), items_loc, cap)
    scores = lax.dot_general(
        vectors.astype(jnp.bfloat16),
        items_ref[...],
        (((1,), (1,)), ((), ())),
        preferred_element_type=jnp.float32,
    )
    scores = (scores * scale).astype(jnp.bfloat16)
    pieces = items_loc // width
    stacked = jnp.concatenate(
        [scores[:, piece * width : (piece + 1) * width] for piece in range(pieces)], axis=0
    )
    kept = out_ref.shape[1] - cap
    entry = lax.broadcasted_iota(jnp.int32, (n_lists * kept, 1), 0)
    wanted = jnp.where(entry % kept < pieces * user_dev, entry % kept * n_lists + entry // kept, -1)
    spread = jnp.dot(
        picks(wanted, stacked.shape[0]), stacked, preferred_element_type=jnp.float32
    ).astype(jnp.bfloat16)
    out_ref[:, cap:, :] = spread.reshape(n_lists, kept, width)
    step = max(1, 288 // cap)
    sends = []
    for number, first in enumerate(range(0, n_lists, step)):
        last = min(n_lists, first + step)
        rows = jnp.dot(
            picks(jnp.concatenate(index[first:last], axis=0), items_loc),
            items_ref[...],
            preferred_element_type=jnp.float32,
        ).astype(jnp.bfloat16)
        out_ref[first:last, :cap, :] = rows.reshape(last - first, cap, width)
        send = pltpu.make_async_copy(out_ref.at[first:last], out_hbm.at[first:last], out_sems.at[number])
        send.start()
        sends.append(send)
    for send in sends:
        send.wait()


def placed(column, known_ref, slots, fetched_ref, out_ref):
    n_lists, block, width = fetched_ref.shape
    share = out_ref.shape[0]
    slots[...] = jnp.transpose(known_ref[...])
    start = pl.multiple_of(column * share, share)
    slot = slots[pl.ds(start, share), :][:, :1].astype(jnp.int32)
    out_ref[...] = jnp.dot(
        picks(slot, n_lists * block),
        fetched_ref[...].reshape(n_lists * block, width),
        preferred_element_type=jnp.float32,
    ).astype(jnp.bfloat16)


def place_kernel(n_users, col_ref, known_ref, fetched_ref, *refs):
    sent_refs, slots = refs[:-1], refs[-1]
    for shift, ref in enumerate(sent_refs):
        placed((col_ref[0] + shift + 1) % n_users, known_ref, slots, fetched_ref, ref)


def attend_kernel(n_parts, *refs):
    parts, (keys_ref, values_ref, turned_ref, out_weight_ref, out_ref) = refs[:n_parts], refs[n_parts:]
    heads, events, features = keys_ref.shape
    head_dim = features - ROW_TILE
    rows = parts[0][...]
    for part in parts[1:]:
        rows = rows + part[...]
    queries = lax.dot_general(
        turned_ref[...], rows, (((1,), (1,)), ((), ())), preferred_element_type=jnp.float32
    )
    queries = (queries * head_dim ** (-0.5)).astype(jnp.bfloat16)
    feature = lax.broadcasted_iota(jnp.int32, (ROW_TILE, rows.shape[0]), 0)
    one = jnp.where(feature == 0, 1.0, 0.0).astype(jnp.bfloat16)

    def score(h):
        query = jnp.concatenate([queries[h * head_dim : (h + 1) * head_dim], one], axis=0)
        return jnp.dot(keys_ref[h], query, preferred_element_type=jnp.float32)

    ahead = [score(h) for h in range(min(2, heads))]
    mixed = []
    for h in range(heads):
        if h + 2 < heads:
            ahead.append(score(h + 2))
        exponentials = jnp.exp(ahead[h] - jnp.max(ahead[h], axis=0, keepdims=True))
        total = jnp.sum(exponentials, axis=0, keepdims=True)
        span = slice(h * head_dim, (h + 1) * head_dim)
        head = jnp.dot(values_ref[span, :], exponentials.astype(jnp.bfloat16), preferred_element_type=jnp.float32)
        mixed.append(head / total)
    attended = jnp.transpose(jnp.concatenate(mixed, axis=0)).astype(jnp.bfloat16)
    out_ref[...] = jnp.dot(attended, out_weight_ref[...], preferred_element_type=jnp.float32).astype(jnp.bfloat16)


def expand_kernel(user_dev, pieces, cap, col_ref, known_ref, fetched_ref, out_hbm, own_ref, out_ref, slots, sems):
    n_lists, block, width = fetched_ref.shape
    kept = block - cap
    rows = n_lists * kept
    returned = fetched_ref[:, cap:, :].reshape(rows, width)
    count = out_ref.shape[0]
    probe = jnp.transpose(known_ref[:, :count])[:, 1:2].astype(jnp.int32)
    user = lax.broadcasted_iota(jnp.int32, (count, 1), 0) // (count // user_dev)
    sends = []
    for piece in range(pieces):
        wanted = probe * kept + piece * user_dev + user
        span = pl.ds(piece * width, width)
        out_ref[:, span] = jnp.dot(picks(wanted, rows), returned, preferred_element_type=jnp.float32).astype(
            jnp.bfloat16
        )
        sends.append(pltpu.make_async_copy(out_ref.at[:, span], out_hbm.at[:, span], sems.at[piece]))
        sends[-1].start()
    placed(col_ref[0], known_ref, slots, fetched_ref, own_ref)
    for send in sends:
        send.wait()


SMEM = pl.BlockSpec(memory_space=pltpu.SMEM)
VMEM = pl.BlockSpec(memory_space=pltpu.VMEM)
HBM = pl.BlockSpec(memory_space=pltpu.HBM)
PARAMS = pltpu.CompilerParams(vmem_limit_bytes=VMEM_BYTES)


def exchange(value):
    return lax.all_to_all(value, "lists", split_axis=0, concat_axis=0, tiled=True)


def shards(
    user_vectors,
    probe_lists,
    list_items,
    candidate_ids,
    history,
    history_lengths,
    query_weight,
    key_value_weight,
    out_weight,
):
    n_lists = lax.axis_size("lists")
    n_users = lax.axis_size("users")
    _, items_loc, width = list_items.shape
    user_dev, probes = probe_lists.shape
    _, cands = candidate_ids.shape
    bf16 = jnp.bfloat16
    cap = max(2, 3 * cands // (n_lists * n_users))
    cap = round_up(cap, ROW_TILE)
    kept = round_up(items_loc // width * user_dev, ROW_TILE)
    share = cands // n_users
    pieces = items_loc // width
    digits = 1
    while BASE**digits < n_lists * n_users * items_loc:
        digits += 1
    pack_rows = round_up((user_dev + digits) * (width // LANES), 8)
    line = lax.axis_index("lists").astype(jnp.int32)
    col = lax.axis_index("users").astype(jnp.int32)
    col_arg = col.reshape(1)
    base_arg = ((line * n_users + col) * items_loc).reshape(1)
    block = cap + kept

    flat_items = list_items.reshape(items_loc, width)
    pack = pl.pallas_call(
        functools.partial(pack_kernel, digits),
        out_shape=jax.ShapeDtypeStruct((n_lists, pack_rows, LANES), bf16),
        in_specs=[VMEM, VMEM],
        out_specs=VMEM,
        compiler_params=pltpu.CompilerParams(vmem_limit_bytes=ALL_VMEM_BYTES),
    )(candidate_ids, user_vectors)
    gathered = exchange(pack)
    gathered = gathered.reshape(n_lists * pack_rows, LANES)

    items = pl.pallas_call(
        items_kernel,
        out_shape=jax.ShapeDtypeStruct((items_loc, width), bf16),
        in_specs=[HBM],
        out_specs=VMEM,
        scratch_shapes=[pltpu.SemaphoreType.DMA((4,))],
        compiler_params=PARAMS,
    )(flat_items)
    gathered, items = lax.optimization_barrier((gathered, items))

    known = pl.pallas_call(
        functools.partial(known_kernel, n_lists, items_loc, n_users, block),
        out_shape=jax.ShapeDtypeStruct((8, cands), jnp.float32),
        in_specs=[SMEM, VMEM, VMEM],
        out_specs=VMEM,
        compiler_params=PARAMS,
    )(col_arg, candidate_ids, probe_lists)

    events = history.reshape(-1, width)
    hist = [events]
    for shift in range(1, n_users):
        hist.append(lax.ppermute(events, "users", [(i, (i + shift) % n_users) for i in range(n_users)]))
    total_events = n_users * events.shape[0]
    keys, values, turned = pl.pallas_call(
        functools.partial(pairs_kernel, n_users),
        out_shape=(
            jax.ShapeDtypeStruct((HEADS, total_events, width // HEADS + ROW_TILE), bf16),
            jax.ShapeDtypeStruct((width, total_events), bf16),
            jax.ShapeDtypeStruct((width, width), bf16),
        ),
        in_specs=[SMEM, SMEM] + [VMEM] * (n_users + 2),
        out_specs=(VMEM, VMEM, VMEM),
        compiler_params=PARAMS,
    )(col_arg, history_lengths, *hist, key_value_weight, query_weight)

    step = max(1, 288 // cap)
    answers = pl.pallas_call(
        functools.partial(owner_kernel, n_lists, user_dev, digits, cap, width ** (-0.5)),
        out_shape=jax.ShapeDtypeStruct((n_lists, block, width), bf16),
        in_specs=[SMEM, VMEM, VMEM],
        out_specs=pl.BlockSpec(memory_space=pl.ANY),
        scratch_shapes=[
            pltpu.VMEM((n_lists * pack_rows, LANES), jnp.float32),
            pltpu.VMEM((n_lists, block, width), bf16),
            pltpu.SemaphoreType.DMA((-(-n_lists // step),)),
        ],
        compiler_params=PARAMS,
    )(base_arg, gathered, items)
    fetched = exchange(answers)

    fetched, known, keys, values, turned = lax.optimization_barrier((fetched, known, keys, values, turned))

    sent = []
    if n_users > 1:
        sent = pl.pallas_call(
            functools.partial(place_kernel, n_users),
            out_shape=tuple(jax.ShapeDtypeStruct((share, width), bf16) for _ in range(n_users - 1)),
            in_specs=[SMEM, VMEM, VMEM],
            out_specs=tuple(VMEM for _ in range(n_users - 1)),
            scratch_shapes=[pltpu.VMEM((cands, 8), jnp.float32)],
            compiler_params=PARAMS,
        )(col_arg, known, fetched)
    parts = []
    for shift in range(1, n_users):
        parts.append(
            lax.ppermute(sent[shift - 1], "users", [(i, (i + shift) % n_users) for i in range(n_users)])
        )

    list_scores, own = pl.pallas_call(
        functools.partial(expand_kernel, user_dev, pieces, cap),
        out_shape=(
            jax.ShapeDtypeStruct((user_dev * probes, items_loc), bf16),
            jax.ShapeDtypeStruct((share, width), bf16),
        ),
        in_specs=[SMEM, VMEM, VMEM],
        out_specs=(pl.BlockSpec(memory_space=pl.ANY), VMEM),
        scratch_shapes=[
            pltpu.VMEM((user_dev * probes, items_loc), bf16),
            pltpu.VMEM((cands, 8), jnp.float32),
            pltpu.SemaphoreType.DMA((pieces,)),
        ],
        compiler_params=PARAMS,
    )(col_arg, known, fetched)
    ranked = pl.pallas_call(
        functools.partial(attend_kernel, n_users),
        out_shape=jax.ShapeDtypeStruct((share, width), bf16),
        in_specs=[VMEM] * (n_users + 4),
        out_specs=VMEM,
        compiler_params=PARAMS,
    )(own, *parts, keys, values, turned, out_weight)
    return (list_scores.reshape(user_dev, probes, items_loc), ranked.reshape(1, share, width))


def solution(mesh):
    placed = (
        P("lists", None),
        P("lists", None),
        P("lists", "users", None),
        P("lists", None),
        P("lists", "users", None),
        P("lists"),
        P(),
        P(),
        P(),
    )
    return jax.shard_map(
        shards,
        mesh=mesh,
        in_specs=placed,
        out_specs=(P("lists", None, "users"), P("lists", "users", None)),
        check_vma=False,
    )
```

```python
import functools

import jax
import jax.numpy as jnp
from jax import lax
from jax.experimental import pallas as pl
from jax.experimental.pallas import tpu as pltpu
from jax.sharding import PartitionSpec as P

HEADS = 8
BASE = 256
LANES = 128
ROW_TILE = 16
VMEM_BYTES = 28 * 1024 * 1024
ALL_VMEM_BYTES = 62 * 1024 * 1024


def round_up(value, step):
    return (value + step - 1) // step * step


def picks(index, count):
    place = lax.broadcasted_iota(jnp.int32, (index.shape[0], count), 1).astype(jnp.int16)
    one, zero = jnp.bfloat16(1.0), jnp.bfloat16(0.0)
    return jnp.where(index.astype(jnp.int16) == place, one, zero)


def pack_kernel(digits, ids_ref, vectors_ref, pack_ref):
    width = vectors_ref.shape[1]
    vectors = vectors_ref[...].astype(jnp.float32)
    ids = ids_ref[...]
    spans = [slice(start, start + LANES) for start in range(0, width, LANES)]
    rows = [vectors[:, span] for span in spans]
    for digit in range(digits):
        value = ((ids >> (8 * digit)) & (BASE - 1)).astype(jnp.float32)
        rows += [value[:, span] for span in spans]
    count = sum(row.shape[0] for row in rows)
    if pack_ref.shape[1] > count:
        rows.append(jnp.zeros((pack_ref.shape[1] - count, LANES), jnp.float32))
    pack_ref[...] = jnp.broadcast_to(jnp.concatenate(rows, axis=0).astype(jnp.bfloat16)[None], pack_ref.shape)


def earlier(count):
    row = lax.broadcasted_iota(jnp.int32, (count, count), 0)
    column = lax.broadcasted_iota(jnp.int32, (count, count), 1)
    return jnp.where(row < column, 1.0, 0.0).astype(jnp.bfloat16)


def unpack(wide, n_lists, user_dev, digits, spans):
    pack_rows = wide.shape[0] // n_lists

    def line(number):
        return wide[pl.ds(number, n_lists, stride=pack_rows), :]

    vectors = jnp.concatenate(
        [
            jnp.concatenate([line(span * user_dev + u) for span in range(spans)], axis=1)
            for u in range(user_dev)
        ],
        axis=0,
    )
    ids = []
    for span in range(spans):
        value = line(user_dev * spans + span)
        for digit in range(1, digits):
            value = value + line((user_dev + digit) * spans + span) * float(BASE**digit)
        ids.append(value)
    return vectors, ids


def asked(ids, base, items_loc, count):
    n_lists = ids[0].shape[0]
    local = jnp.concatenate([part - base for part in ids], axis=0)
    mine = (local >= 0.0) & (local < items_loc)
    hot = jnp.where(mine, 1.0, 0.0)
    rank = jnp.dot(hot.astype(jnp.bfloat16), earlier(LANES), preferred_element_type=jnp.float32)
    totals = jnp.sum(hot, axis=1, keepdims=True)
    before = jnp.zeros((n_lists, 1), jnp.float32)
    ranks, locals_ = [], []
    for span in range(len(ids)):
        rows = slice(span * n_lists, (span + 1) * n_lists)
        ranks.append(jnp.where(mine[rows], rank[rows] + before, -1.0))
        locals_.append(local[rows] + 1.0)
        before = before + totals[rows]
    rank, local = jnp.concatenate(ranks, axis=1), jnp.concatenate(locals_, axis=1)
    place = lax.broadcasted_iota(jnp.int32, (count, rank.shape[1]), 0).astype(jnp.float32)
    index = []
    for r in range(n_lists):
        picked = jnp.where(rank[r : r + 1] == place, local[r : r + 1], 0.0)
        index.append(jnp.sum(picked, axis=1, keepdims=True).astype(jnp.int32) - 1)
    return index


def position(index, count):
    if count % 4:
        return index
    quarter = count // 4
    return index // (2 * quarter) * (2 * quarter) + index % quarter * 2 + index // quarter % 2


def items_kernel(items_hbm, items_ref, sems):
    part = items_ref.shape[0] // sems.shape[0]
    loads = []
    for p in range(sems.shape[0]):
        span = pl.ds(p * part, part)
        loads.append(pltpu.make_async_copy(items_hbm.at[span], items_ref.at[span], sems.at[p]))
        loads[-1].start()
    for load in loads:
        load.wait()


def known_kernel(n_lists, items_loc, n_users, block, col_ref, ids_ref, probes_ref, known_ref):
    ids = ids_ref[...]
    cands = ids.shape[1]
    bins = ids // items_loc
    mine = bins % n_users == col_ref[0]
    owner = bins // n_users
    lists = lax.broadcasted_iota(jnp.int32, (n_lists, cands), 0)
    hot = jnp.where((lists == owner) & mine, 1.0, 0.0)
    before = jnp.dot(hot.astype(jnp.bfloat16), earlier(cands), preferred_element_type=jnp.float32)
    rank = jnp.sum(before * hot, axis=0, keepdims=True)
    slot = jnp.where(mine, position(owner, n_lists).astype(jnp.float32) * block + rank, -1.0)
    probes = position(probes_ref[...], n_lists).astype(jnp.float32)
    flat = jnp.concatenate([probes[u : u + 1] for u in range(probes.shape[0])], axis=1)
    if flat.shape[1] < cands:
        flat = jnp.concatenate([flat, jnp.zeros((1, cands - flat.shape[1]), jnp.float32)], axis=1)
    row = lax.broadcasted_iota(jnp.int32, known_ref.shape, 0)
    known_ref[...] = jnp.where(row == 0, slot, flat)


def pairs_kernel(n_parts, col_ref, length_ref, *refs):
    parts, (weight_ref, query_ref, keys_ref, values_ref, turned_ref) = refs[:n_parts], refs[n_parts:]
    history = jnp.concatenate([part[...] for part in parts], axis=0)
    pairs = jnp.dot(history, weight_ref[...], preferred_element_type=jnp.float32)
    heads, events, features = keys_ref.shape
    head_dim = features - ROW_TILE
    width = heads * head_dim
    hist_dev = events // n_parts
    event = lax.broadcasted_iota(jnp.int32, (events, ROW_TILE), 0)
    feature = lax.broadcasted_iota(jnp.int32, (events, ROW_TILE), 1)
    position = (col_ref[0] - event // hist_dev + n_parts) % n_parts * hist_dev + event % hist_dev
    mask = jnp.where((position >= length_ref[0]) & (feature == 0), -1e30, 0.0)
    for h in range(heads):
        keys = pairs[:, h * head_dim : (h + 1) * head_dim]
        keys_ref[h] = jnp.concatenate([keys, mask], axis=1).astype(jnp.bfloat16)
    values_ref[...] = jnp.transpose(pairs[:, width:]).astype(jnp.bfloat16)
    turned_ref[...] = jnp.transpose(query_ref[...].astype(jnp.float32)).astype(jnp.bfloat16)


def owner_kernel(n_lists, user_dev, digits, cap, scale, base_ref, gathered_ref, items_ref, *refs):
    out_hbm, wide, out_ref, out_sems = refs
    items_loc, width = items_ref.shape
    wide[...] = gathered_ref[...].astype(jnp.float32)
    vectors, ids = unpack(wide, n_lists, user_dev, digits, width // LANES)
    index = asked(ids, base_ref[0].astype(jnp.float32), items_loc, cap)
    scores = lax.dot_general(
        vectors.astype(jnp.bfloat16),
        items_ref[...],
        (((1,), (1,)), ((), ())),
        preferred_element_type=jnp.float32,
    )
    scores = (scores * scale).astype(jnp.bfloat16)
    pieces = items_loc // width
    stacked = jnp.concatenate(
        [scores[:, piece * width : (piece + 1) * width] for piece in range(pieces)], axis=0
    )
    kept = out_ref.shape[1] - cap
    entry = lax.broadcasted_iota(jnp.int32, (n_lists * kept, 1), 0)
    wanted = jnp.where(entry % kept < pieces * user_dev, entry % kept * n_lists + entry // kept, -1)
    spread = jnp.dot(
        picks(wanted, stacked.shape[0]), stacked, preferred_element_type=jnp.float32
    ).astype(jnp.bfloat16)
    out_ref[:, cap:, :] = spread.reshape(n_lists, kept, width)
    step = max(1, 288 // cap)
    sends = []
    for number, first in enumerate(range(0, n_lists, step)):
        last = min(n_lists, first + step)
        rows = jnp.dot(
            picks(jnp.concatenate(index[first:last], axis=0), items_loc),
            items_ref[...],
            preferred_element_type=jnp.float32,
        ).astype(jnp.bfloat16)
        out_ref[first:last, :cap, :] = rows.reshape(last - first, cap, width)
        send = pltpu.make_async_copy(out_ref.at[first:last], out_hbm.at[first:last], out_sems.at[number])
        send.start()
        sends.append(send)
    for send in sends:
        send.wait()


def placed(column, known_ref, slots, fetched_ref, out_ref):
    n_lists, block, width = fetched_ref.shape
    share = out_ref.shape[0]
    slots[...] = jnp.transpose(known_ref[...])
    start = pl.multiple_of(column * share, share)
    slot = slots[pl.ds(start, share), :][:, :1].astype(jnp.int32)
    out_ref[...] = jnp.dot(
        picks(slot, n_lists * block),
        fetched_ref[...].reshape(n_lists * block, width),
        preferred_element_type=jnp.float32,
    ).astype(jnp.bfloat16)


def place_kernel(n_users, col_ref, known_ref, fetched_ref, *refs):
    sent_refs, slots = refs[:-1], refs[-1]
    for shift, ref in enumerate(sent_refs):
        placed((col_ref[0] + shift + 1) % n_users, known_ref, slots, fetched_ref, ref)


def attend_kernel(n_parts, *refs):
    parts, (keys_ref, values_ref, turned_ref, out_weight_ref, out_ref) = refs[:n_parts], refs[n_parts:]
    heads, events, features = keys_ref.shape
    head_dim = features - ROW_TILE
    rows = parts[0][...]
    for part in parts[1:]:
        rows = rows + part[...]
    queries = lax.dot_general(
        turned_ref[...], rows, (((1,), (1,)), ((), ())), preferred_element_type=jnp.float32
    )
    queries = (queries * head_dim ** (-0.5)).astype(jnp.bfloat16)
    feature = lax.broadcasted_iota(jnp.int32, (ROW_TILE, rows.shape[0]), 0)
    one = jnp.where(feature == 0, 1.0, 0.0).astype(jnp.bfloat16)

    def score(h):
        query = jnp.concatenate([queries[h * head_dim : (h + 1) * head_dim], one], axis=0)
        return jnp.dot(keys_ref[h], query, preferred_element_type=jnp.float32)

    ahead = [score(h) for h in range(min(2, heads))]
    mixed = []
    for h in range(heads):
        if h + 2 < heads:
            ahead.append(score(h + 2))
        exponentials = jnp.exp(ahead[h] - jnp.max(ahead[h], axis=0, keepdims=True))
        total = jnp.sum(exponentials, axis=0, keepdims=True)
        span = slice(h * head_dim, (h + 1) * head_dim)
        head = jnp.dot(values_ref[span, :], exponentials.astype(jnp.bfloat16), preferred_element_type=jnp.float32)
        mixed.append(head / total)
    attended = jnp.transpose(jnp.concatenate(mixed, axis=0)).astype(jnp.bfloat16)
    out_ref[...] = jnp.dot(attended, out_weight_ref[...], preferred_element_type=jnp.float32).astype(jnp.bfloat16)


def expand_kernel(user_dev, pieces, cap, col_ref, known_ref, fetched_ref, out_hbm, own_ref, out_ref, slots, sems):
    n_lists, block, width = fetched_ref.shape
    kept = block - cap
    rows = n_lists * kept
    returned = fetched_ref[:, cap:, :].reshape(rows, width)
    count = out_ref.shape[0]
    probe = jnp.transpose(known_ref[:, :count])[:, 1:2].astype(jnp.int32)
    user = lax.broadcasted_iota(jnp.int32, (count, 1), 0) // (count // user_dev)
    sends = []
    for piece in range(pieces):
        wanted = probe * kept + piece * user_dev + user
        span = pl.ds(piece * width, width)
        out_ref[:, span] = jnp.dot(picks(wanted, rows), returned, preferred_element_type=jnp.float32).astype(
            jnp.bfloat16
        )
        sends.append(pltpu.make_async_copy(out_ref.at[:, span], out_hbm.at[:, span], sems.at[piece]))
        sends[-1].start()
    placed(col_ref[0], known_ref, slots, fetched_ref, own_ref)
    for send in sends:
        send.wait()


SMEM = pl.BlockSpec(memory_space=pltpu.SMEM)
VMEM = pl.BlockSpec(memory_space=pltpu.VMEM)
HBM = pl.BlockSpec(memory_space=pltpu.HBM)
PARAMS = pltpu.CompilerParams(vmem_limit_bytes=VMEM_BYTES)


def exchange(value):
    count = lax.axis_size("lists")
    group = sorted(range(count), key=lambda index: position(index, count))
    return lax.all_to_all(
        value, "lists", split_axis=0, concat_axis=0, axis_index_groups=[group], tiled=True
    )


def shards(
    user_vectors,
    probe_lists,
    list_items,
    candidate_ids,
    history,
    history_lengths,
    query_weight,
    key_value_weight,
    out_weight,
):
    n_lists = lax.axis_size("lists")
    n_users = lax.axis_size("users")
    _, items_loc, width = list_items.shape
    user_dev, probes = probe_lists.shape
    _, cands = candidate_ids.shape
    bf16 = jnp.bfloat16
    cap = max(2, 3 * cands // (n_lists * n_users))
    cap = round_up(cap, ROW_TILE)
    kept = round_up(items_loc // width * user_dev, ROW_TILE)
    share = cands // n_users
    pieces = items_loc // width
    digits = 1
    while BASE**digits < n_lists * n_users * items_loc:
        digits += 1
    pack_rows = round_up((user_dev + digits) * (width // LANES), 8)
    line = lax.axis_index("lists").astype(jnp.int32)
    col = lax.axis_index("users").astype(jnp.int32)
    col_arg = col.reshape(1)
    base_arg = ((line * n_users + col) * items_loc).reshape(1)
    block = cap + kept

    flat_items = list_items.reshape(items_loc, width)
    pack = pl.pallas_call(
        functools.partial(pack_kernel, digits),
        out_shape=jax.ShapeDtypeStruct((n_lists, pack_rows, LANES), bf16),
        in_specs=[VMEM, VMEM],
        out_specs=VMEM,
        compiler_params=pltpu.CompilerParams(vmem_limit_bytes=ALL_VMEM_BYTES),
    )(candidate_ids, user_vectors)
    gathered = exchange(pack)
    gathered = gathered.reshape(n_lists * pack_rows, LANES)

    items = pl.pallas_call(
        items_kernel,
        out_shape=jax.ShapeDtypeStruct((items_loc, width), bf16),
        in_specs=[HBM],
        out_specs=VMEM,
        scratch_shapes=[pltpu.SemaphoreType.DMA((4,))],
        compiler_params=PARAMS,
    )(flat_items)
    gathered, items = lax.optimization_barrier((gathered, items))

    known = pl.pallas_call(
        functools.partial(known_kernel, n_lists, items_loc, n_users, block),
        out_shape=jax.ShapeDtypeStruct((8, cands), jnp.float32),
        in_specs=[SMEM, VMEM, VMEM],
        out_specs=VMEM,
        compiler_params=PARAMS,
    )(col_arg, candidate_ids, probe_lists)

    events = history.reshape(-1, width)
    hist = [events]
    for shift in range(1, n_users):
        hist.append(lax.ppermute(events, "users", [(i, (i + shift) % n_users) for i in range(n_users)]))
    total_events = n_users * events.shape[0]
    keys, values, turned = pl.pallas_call(
        functools.partial(pairs_kernel, n_users),
        out_shape=(
            jax.ShapeDtypeStruct((HEADS, total_events, width // HEADS + ROW_TILE), bf16),
            jax.ShapeDtypeStruct((width, total_events), bf16),
            jax.ShapeDtypeStruct((width, width), bf16),
        ),
        in_specs=[SMEM, SMEM] + [VMEM] * (n_users + 2),
        out_specs=(VMEM, VMEM, VMEM),
        compiler_params=PARAMS,
    )(col_arg, history_lengths, *hist, key_value_weight, query_weight)

    step = max(1, 288 // cap)
    answers = pl.pallas_call(
        functools.partial(owner_kernel, n_lists, user_dev, digits, cap, width ** (-0.5)),
        out_shape=jax.ShapeDtypeStruct((n_lists, block, width), bf16),
        in_specs=[SMEM, VMEM, VMEM],
        out_specs=pl.BlockSpec(memory_space=pl.ANY),
        scratch_shapes=[
            pltpu.VMEM((n_lists * pack_rows, LANES), jnp.float32),
            pltpu.VMEM((n_lists, block, width), bf16),
            pltpu.SemaphoreType.DMA((-(-n_lists // step),)),
        ],
        compiler_params=PARAMS,
    )(base_arg, gathered, items)
    fetched = exchange(answers)

    fetched, known, keys, values, turned = lax.optimization_barrier((fetched, known, keys, values, turned))

    sent = []
    if n_users > 1:
        sent = pl.pallas_call(
            functools.partial(place_kernel, n_users),
            out_shape=tuple(jax.ShapeDtypeStruct((share, width), bf16) for _ in range(n_users - 1)),
            in_specs=[SMEM, VMEM, VMEM],
            out_specs=tuple(VMEM for _ in range(n_users - 1)),
            scratch_shapes=[pltpu.VMEM((cands, 8), jnp.float32)],
            compiler_params=PARAMS,
        )(col_arg, known, fetched)
    parts = []
    for shift in range(1, n_users):
        parts.append(
            lax.ppermute(sent[shift - 1], "users", [(i, (i + shift) % n_users) for i in range(n_users)])
        )

    list_scores, own = pl.pallas_call(
        functools.partial(expand_kernel, user_dev, pieces, cap),
        out_shape=(
            jax.ShapeDtypeStruct((user_dev * probes, items_loc), bf16),
            jax.ShapeDtypeStruct((share, width), bf16),
        ),
        in_specs=[SMEM, VMEM, VMEM],
        out_specs=(pl.BlockSpec(memory_space=pl.ANY), VMEM),
        scratch_shapes=[
            pltpu.VMEM((user_dev * probes, items_loc), bf16),
            pltpu.VMEM((cands, 8), jnp.float32),
            pltpu.SemaphoreType.DMA((pieces,)),
        ],
        compiler_params=PARAMS,
    )(col_arg, known, fetched)
    ranked = pl.pallas_call(
        functools.partial(attend_kernel, n_users),
        out_shape=jax.ShapeDtypeStruct((share, width), bf16),
        in_specs=[VMEM] * (n_users + 4),
        out_specs=VMEM,
        compiler_params=PARAMS,
    )(own, *parts, keys, values, turned, out_weight)
    return (list_scores.reshape(user_dev, probes, items_loc), ranked.reshape(1, share, width))


def solution(mesh):
    placed = (
        P("lists", None),
        P("lists", None),
        P("lists", "users", None),
        P("lists", None),
        P("lists", "users", None),
        P("lists"),
        P(),
        P(),
        P(),
    )
    return jax.shard_map(
        shards,
        mesh=mesh,
        in_specs=placed,
        out_specs=(P("lists", None, "users"), P("lists", "users", None)),
        check_vma=False,
    )
```

```python
import functools

import jax
import jax.numpy as jnp
from jax import lax
from jax.experimental import pallas as pl
from jax.experimental.pallas import tpu as pltpu
from jax.sharding import PartitionSpec as P

HEADS = 8
BASE = 256
LANES = 128
ROW_TILE = 16
VMEM_BYTES = 28 * 1024 * 1024
ALL_VMEM_BYTES = 62 * 1024 * 1024


def round_up(value, step):
    return (value + step - 1) // step * step


def picks(index, count):
    place = lax.broadcasted_iota(jnp.int32, (index.shape[0], count), 1).astype(jnp.int16)
    one, zero = jnp.bfloat16(1.0), jnp.bfloat16(0.0)
    return jnp.where(index.astype(jnp.int16) == place, one, zero)


def pack_kernel(digits, ids_ref, vectors_ref, pack_ref):
    width = vectors_ref.shape[1]
    vectors = vectors_ref[...].astype(jnp.float32)
    ids = ids_ref[...]
    spans = [slice(start, start + LANES) for start in range(0, width, LANES)]
    rows = [vectors[:, span] for span in spans]
    for digit in range(digits):
        value = ((ids >> (8 * digit)) & (BASE - 1)).astype(jnp.float32)
        rows += [value[:, span] for span in spans]
    count = sum(row.shape[0] for row in rows)
    if pack_ref.shape[1] > count:
        rows.append(jnp.zeros((pack_ref.shape[1] - count, LANES), jnp.float32))
    pack_ref[...] = jnp.broadcast_to(jnp.concatenate(rows, axis=0).astype(jnp.bfloat16)[None], pack_ref.shape)


def earlier(count):
    row = lax.broadcasted_iota(jnp.int32, (count, count), 0)
    column = lax.broadcasted_iota(jnp.int32, (count, count), 1)
    return jnp.where(row < column, 1.0, 0.0).astype(jnp.bfloat16)


def unpack(wide, n_lists, user_dev, digits, spans):
    pack_rows = wide.shape[0] // n_lists

    def line(number):
        return wide[pl.ds(number, n_lists, stride=pack_rows), :]

    vectors = jnp.concatenate(
        [
            jnp.concatenate([line(span * user_dev + u) for span in range(spans)], axis=1)
            for u in range(user_dev)
        ],
        axis=0,
    )
    ids = []
    for span in range(spans):
        value = line(user_dev * spans + span)
        for digit in range(1, digits):
            value = value + line((user_dev + digit) * spans + span) * float(BASE**digit)
        ids.append(value)
    return vectors, ids


def asked(ids, base, items_loc, first, count):
    n_lists = ids[0].shape[0]
    local = jnp.concatenate([part - base for part in ids], axis=0)
    mine = (local >= 0.0) & (local < items_loc)
    hot = jnp.where(mine, 1.0, 0.0)
    rank = jnp.dot(hot.astype(jnp.bfloat16), earlier(LANES), preferred_element_type=jnp.float32)
    totals = jnp.sum(hot, axis=1, keepdims=True)
    before = jnp.zeros((n_lists, 1), jnp.float32)
    ranks, locals_ = [], []
    for span in range(len(ids)):
        rows = slice(span * n_lists, (span + 1) * n_lists)
        ranks.append(jnp.where(mine[rows], rank[rows] + before, -1.0))
        locals_.append(local[rows] + 1.0)
        before = before + totals[rows]
    rank, local = jnp.concatenate(ranks, axis=1), jnp.concatenate(locals_, axis=1)
    place = (lax.broadcasted_iota(jnp.int32, (count, rank.shape[1]), 0) + first).astype(jnp.float32)
    index = []
    for r in range(n_lists):
        picked = jnp.where(rank[r : r + 1] == place, local[r : r + 1], 0.0)
        index.append(jnp.sum(picked, axis=1, keepdims=True).astype(jnp.int32) - 1)
    return index, before


def items_kernel(items_hbm, items_ref, sems):
    part = items_ref.shape[0] // sems.shape[0]
    loads = []
    for p in range(sems.shape[0]):
        span = pl.ds(p * part, part)
        loads.append(pltpu.make_async_copy(items_hbm.at[span], items_ref.at[span], sems.at[p]))
        loads[-1].start()
    for load in loads:
        load.wait()


def crowded(ids, n_lists, items_loc, main, spare):
    bins = [part.astype(jnp.int32) // items_loc for part in ids]
    worst = jnp.zeros((n_lists, 1), jnp.float32)
    for owner in range(n_lists):
        count = []
        for c in range(2):
            hits = [jnp.where(part == owner * 2 + c, 1.0, 0.0) for part in bins]
            count.append(jnp.sum(sum(hits[1:], hits[0]), axis=1, keepdims=True))
        for one, other in ((0, 1), (1, 0)):
            clash = (count[one] > float(main - spare)) & (count[other] > float(main))
            worst = jnp.maximum(worst, jnp.where(clash, 1.0, 0.0))
    return jnp.max(worst)


def known_kernel(
    n_lists, items_loc, n_users, user_dev, digits, main, spare, kept, *refs
):
    line_ref, col_ref, ids_ref, probes_ref, gathered_ref, known_ref, many_ref, wide = refs
    block = kept + main
    ids = ids_ref[...]
    cands = ids.shape[1]
    bins = ids // items_loc
    mine = bins % n_users == col_ref[0]
    owner = bins // n_users
    lists = lax.broadcasted_iota(jnp.int32, (n_lists * n_users, cands), 0)
    hot = jnp.where(lists == bins, 1.0, 0.0)
    before = jnp.dot(hot.astype(jnp.bfloat16), earlier(cands), preferred_element_type=jnp.float32)
    rank = jnp.sum(before * hot, axis=0, keepdims=True)
    slot = owner.astype(jnp.float32) * block + kept + rank
    if spare:
        wide[...] = gathered_ref[...].astype(jnp.float32)
        _, asked_ids = unpack(wide, n_lists, user_dev, digits, cands // LANES)
        many = crowded(asked_ids, n_lists, items_loc, main, spare)
        many_ref[0] = many.astype(jnp.int32)
        apart = n_lists * block + (owner ^ line_ref[0]).astype(jnp.float32) * spare + rank - main
        apart = jnp.where(many > 0.5, apart, -1.0)
        there = jnp.where((rank >= float(main)) & (many < 0.5), slot - spare, -1.0)
        slot = jnp.where(mine, jnp.where(rank < float(main), slot, apart), there)
    else:
        many_ref[0] = jnp.int32(0)
        slot = jnp.where(mine, slot, -1.0)
    probes = probes_ref[...].astype(jnp.float32)
    flat = jnp.concatenate([probes[u : u + 1] for u in range(probes.shape[0])], axis=1)
    if flat.shape[1] < cands:
        flat = jnp.concatenate([flat, jnp.zeros((1, cands - flat.shape[1]), jnp.float32)], axis=1)
    row = lax.broadcasted_iota(jnp.int32, known_ref.shape, 0)
    known_ref[...] = jnp.where(row == 0, slot, flat)


def pairs_kernel(n_parts, col_ref, length_ref, *refs):
    parts, (weight_ref, query_ref, keys_ref, values_ref, turned_ref) = refs[:n_parts], refs[n_parts:]
    history = jnp.concatenate([part[...] for part in parts], axis=0)
    pairs = jnp.dot(history, weight_ref[...], preferred_element_type=jnp.float32)
    heads, events, features = keys_ref.shape
    head_dim = features - ROW_TILE
    width = heads * head_dim
    hist_dev = events // n_parts
    event = lax.broadcasted_iota(jnp.int32, (events, ROW_TILE), 0)
    feature = lax.broadcasted_iota(jnp.int32, (events, ROW_TILE), 1)
    position = (col_ref[0] - event // hist_dev + n_parts) % n_parts * hist_dev + event % hist_dev
    mask = jnp.where((position >= length_ref[0]) & (feature == 0), -1e30, 0.0)
    for h in range(heads):
        keys = pairs[:, h * head_dim : (h + 1) * head_dim]
        keys_ref[h] = jnp.concatenate([keys, mask], axis=1).astype(jnp.bfloat16)
    values_ref[...] = jnp.transpose(pairs[:, width:]).astype(jnp.bfloat16)
    turned_ref[...] = jnp.transpose(query_ref[...].astype(jnp.float32)).astype(jnp.bfloat16)


def owner_kernel(
    n_lists, user_dev, digits, main, spare, scale, base_ref, other_ref, gathered_ref, items_ref, *refs
):
    sibling_ref = refs[0] if spare else None
    out_hbm, wide, out_ref, out_sems = refs[-4:]
    items_loc, width = items_ref.shape
    wide[...] = gathered_ref[...].astype(jnp.float32)
    vectors, ids = unpack(wide, n_lists, user_dev, digits, width // LANES)
    index, own = asked(ids, base_ref[0].astype(jnp.float32), items_loc, 0, main)
    scores = lax.dot_general(
        vectors.astype(jnp.bfloat16),
        items_ref[...],
        (((1,), (1,)), ((), ())),
        preferred_element_type=jnp.float32,
    )
    scores = (scores * scale).astype(jnp.bfloat16)
    pieces = items_loc // width
    stacked = jnp.concatenate(
        [scores[:, piece * width : (piece + 1) * width] for piece in range(pieces)], axis=0
    )
    kept = out_ref.shape[1] - main
    entry = lax.broadcasted_iota(jnp.int32, (n_lists * kept, 1), 0)
    wanted = jnp.where(entry % kept < pieces * user_dev, entry % kept * n_lists + entry // kept, -1)
    spread = jnp.dot(
        picks(wanted, stacked.shape[0]), stacked, preferred_element_type=jnp.float32
    ).astype(jnp.bfloat16)
    out_ref[:, :kept, :] = spread.reshape(n_lists, kept, width)
    if spare:
        over, _ = asked(ids, other_ref[0].astype(jnp.float32), items_loc, main, spare)
        over = [jnp.where(own[r : r + 1] > float(main - spare), -1, over[r]) for r in range(n_lists)]
        shared = jnp.dot(
            picks(jnp.concatenate(over, axis=0), items_loc), sibling_ref[...], preferred_element_type=jnp.float32
        )
    step = max(1, 288 // main)
    sends = []
    for number, first in enumerate(range(0, n_lists, step)):
        last = min(n_lists, first + step)
        rows = jnp.dot(
            picks(jnp.concatenate(index[first:last], axis=0), items_loc),
            items_ref[...],
            preferred_element_type=jnp.float32,
        )
        for r in range(first, last):
            mine = rows[(r - first) * main : (r - first + 1) * main]
            out_ref[r, kept : kept + main - spare, :] = mine[: main - spare].astype(jnp.bfloat16)
            if spare:
                both = mine[main - spare :] + shared[r * spare : (r + 1) * spare]
                out_ref[r, kept + main - spare :, :] = both.astype(jnp.bfloat16)
        send = pltpu.make_async_copy(out_ref.at[first:last], out_hbm.at[first:last], out_sems.at[number])
        send.start()
        sends.append(send)
    for send in sends:
        send.wait()


def spill_kernel(n_lists, user_dev, digits, main, base_ref, gathered_ref, items_ref, spill_ref, wide):
    items_loc, width = items_ref.shape
    spare = spill_ref.shape[1]
    wide[...] = gathered_ref[...].astype(jnp.float32)
    _, ids = unpack(wide, n_lists, user_dev, digits, width // LANES)
    index, _ = asked(ids, base_ref[0].astype(jnp.float32), items_loc, main, spare)
    rows = jnp.dot(
        picks(jnp.concatenate(index, axis=0), items_loc), items_ref[...], preferred_element_type=jnp.float32
    )
    spill_ref[...] = rows.astype(jnp.bfloat16).reshape(spill_ref.shape)


def stay_kernel(came_ref, here_ref):
    here_ref[...] = came_ref[...]


def placed(column, known_ref, slots, fetched_ref, extra_refs, out_ref):
    n_lists, block, width = fetched_ref.shape
    share = out_ref.shape[0]
    slots[...] = jnp.transpose(known_ref[...])
    start = pl.multiple_of(column * share, share)
    slot = slots[pl.ds(start, share), :][:, :1].astype(jnp.int32)
    rows = jnp.dot(
        picks(slot, n_lists * block),
        fetched_ref[...].reshape(n_lists * block, width),
        preferred_element_type=jnp.float32,
    )
    for ref in extra_refs:
        rows = rows + jnp.dot(
            picks(slot - n_lists * block, ref.shape[0]), ref[...], preferred_element_type=jnp.float32
        )
    out_ref[...] = rows.astype(jnp.bfloat16)


def place_kernel(n_users, col_ref, known_ref, fetched_ref, *refs):
    extra_refs, sent_refs, slots = refs[: -n_users], refs[-n_users:-1], refs[-1]
    for shift, ref in enumerate(sent_refs):
        placed((col_ref[0] + shift + 1) % n_users, known_ref, slots, fetched_ref, extra_refs, ref)


def attend_kernel(n_parts, *refs):
    parts, (keys_ref, values_ref, turned_ref, out_weight_ref, out_ref) = refs[:n_parts], refs[n_parts:]
    heads, events, features = keys_ref.shape
    head_dim = features - ROW_TILE
    rows = parts[0][...]
    for part in parts[1:]:
        rows = rows + part[...]
    queries = lax.dot_general(
        turned_ref[...], rows, (((1,), (1,)), ((), ())), preferred_element_type=jnp.float32
    )
    queries = (queries * head_dim ** (-0.5)).astype(jnp.bfloat16)
    feature = lax.broadcasted_iota(jnp.int32, (ROW_TILE, rows.shape[0]), 0)
    one = jnp.where(feature == 0, 1.0, 0.0).astype(jnp.bfloat16)

    def score(h):
        query = jnp.concatenate([queries[h * head_dim : (h + 1) * head_dim], one], axis=0)
        return jnp.dot(keys_ref[h], query, preferred_element_type=jnp.float32)

    ahead = [score(h) for h in range(min(2, heads))]
    mixed = []
    for h in range(heads):
        if h + 2 < heads:
            ahead.append(score(h + 2))
        exponentials = jnp.exp(ahead[h] - jnp.max(ahead[h], axis=0, keepdims=True))
        total = jnp.sum(exponentials, axis=0, keepdims=True)
        span = slice(h * head_dim, (h + 1) * head_dim)
        head = jnp.dot(values_ref[span, :], exponentials.astype(jnp.bfloat16), preferred_element_type=jnp.float32)
        mixed.append(head / total)
    attended = jnp.transpose(jnp.concatenate(mixed, axis=0)).astype(jnp.bfloat16)
    out_ref[...] = jnp.dot(attended, out_weight_ref[...], preferred_element_type=jnp.float32).astype(jnp.bfloat16)


def expand_kernel(user_dev, pieces, kept, col_ref, known_ref, fetched_ref, *refs):
    extra_refs, (out_hbm, own_ref, out_ref, slots, sems) = refs[:-5], refs[-5:]
    n_lists, _, width = fetched_ref.shape
    rows = n_lists * kept
    returned = fetched_ref[:, :kept, :].reshape(rows, width)
    count = out_ref.shape[0]
    probe = jnp.transpose(known_ref[:, :count])[:, 1:2].astype(jnp.int32)
    user = lax.broadcasted_iota(jnp.int32, (count, 1), 0) // (count // user_dev)
    sends = []
    for piece in range(pieces):
        wanted = probe * kept + piece * user_dev + user
        span = pl.ds(piece * width, width)
        out_ref[:, span] = jnp.dot(picks(wanted, rows), returned, preferred_element_type=jnp.float32).astype(
            jnp.bfloat16
        )
        sends.append(pltpu.make_async_copy(out_ref.at[:, span], out_hbm.at[:, span], sems.at[piece]))
        sends[-1].start()
    placed(col_ref[0], known_ref, slots, fetched_ref, extra_refs, own_ref)
    for send in sends:
        send.wait()


SMEM = pl.BlockSpec(memory_space=pltpu.SMEM)
VMEM = pl.BlockSpec(memory_space=pltpu.VMEM)
HBM = pl.BlockSpec(memory_space=pltpu.HBM)
PARAMS = pltpu.CompilerParams(vmem_limit_bytes=VMEM_BYTES)


def exchange(value):
    return lax.all_to_all(value, "lists", split_axis=0, concat_axis=0, tiled=True)


def shards(
    user_vectors,
    probe_lists,
    list_items,
    candidate_ids,
    history,
    history_lengths,
    query_weight,
    key_value_weight,
    out_weight,
):
    n_lists = lax.axis_size("lists")
    n_users = lax.axis_size("users")
    _, items_loc, width = list_items.shape
    user_dev, probes = probe_lists.shape
    _, cands = candidate_ids.shape
    bf16 = jnp.bfloat16
    cap = max(2, 3 * cands // (n_lists * n_users))
    cap = round_up(cap, ROW_TILE)
    kept = round_up(items_loc // width * user_dev, ROW_TILE)
    share = cands // n_users
    pieces = items_loc // width
    digits = 1
    while BASE**digits < n_lists * n_users * items_loc:
        digits += 1
    pack_rows = round_up((user_dev + digits) * (width // LANES), 8)
    line = lax.axis_index("lists").astype(jnp.int32)
    col = lax.axis_index("users").astype(jnp.int32)
    col_arg = col.reshape(1)
    line_arg = line.reshape(1)
    base_arg = ((line * n_users + col) * items_loc).reshape(1)
    other_arg = ((line * n_users + n_users - 1 - col) * items_loc).reshape(1)
    spare = 8 if n_users == 2 and cap >= 48 else 0
    main = cap - spare
    block = main + kept

    flat_items = list_items.reshape(items_loc, width)
    pack = pl.pallas_call(
        functools.partial(pack_kernel, digits),
        out_shape=jax.ShapeDtypeStruct((n_lists, pack_rows, LANES), bf16),
        in_specs=[VMEM, VMEM],
        out_specs=VMEM,
        compiler_params=pltpu.CompilerParams(vmem_limit_bytes=ALL_VMEM_BYTES),
    )(candidate_ids, user_vectors)
    gathered = exchange(pack)
    gathered = gathered.reshape(n_lists * pack_rows, LANES)

    items = pl.pallas_call(
        items_kernel,
        out_shape=jax.ShapeDtypeStruct((items_loc, width), bf16),
        in_specs=[HBM],
        out_specs=VMEM,
        scratch_shapes=[pltpu.SemaphoreType.DMA((4,))],
        compiler_params=PARAMS,
    )(flat_items)
    gathered, items = lax.optimization_barrier((gathered, items))

    siblings = []
    if spare:
        siblings.append(lax.ppermute(flat_items, "users", [(0, 1), (1, 0)]))

    known, many = pl.pallas_call(
        functools.partial(known_kernel, n_lists, items_loc, n_users, user_dev, digits, main, spare, kept),
        out_shape=(
            jax.ShapeDtypeStruct((8, cands), jnp.float32),
            jax.ShapeDtypeStruct((1,), jnp.int32),
        ),
        in_specs=[SMEM, SMEM, VMEM, VMEM, VMEM],
        out_specs=(VMEM, SMEM),
        scratch_shapes=[pltpu.VMEM((n_lists * pack_rows, LANES), jnp.float32)],
        compiler_params=PARAMS,
    )(line_arg, col_arg, candidate_ids, probe_lists, gathered)

    extras = []
    if spare:

        def spill_apart():
            spill = pl.pallas_call(
                functools.partial(spill_kernel, n_lists, user_dev, digits, main),
                out_shape=jax.ShapeDtypeStruct((n_lists, spare, width), bf16),
                in_specs=[SMEM, VMEM, VMEM],
                out_specs=VMEM,
                scratch_shapes=[pltpu.VMEM((n_lists * pack_rows, LANES), jnp.float32)],
                compiler_params=PARAMS,
            )(base_arg, gathered, flat_items)
            spill = spill[jnp.arange(n_lists, dtype=jnp.int32) ^ line]
            blocks = [spill[:1]]
            for k in range(1, n_lists):
                blocks.append(lax.ppermute(spill[k : k + 1], "lists", [(i, i ^ k) for i in range(n_lists)]))
            return jnp.concatenate(blocks, axis=0).reshape(n_lists * spare, width)

        came = lax.cond(many[0] > 0, spill_apart, lambda: jnp.zeros((n_lists * spare, width), bf16))
        extras.append(
            pl.pallas_call(
                stay_kernel,
                out_shape=jax.ShapeDtypeStruct(came.shape, bf16),
                in_specs=[VMEM],
                out_specs=VMEM,
                compiler_params=PARAMS,
            )(came)
        )

    events = history.reshape(-1, width)
    hist = [events]
    for shift in range(1, n_users):
        hist.append(lax.ppermute(events, "users", [(i, (i + shift) % n_users) for i in range(n_users)]))
    total_events = n_users * events.shape[0]
    keys, values, turned = pl.pallas_call(
        functools.partial(pairs_kernel, n_users),
        out_shape=(
            jax.ShapeDtypeStruct((HEADS, total_events, width // HEADS + ROW_TILE), bf16),
            jax.ShapeDtypeStruct((width, total_events), bf16),
            jax.ShapeDtypeStruct((width, width), bf16),
        ),
        in_specs=[SMEM, SMEM] + [VMEM] * (n_users + 2),
        out_specs=(VMEM, VMEM, VMEM),
        compiler_params=PARAMS,
    )(col_arg, history_lengths, *hist, key_value_weight, query_weight)

    step = max(1, 288 // main)
    answers = pl.pallas_call(
        functools.partial(owner_kernel, n_lists, user_dev, digits, main, spare, width ** (-0.5)),
        out_shape=jax.ShapeDtypeStruct((n_lists, block, width), bf16),
        in_specs=[SMEM, SMEM] + [VMEM] * (2 + len(siblings)),
        out_specs=pl.BlockSpec(memory_space=pl.ANY),
        scratch_shapes=[
            pltpu.VMEM((n_lists * pack_rows, LANES), jnp.float32),
            pltpu.VMEM((n_lists, block, width), bf16),
            pltpu.SemaphoreType.DMA((-(-n_lists // step),)),
        ],
        compiler_params=PARAMS,
    )(base_arg, other_arg, gathered, items, *siblings)
    fetched = exchange(answers)

    fetched, known, extras, keys, values, turned = lax.optimization_barrier(
        (fetched, known, extras, keys, values, turned)
    )

    sent = []
    if n_users > 1:
        sent = pl.pallas_call(
            functools.partial(place_kernel, n_users),
            out_shape=tuple(jax.ShapeDtypeStruct((share, width), bf16) for _ in range(n_users - 1)),
            in_specs=[SMEM, VMEM, VMEM] + [VMEM] * len(extras),
            out_specs=tuple(VMEM for _ in range(n_users - 1)),
            scratch_shapes=[pltpu.VMEM((cands, 8), jnp.float32)],
            compiler_params=PARAMS,
        )(col_arg, known, fetched, *extras)
    parts = []
    for shift in range(1, n_users):
        parts.append(
            lax.ppermute(sent[shift - 1], "users", [(i, (i + shift) % n_users) for i in range(n_users)])
        )

    list_scores, own = pl.pallas_call(
        functools.partial(expand_kernel, user_dev, pieces, kept),
        out_shape=(
            jax.ShapeDtypeStruct((user_dev * probes, items_loc), bf16),
            jax.ShapeDtypeStruct((share, width), bf16),
        ),
        in_specs=[SMEM, VMEM, VMEM] + [VMEM] * len(extras),
        out_specs=(pl.BlockSpec(memory_space=pl.ANY), VMEM),
        scratch_shapes=[
            pltpu.VMEM((user_dev * probes, items_loc), bf16),
            pltpu.VMEM((cands, 8), jnp.float32),
            pltpu.SemaphoreType.DMA((pieces,)),
        ],
        compiler_params=PARAMS,
    )(col_arg, known, fetched, *extras)
    ranked = pl.pallas_call(
        functools.partial(attend_kernel, n_users),
        out_shape=jax.ShapeDtypeStruct((share, width), bf16),
        in_specs=[VMEM] * (n_users + 4),
        out_specs=VMEM,
        compiler_params=PARAMS,
    )(own, *parts, keys, values, turned, out_weight)
    return (list_scores.reshape(user_dev, probes, items_loc), ranked.reshape(1, share, width))


def solution(mesh):
    placed = (
        P("lists", None),
        P("lists", None),
        P("lists", "users", None),
        P("lists", None),
        P("lists", "users", None),
        P("lists"),
        P(),
        P(),
        P(),
    )
    return jax.shard_map(
        shards,
        mesh=mesh,
        in_specs=placed,
        out_specs=(P("lists", None, "users"), P("lists", "users", None)),
        check_vma=False,
    )
```

```python
import functools

import jax
import jax.numpy as jnp
from jax import lax
from jax.experimental import pallas as pl
from jax.experimental.pallas import tpu as pltpu
from jax.sharding import PartitionSpec as P

HEADS = 8
BASE = 256
LANES = 128
ROW_TILE = 16
VMEM_BYTES = 28 * 1024 * 1024
ALL_VMEM_BYTES = 62 * 1024 * 1024


def round_up(value, step):
    return (value + step - 1) // step * step


def picks(index, count):
    place = lax.broadcasted_iota(jnp.int32, (index.shape[0], count), 1).astype(jnp.int16)
    one, zero = jnp.bfloat16(1.0), jnp.bfloat16(0.0)
    return jnp.where(index.astype(jnp.int16) == place, one, zero)


def pack_kernel(digits, ids_ref, vectors_ref, pack_ref):
    width = vectors_ref.shape[1]
    vectors = vectors_ref[...].astype(jnp.float32)
    ids = ids_ref[...]
    spans = [slice(start, start + LANES) for start in range(0, width, LANES)]
    rows = [vectors[:, span] for span in spans]
    for digit in range(digits):
        value = ((ids >> (8 * digit)) & (BASE - 1)).astype(jnp.float32)
        rows += [value[:, span] for span in spans]
    count = sum(row.shape[0] for row in rows)
    if pack_ref.shape[1] > count:
        rows.append(jnp.zeros((pack_ref.shape[1] - count, LANES), jnp.float32))
    pack_ref[...] = jnp.broadcast_to(jnp.concatenate(rows, axis=0).astype(jnp.bfloat16)[None], pack_ref.shape)


def earlier(count):
    row = lax.broadcasted_iota(jnp.int32, (count, count), 0)
    column = lax.broadcasted_iota(jnp.int32, (count, count), 1)
    return jnp.where(row < column, 1.0, 0.0).astype(jnp.bfloat16)


def unpack(wide, n_lists, user_dev, digits, spans):
    pack_rows = wide.shape[0] // n_lists

    def line(number):
        return wide[pl.ds(number, n_lists, stride=pack_rows), :]

    vectors = jnp.concatenate(
        [
            jnp.concatenate([line(span * user_dev + u) for span in range(spans)], axis=1)
            for u in range(user_dev)
        ],
        axis=0,
    )
    ids = []
    for span in range(spans):
        value = line(user_dev * spans + span)
        for digit in range(1, digits):
            value = value + line((user_dev + digit) * spans + span) * float(BASE**digit)
        ids.append(value)
    return vectors, ids


def asked(ids, base, items_loc, first, count):
    n_lists = ids[0].shape[0]
    local = jnp.concatenate([part - base for part in ids], axis=0)
    mine = (local >= 0.0) & (local < items_loc)
    hot = jnp.where(mine, 1.0, 0.0)
    rank = jnp.dot(hot.astype(jnp.bfloat16), earlier(LANES), preferred_element_type=jnp.float32)
    totals = jnp.sum(hot, axis=1, keepdims=True)
    before = jnp.zeros((n_lists, 1), jnp.float32)
    ranks, locals_ = [], []
    for span in range(len(ids)):
        rows = slice(span * n_lists, (span + 1) * n_lists)
        ranks.append(jnp.where(mine[rows], rank[rows] + before, -1.0))
        locals_.append(local[rows] + 1.0)
        before = before + totals[rows]
    rank, local = jnp.concatenate(ranks, axis=1), jnp.concatenate(locals_, axis=1)
    place = (lax.broadcasted_iota(jnp.int32, (count, rank.shape[1]), 0) + first).astype(jnp.float32)
    index = []
    for r in range(n_lists):
        picked = jnp.where(rank[r : r + 1] == place, local[r : r + 1], 0.0)
        index.append(jnp.sum(picked, axis=1, keepdims=True).astype(jnp.int32) - 1)
    return index, before


def items_kernel(*refs):
    count = len(refs) // 2
    sems = refs[-1]
    parts = sems.shape[1]
    loads = []
    for k in range(count):
        source, target = refs[k], refs[count + k]
        part = source.shape[0] // parts
        for p in range(parts):
            span = pl.ds(p * part, part)
            loads.append(pltpu.make_async_copy(source.at[span], target.at[span], sems.at[k, p]))
            loads[-1].start()
    for load in loads:
        load.wait()


def crowded(ids, n_lists, items_loc, main, spare):
    bins = [part.astype(jnp.int32) // items_loc for part in ids]
    worst = jnp.zeros((n_lists, 1), jnp.float32)
    for owner in range(n_lists):
        count = []
        for c in range(2):
            hits = [jnp.where(part == owner * 2 + c, 1.0, 0.0) for part in bins]
            count.append(jnp.sum(sum(hits[1:], hits[0]), axis=1, keepdims=True))
        for one, other in ((0, 1), (1, 0)):
            clash = (count[one] > float(main - spare)) & (count[other] > float(main))
            worst = jnp.maximum(worst, jnp.where(clash, 1.0, 0.0))
    return jnp.max(worst)


def known_kernel(
    n_lists, items_loc, n_users, user_dev, digits, main, spare, kept, *refs
):
    line_ref, col_ref, ids_ref, probes_ref, gathered_ref, known_ref, many_ref, wide = refs
    block = kept + main
    ids = ids_ref[...]
    cands = ids.shape[1]
    bins = ids // items_loc
    mine = bins % n_users == col_ref[0]
    owner = bins // n_users
    lists = lax.broadcasted_iota(jnp.int32, (n_lists * n_users, cands), 0)
    hot = jnp.where(lists == bins, 1.0, 0.0)
    before = jnp.dot(hot.astype(jnp.bfloat16), earlier(cands), preferred_element_type=jnp.float32)
    rank = jnp.sum(before * hot, axis=0, keepdims=True)
    slot = owner.astype(jnp.float32) * block + kept + rank
    if spare:
        wide[...] = gathered_ref[...].astype(jnp.float32)
        _, asked_ids = unpack(wide, n_lists, user_dev, digits, cands // LANES)
        many = crowded(asked_ids, n_lists, items_loc, main, spare)
        many_ref[0] = many.astype(jnp.int32)
        apart = n_lists * block + (owner ^ line_ref[0]).astype(jnp.float32) * spare + rank - main
        apart = jnp.where(many > 0.5, apart, -1.0)
        there = jnp.where((rank >= float(main)) & (many < 0.5), slot - spare, -1.0)
        slot = jnp.where(mine, jnp.where(rank < float(main), slot, apart), there)
    else:
        many_ref[0] = jnp.int32(0)
        slot = jnp.where(mine, slot, -1.0)
    probes = probes_ref[...].astype(jnp.float32)
    flat = jnp.concatenate([probes[u : u + 1] for u in range(probes.shape[0])], axis=1)
    if flat.shape[1] < cands:
        flat = jnp.concatenate([flat, jnp.zeros((1, cands - flat.shape[1]), jnp.float32)], axis=1)
    row = lax.broadcasted_iota(jnp.int32, known_ref.shape, 0)
    known_ref[...] = jnp.where(row == 0, slot, flat)


def pairs_kernel(n_parts, col_ref, length_ref, *refs):
    parts, (weight_ref, query_ref, keys_ref, values_ref, turned_ref) = refs[:n_parts], refs[n_parts:]
    history = jnp.concatenate([part[...] for part in parts], axis=0)
    pairs = jnp.dot(history, weight_ref[...], preferred_element_type=jnp.float32)
    heads, events, features = keys_ref.shape
    head_dim = features - ROW_TILE
    width = heads * head_dim
    hist_dev = events // n_parts
    event = lax.broadcasted_iota(jnp.int32, (events, ROW_TILE), 0)
    feature = lax.broadcasted_iota(jnp.int32, (events, ROW_TILE), 1)
    position = (col_ref[0] - event // hist_dev + n_parts) % n_parts * hist_dev + event % hist_dev
    mask = jnp.where((position >= length_ref[0]) & (feature == 0), -1e30, 0.0)
    for h in range(heads):
        keys = pairs[:, h * head_dim : (h + 1) * head_dim]
        keys_ref[h] = jnp.concatenate([keys, mask], axis=1).astype(jnp.bfloat16)
    values_ref[...] = jnp.transpose(pairs[:, width:]).astype(jnp.bfloat16)
    turned_ref[...] = jnp.transpose(query_ref[...].astype(jnp.float32)).astype(jnp.bfloat16)


def owner_kernel(
    n_lists, user_dev, digits, main, spare, scale, base_ref, other_ref, gathered_ref, items_ref, *refs
):
    sibling_ref = refs[0] if spare else None
    out_hbm, wide, out_ref, out_sems = refs[-4:]
    items_loc, width = items_ref.shape
    wide[...] = gathered_ref[...].astype(jnp.float32)
    vectors, ids = unpack(wide, n_lists, user_dev, digits, width // LANES)
    index, own = asked(ids, base_ref[0].astype(jnp.float32), items_loc, 0, main)
    scores = lax.dot_general(
        vectors.astype(jnp.bfloat16),
        items_ref[...],
        (((1,), (1,)), ((), ())),
        preferred_element_type=jnp.float32,
    )
    scores = (scores * scale).astype(jnp.bfloat16)
    pieces = items_loc // width
    stacked = jnp.concatenate(
        [scores[:, piece * width : (piece + 1) * width] for piece in range(pieces)], axis=0
    )
    kept = out_ref.shape[1] - main
    entry = lax.broadcasted_iota(jnp.int32, (n_lists * kept, 1), 0)
    wanted = jnp.where(entry % kept < pieces * user_dev, entry % kept * n_lists + entry // kept, -1)
    spread = jnp.dot(
        picks(wanted, stacked.shape[0]), stacked, preferred_element_type=jnp.float32
    ).astype(jnp.bfloat16)
    out_ref[:, :kept, :] = spread.reshape(n_lists, kept, width)
    if spare:
        over, _ = asked(ids, other_ref[0].astype(jnp.float32), items_loc, main, spare)
        over = [jnp.where(own[r : r + 1] > float(main - spare), -1, over[r]) for r in range(n_lists)]
        shared = jnp.dot(
            picks(jnp.concatenate(over, axis=0), items_loc), sibling_ref[...], preferred_element_type=jnp.float32
        )
    step = max(1, 288 // main)
    sends = []
    for number, first in enumerate(range(0, n_lists, step)):
        last = min(n_lists, first + step)
        rows = jnp.dot(
            picks(jnp.concatenate(index[first:last], axis=0), items_loc),
            items_ref[...],
            preferred_element_type=jnp.float32,
        )
        for r in range(first, last):
            mine = rows[(r - first) * main : (r - first + 1) * main]
            out_ref[r, kept : kept + main - spare, :] = mine[: main - spare].astype(jnp.bfloat16)
            if spare:
                both = mine[main - spare :] + shared[r * spare : (r + 1) * spare]
                out_ref[r, kept + main - spare :, :] = both.astype(jnp.bfloat16)
        send = pltpu.make_async_copy(out_ref.at[first:last], out_hbm.at[first:last], out_sems.at[number])
        send.start()
        sends.append(send)
    for send in sends:
        send.wait()


def spill_kernel(n_lists, user_dev, digits, main, base_ref, gathered_ref, items_ref, spill_ref, wide):
    items_loc, width = items_ref.shape
    spare = spill_ref.shape[1]
    wide[...] = gathered_ref[...].astype(jnp.float32)
    _, ids = unpack(wide, n_lists, user_dev, digits, width // LANES)
    index, _ = asked(ids, base_ref[0].astype(jnp.float32), items_loc, main, spare)
    rows = jnp.dot(
        picks(jnp.concatenate(index, axis=0), items_loc), items_ref[...], preferred_element_type=jnp.float32
    )
    spill_ref[...] = rows.astype(jnp.bfloat16).reshape(spill_ref.shape)


def stay_kernel(came_ref, here_ref):
    here_ref[...] = came_ref[...]


def placed(column, known_ref, slots, fetched_ref, extra_refs, out_ref):
    n_lists, block, width = fetched_ref.shape
    share = out_ref.shape[0]
    slots[...] = jnp.transpose(known_ref[...])
    start = pl.multiple_of(column * share, share)
    slot = slots[pl.ds(start, share), :][:, :1].astype(jnp.int32)
    rows = jnp.dot(
        picks(slot, n_lists * block),
        fetched_ref[...].reshape(n_lists * block, width),
        preferred_element_type=jnp.float32,
    )
    for ref in extra_refs:
        rows = rows + jnp.dot(
            picks(slot - n_lists * block, ref.shape[0]), ref[...], preferred_element_type=jnp.float32
        )
    out_ref[...] = rows.astype(jnp.bfloat16)


def place_kernel(n_users, col_ref, known_ref, fetched_ref, *refs):
    extra_refs, sent_refs, slots = refs[: -n_users], refs[-n_users:-1], refs[-1]
    for shift, ref in enumerate(sent_refs):
        placed((col_ref[0] + shift + 1) % n_users, known_ref, slots, fetched_ref, extra_refs, ref)


def attend_kernel(n_parts, *refs):
    parts, (keys_ref, values_ref, turned_ref, out_weight_ref, out_ref) = refs[:n_parts], refs[n_parts:]
    heads, events, features = keys_ref.shape
    head_dim = features - ROW_TILE
    rows = parts[0][...]
    for part in parts[1:]:
        rows = rows + part[...]
    queries = lax.dot_general(
        turned_ref[...], rows, (((1,), (1,)), ((), ())), preferred_element_type=jnp.float32
    )
    queries = (queries * head_dim ** (-0.5)).astype(jnp.bfloat16)
    feature = lax.broadcasted_iota(jnp.int32, (ROW_TILE, rows.shape[0]), 0)
    one = jnp.where(feature == 0, 1.0, 0.0).astype(jnp.bfloat16)

    def score(h):
        query = jnp.concatenate([queries[h * head_dim : (h + 1) * head_dim], one], axis=0)
        return jnp.dot(keys_ref[h], query, preferred_element_type=jnp.float32)

    ahead = [score(h) for h in range(min(2, heads))]
    mixed = []
    for h in range(heads):
        if h + 2 < heads:
            ahead.append(score(h + 2))
        exponentials = jnp.exp(ahead[h] - jnp.max(ahead[h], axis=0, keepdims=True))
        total = jnp.sum(exponentials, axis=0, keepdims=True)
        span = slice(h * head_dim, (h + 1) * head_dim)
        head = jnp.dot(values_ref[span, :], exponentials.astype(jnp.bfloat16), preferred_element_type=jnp.float32)
        mixed.append(head / total)
    attended = jnp.transpose(jnp.concatenate(mixed, axis=0)).astype(jnp.bfloat16)
    out_ref[...] = jnp.dot(attended, out_weight_ref[...], preferred_element_type=jnp.float32).astype(jnp.bfloat16)


def expand_kernel(user_dev, pieces, kept, col_ref, known_ref, fetched_ref, *refs):
    extra_refs, (out_hbm, own_ref, out_ref, slots, sems) = refs[:-5], refs[-5:]
    n_lists, _, width = fetched_ref.shape
    rows = n_lists * kept
    returned = fetched_ref[:, :kept, :].reshape(rows, width)
    count = out_ref.shape[0]
    probe = jnp.transpose(known_ref[:, :count])[:, 1:2].astype(jnp.int32)
    user = lax.broadcasted_iota(jnp.int32, (count, 1), 0) // (count // user_dev)
    sends = []
    for piece in range(pieces):
        wanted = probe * kept + piece * user_dev + user
        span = pl.ds(piece * width, width)
        out_ref[:, span] = jnp.dot(picks(wanted, rows), returned, preferred_element_type=jnp.float32).astype(
            jnp.bfloat16
        )
        sends.append(pltpu.make_async_copy(out_ref.at[:, span], out_hbm.at[:, span], sems.at[piece]))
        sends[-1].start()
    placed(col_ref[0], known_ref, slots, fetched_ref, extra_refs, own_ref)
    for send in sends:
        send.wait()


SMEM = pl.BlockSpec(memory_space=pltpu.SMEM)
VMEM = pl.BlockSpec(memory_space=pltpu.VMEM)
HBM = pl.BlockSpec(memory_space=pltpu.HBM)
PARAMS = pltpu.CompilerParams(vmem_limit_bytes=VMEM_BYTES)


def exchange(value):
    return lax.all_to_all(value, "lists", split_axis=0, concat_axis=0, tiled=True)


def shards(
    user_vectors,
    probe_lists,
    list_items,
    candidate_ids,
    history,
    history_lengths,
    query_weight,
    key_value_weight,
    out_weight,
):
    n_lists = lax.axis_size("lists")
    n_users = lax.axis_size("users")
    _, items_loc, width = list_items.shape
    user_dev, probes = probe_lists.shape
    _, cands = candidate_ids.shape
    bf16 = jnp.bfloat16
    cap = max(2, 3 * cands // (n_lists * n_users))
    cap = round_up(cap, ROW_TILE)
    kept = round_up(items_loc // width * user_dev, ROW_TILE)
    share = cands // n_users
    pieces = items_loc // width
    digits = 1
    while BASE**digits < n_lists * n_users * items_loc:
        digits += 1
    pack_rows = round_up((user_dev + digits) * (width // LANES), 8)
    line = lax.axis_index("lists").astype(jnp.int32)
    col = lax.axis_index("users").astype(jnp.int32)
    col_arg = col.reshape(1)
    line_arg = line.reshape(1)
    base_arg = ((line * n_users + col) * items_loc).reshape(1)
    other_arg = ((line * n_users + n_users - 1 - col) * items_loc).reshape(1)
    spare = 8 if n_users == 2 and cap >= 48 else 0
    main = cap - spare
    block = main + kept

    flat_items = list_items.reshape(items_loc, width)
    pack = pl.pallas_call(
        functools.partial(pack_kernel, digits),
        out_shape=jax.ShapeDtypeStruct((n_lists, pack_rows, LANES), bf16),
        in_specs=[VMEM, VMEM],
        out_specs=VMEM,
        compiler_params=pltpu.CompilerParams(vmem_limit_bytes=ALL_VMEM_BYTES),
    )(candidate_ids, user_vectors)
    gathered = exchange(pack)
    gathered = gathered.reshape(n_lists * pack_rows, LANES)

    halves = [flat_items]
    if spare:
        halves.append(lax.ppermute(flat_items, "users", [(0, 1), (1, 0)]))
    items, *siblings = pl.pallas_call(
        items_kernel,
        out_shape=tuple(jax.ShapeDtypeStruct((items_loc, width), bf16) for _ in halves),
        in_specs=[HBM] * len(halves),
        out_specs=tuple(VMEM for _ in halves),
        scratch_shapes=[pltpu.SemaphoreType.DMA((len(halves), 4))],
        compiler_params=PARAMS,
    )(*halves)
    gathered, items, siblings = lax.optimization_barrier((gathered, items, siblings))

    known, many = pl.pallas_call(
        functools.partial(known_kernel, n_lists, items_loc, n_users, user_dev, digits, main, spare, kept),
        out_shape=(
            jax.ShapeDtypeStruct((8, cands), jnp.float32),
            jax.ShapeDtypeStruct((1,), jnp.int32),
        ),
        in_specs=[SMEM, SMEM, VMEM, VMEM, VMEM],
        out_specs=(VMEM, SMEM),
        scratch_shapes=[pltpu.VMEM((n_lists * pack_rows, LANES), jnp.float32)],
        compiler_params=PARAMS,
    )(line_arg, col_arg, candidate_ids, probe_lists, gathered)

    extras = []
    if spare:

        def spill_apart():
            spill = pl.pallas_call(
                functools.partial(spill_kernel, n_lists, user_dev, digits, main),
                out_shape=jax.ShapeDtypeStruct((n_lists, spare, width), bf16),
                in_specs=[SMEM, VMEM, VMEM],
                out_specs=VMEM,
                scratch_shapes=[pltpu.VMEM((n_lists * pack_rows, LANES), jnp.float32)],
                compiler_params=PARAMS,
            )(base_arg, gathered, flat_items)
            spill = spill[jnp.arange(n_lists, dtype=jnp.int32) ^ line]
            blocks = [spill[:1]]
            for k in range(1, n_lists):
                blocks.append(lax.ppermute(spill[k : k + 1], "lists", [(i, i ^ k) for i in range(n_lists)]))
            return jnp.concatenate(blocks, axis=0).reshape(n_lists * spare, width)

        came = lax.cond(many[0] > 0, spill_apart, lambda: jnp.zeros((n_lists * spare, width), bf16))
        extras.append(
            pl.pallas_call(
                stay_kernel,
                out_shape=jax.ShapeDtypeStruct(came.shape, bf16),
                in_specs=[VMEM],
                out_specs=VMEM,
                compiler_params=PARAMS,
            )(came)
        )

    events = history.reshape(-1, width)
    hist = [events]
    for shift in range(1, n_users):
        hist.append(lax.ppermute(events, "users", [(i, (i + shift) % n_users) for i in range(n_users)]))
    total_events = n_users * events.shape[0]
    keys, values, turned = pl.pallas_call(
        functools.partial(pairs_kernel, n_users),
        out_shape=(
            jax.ShapeDtypeStruct((HEADS, total_events, width // HEADS + ROW_TILE), bf16),
            jax.ShapeDtypeStruct((width, total_events), bf16),
            jax.ShapeDtypeStruct((width, width), bf16),
        ),
        in_specs=[SMEM, SMEM] + [VMEM] * (n_users + 2),
        out_specs=(VMEM, VMEM, VMEM),
        compiler_params=PARAMS,
    )(col_arg, history_lengths, *hist, key_value_weight, query_weight)

    step = max(1, 288 // main)
    answers = pl.pallas_call(
        functools.partial(owner_kernel, n_lists, user_dev, digits, main, spare, width ** (-0.5)),
        out_shape=jax.ShapeDtypeStruct((n_lists, block, width), bf16),
        in_specs=[SMEM, SMEM] + [VMEM] * (2 + len(siblings)),
        out_specs=pl.BlockSpec(memory_space=pl.ANY),
        scratch_shapes=[
            pltpu.VMEM((n_lists * pack_rows, LANES), jnp.float32),
            pltpu.VMEM((n_lists, block, width), bf16),
            pltpu.SemaphoreType.DMA((-(-n_lists // step),)),
        ],
        compiler_params=PARAMS,
    )(base_arg, other_arg, gathered, items, *siblings)
    fetched = exchange(answers)

    fetched, known, extras, keys, values, turned = lax.optimization_barrier(
        (fetched, known, extras, keys, values, turned)
    )

    sent = []
    if n_users > 1:
        sent = pl.pallas_call(
            functools.partial(place_kernel, n_users),
            out_shape=tuple(jax.ShapeDtypeStruct((share, width), bf16) for _ in range(n_users - 1)),
            in_specs=[SMEM, VMEM, VMEM] + [VMEM] * len(extras),
            out_specs=tuple(VMEM for _ in range(n_users - 1)),
            scratch_shapes=[pltpu.VMEM((cands, 8), jnp.float32)],
            compiler_params=PARAMS,
        )(col_arg, known, fetched, *extras)
    parts = []
    for shift in range(1, n_users):
        parts.append(
            lax.ppermute(sent[shift - 1], "users", [(i, (i + shift) % n_users) for i in range(n_users)])
        )

    list_scores, own = pl.pallas_call(
        functools.partial(expand_kernel, user_dev, pieces, kept),
        out_shape=(
            jax.ShapeDtypeStruct((user_dev * probes, items_loc), bf16),
            jax.ShapeDtypeStruct((share, width), bf16),
        ),
        in_specs=[SMEM, VMEM, VMEM] + [VMEM] * len(extras),
        out_specs=(pl.BlockSpec(memory_space=pl.ANY), VMEM),
        scratch_shapes=[
            pltpu.VMEM((user_dev * probes, items_loc), bf16),
            pltpu.VMEM((cands, 8), jnp.float32),
            pltpu.SemaphoreType.DMA((pieces,)),
        ],
        compiler_params=PARAMS,
    )(col_arg, known, fetched, *extras)
    ranked = pl.pallas_call(
        functools.partial(attend_kernel, n_users),
        out_shape=jax.ShapeDtypeStruct((share, width), bf16),
        in_specs=[VMEM] * (n_users + 4),
        out_specs=VMEM,
        compiler_params=PARAMS,
    )(own, *parts, keys, values, turned, out_weight)
    return (list_scores.reshape(user_dev, probes, items_loc), ranked.reshape(1, share, width))


def solution(mesh):
    placed = (
        P("lists", None),
        P("lists", None),
        P("lists", "users", None),
        P("lists", None),
        P("lists", "users", None),
        P("lists"),
        P(),
        P(),
        P(),
    )
    return jax.shard_map(
        shards,
        mesh=mesh,
        in_specs=placed,
        out_specs=(P("lists", None, "users"), P("lists", "users", None)),
        check_vma=False,
    )
```

```python
import functools

import jax
import jax.numpy as jnp
from jax import lax
from jax.experimental import pallas as pl
from jax.experimental.pallas import tpu as pltpu
from jax.sharding import PartitionSpec as P

HEADS = 8
BASE = 256
LANES = 128
ROW_TILE = 16
VMEM_BYTES = 28 * 1024 * 1024
ALL_VMEM_BYTES = 62 * 1024 * 1024


def round_up(value, step):
    return (value + step - 1) // step * step


def picks(index, count):
    place = lax.broadcasted_iota(jnp.int32, (index.shape[0], count), 1).astype(jnp.int16)
    one, zero = jnp.bfloat16(1.0), jnp.bfloat16(0.0)
    return jnp.where(index.astype(jnp.int16) == place, one, zero)


def pack_kernel(digits, ids_ref, vectors_ref, pack_ref):
    width = vectors_ref.shape[1]
    vectors = vectors_ref[...].astype(jnp.float32)
    ids = ids_ref[...]
    spans = [slice(start, start + LANES) for start in range(0, width, LANES)]
    rows = [vectors[:, span] for span in spans]
    for digit in range(digits):
        value = ((ids >> (8 * digit)) & (BASE - 1)).astype(jnp.float32)
        rows += [value[:, span] for span in spans]
    count = sum(row.shape[0] for row in rows)
    if pack_ref.shape[1] > count:
        rows.append(jnp.zeros((pack_ref.shape[1] - count, LANES), jnp.float32))
    pack_ref[...] = jnp.broadcast_to(jnp.concatenate(rows, axis=0).astype(jnp.bfloat16)[None], pack_ref.shape)


def earlier(count):
    row = lax.broadcasted_iota(jnp.int32, (count, count), 0)
    column = lax.broadcasted_iota(jnp.int32, (count, count), 1)
    return jnp.where(row < column, 1.0, 0.0).astype(jnp.bfloat16)


def unpack(wide, n_lists, user_dev, digits, spans):
    pack_rows = wide.shape[0] // n_lists

    def line(number):
        return wide[pl.ds(number, n_lists, stride=pack_rows), :]

    vectors = jnp.concatenate(
        [
            jnp.concatenate([line(span * user_dev + u) for span in range(spans)], axis=1)
            for u in range(user_dev)
        ],
        axis=0,
    )
    ids = []
    for span in range(spans):
        value = line(user_dev * spans + span)
        for digit in range(1, digits):
            value = value + line((user_dev + digit) * spans + span) * float(BASE**digit)
        ids.append(value)
    return vectors, ids


def asked(ids, base, items_loc, first, count):
    n_lists = ids[0].shape[0]
    local = jnp.concatenate([part - base for part in ids], axis=0)
    mine = (local >= 0.0) & (local < items_loc)
    hot = jnp.where(mine, 1.0, 0.0)
    rank = jnp.dot(hot.astype(jnp.bfloat16), earlier(LANES), preferred_element_type=jnp.float32)
    totals = jnp.sum(hot, axis=1, keepdims=True)
    before = jnp.zeros((n_lists, 1), jnp.float32)
    ranks, locals_ = [], []
    for span in range(len(ids)):
        rows = slice(span * n_lists, (span + 1) * n_lists)
        ranks.append(jnp.where(mine[rows], rank[rows] + before, -1.0))
        locals_.append(local[rows] + 1.0)
        before = before + totals[rows]
    rank, local = jnp.concatenate(ranks, axis=1), jnp.concatenate(locals_, axis=1)
    place = (lax.broadcasted_iota(jnp.int32, (count, rank.shape[1]), 0) + first).astype(jnp.float32)
    index = []
    for r in range(n_lists):
        picked = jnp.where(rank[r : r + 1] == place, local[r : r + 1], 0.0)
        index.append(jnp.sum(picked, axis=1, keepdims=True).astype(jnp.int32) - 1)
    return index, before


def items_kernel(items_hbm, items_ref, sems):
    part = items_ref.shape[0] // sems.shape[0]
    loads = []
    for p in range(sems.shape[0]):
        span = pl.ds(p * part, part)
        loads.append(pltpu.make_async_copy(items_hbm.at[span], items_ref.at[span], sems.at[p]))
        loads[-1].start()
    for load in loads:
        load.wait()


def crowded(ids, n_lists, items_loc, main, spare):
    bins = [part.astype(jnp.int32) // items_loc for part in ids]
    worst = jnp.zeros((n_lists, 1), jnp.float32)
    for owner in range(n_lists):
        count = []
        for c in range(2):
            hits = [jnp.where(part == owner * 2 + c, 1.0, 0.0) for part in bins]
            count.append(jnp.sum(sum(hits[1:], hits[0]), axis=1, keepdims=True))
        for one, other in ((0, 1), (1, 0)):
            clash = (count[one] > float(main - spare)) & (count[other] > float(main))
            worst = jnp.maximum(worst, jnp.where(clash, 1.0, 0.0))
    return jnp.max(worst)


def known_kernel(
    n_lists, items_loc, n_users, user_dev, digits, main, spare, kept, *refs
):
    line_ref, col_ref, ids_ref, probes_ref, gathered_ref, known_ref, many_ref, wide = refs
    block = kept + main
    ids = ids_ref[...]
    cands = ids.shape[1]
    bins = ids // items_loc
    mine = bins % n_users == col_ref[0]
    owner = bins // n_users
    lists = lax.broadcasted_iota(jnp.int32, (n_lists * n_users, cands), 0)
    hot = jnp.where(lists == bins, 1.0, 0.0)
    before = jnp.dot(hot.astype(jnp.bfloat16), earlier(cands), preferred_element_type=jnp.float32)
    rank = jnp.sum(before * hot, axis=0, keepdims=True)
    slot = owner.astype(jnp.float32) * block + kept + rank
    if spare:
        wide[...] = gathered_ref[...].astype(jnp.float32)
        _, asked_ids = unpack(wide, n_lists, user_dev, digits, cands // LANES)
        many = crowded(asked_ids, n_lists, items_loc, main, spare)
        many_ref[0] = many.astype(jnp.int32)
        apart = n_lists * block + (owner ^ line_ref[0]).astype(jnp.float32) * spare + rank - main
        apart = jnp.where(many > 0.5, apart, -1.0)
        there = jnp.where((rank >= float(main)) & (many < 0.5), slot - spare, -1.0)
        slot = jnp.where(mine, jnp.where(rank < float(main), slot, apart), there)
    else:
        many_ref[0] = jnp.int32(0)
        slot = jnp.where(mine, slot, -1.0)
    probes = probes_ref[...].astype(jnp.float32)
    flat = jnp.concatenate([probes[u : u + 1] for u in range(probes.shape[0])], axis=1)
    if flat.shape[1] < cands:
        flat = jnp.concatenate([flat, jnp.zeros((1, cands - flat.shape[1]), jnp.float32)], axis=1)
    row = lax.broadcasted_iota(jnp.int32, known_ref.shape, 0)
    known_ref[...] = jnp.where(row == 0, slot, flat)


def pairs_kernel(n_parts, col_ref, length_ref, *refs):
    parts, (weight_ref, query_ref, keys_ref, values_ref, turned_ref) = refs[:n_parts], refs[n_parts:]
    history = jnp.concatenate([part[...] for part in parts], axis=0)
    pairs = jnp.dot(history, weight_ref[...], preferred_element_type=jnp.float32)
    heads, events, features = keys_ref.shape
    head_dim = features - ROW_TILE
    width = heads * head_dim
    hist_dev = events // n_parts
    event = lax.broadcasted_iota(jnp.int32, (events, ROW_TILE), 0)
    feature = lax.broadcasted_iota(jnp.int32, (events, ROW_TILE), 1)
    position = (col_ref[0] - event // hist_dev + n_parts) % n_parts * hist_dev + event % hist_dev
    mask = jnp.where((position >= length_ref[0]) & (feature == 0), -1e30, 0.0)
    for h in range(heads):
        keys = pairs[:, h * head_dim : (h + 1) * head_dim]
        keys_ref[h] = jnp.concatenate([keys, mask], axis=1).astype(jnp.bfloat16)
    values_ref[...] = jnp.transpose(pairs[:, width:]).astype(jnp.bfloat16)
    turned_ref[...] = jnp.transpose(query_ref[...].astype(jnp.float32)).astype(jnp.bfloat16)


def owner_kernel(
    n_lists, user_dev, digits, main, spare, scale, base_ref, other_ref, gathered_ref, items_ref, *refs
):
    loads = []
    if spare:
        sibling_hbm, out_hbm, wide, out_ref, out_sems, sibling_ref, in_sems = refs
        part = sibling_ref.shape[0] // in_sems.shape[0]
        for p in range(in_sems.shape[0]):
            span = pl.ds(p * part, part)
            loads.append(pltpu.make_async_copy(sibling_hbm.at[span], sibling_ref.at[span], in_sems.at[p]))
            loads[-1].start()
    else:
        out_hbm, wide, out_ref, out_sems = refs
    items_loc, width = items_ref.shape
    wide[...] = gathered_ref[...].astype(jnp.float32)
    vectors, ids = unpack(wide, n_lists, user_dev, digits, width // LANES)
    index, own = asked(ids, base_ref[0].astype(jnp.float32), items_loc, 0, main)
    scores = lax.dot_general(
        vectors.astype(jnp.bfloat16),
        items_ref[...],
        (((1,), (1,)), ((), ())),
        preferred_element_type=jnp.float32,
    )
    scores = (scores * scale).astype(jnp.bfloat16)
    pieces = items_loc // width
    stacked = jnp.concatenate(
        [scores[:, piece * width : (piece + 1) * width] for piece in range(pieces)], axis=0
    )
    kept = out_ref.shape[1] - main
    entry = lax.broadcasted_iota(jnp.int32, (n_lists * kept, 1), 0)
    wanted = jnp.where(entry % kept < pieces * user_dev, entry % kept * n_lists + entry // kept, -1)
    spread = jnp.dot(
        picks(wanted, stacked.shape[0]), stacked, preferred_element_type=jnp.float32
    ).astype(jnp.bfloat16)
    out_ref[:, :kept, :] = spread.reshape(n_lists, kept, width)
    if spare:
        over, _ = asked(ids, other_ref[0].astype(jnp.float32), items_loc, main, spare)
        over = [jnp.where(own[r : r + 1] > float(main - spare), -1, over[r]) for r in range(n_lists)]
    step = max(1, 288 // main)
    sends = []
    for number, first in enumerate(range(0, n_lists, step)):
        last = min(n_lists, first + step)
        rows = jnp.dot(
            picks(jnp.concatenate(index[first:last], axis=0), items_loc),
            items_ref[...],
            preferred_element_type=jnp.float32,
        )
        if spare and first == 0:
            for load in loads:
                load.wait()
            shared = jnp.dot(
                picks(jnp.concatenate(over, axis=0), items_loc),
                sibling_ref[...],
                preferred_element_type=jnp.float32,
            )
        for r in range(first, last):
            mine = rows[(r - first) * main : (r - first + 1) * main]
            out_ref[r, kept : kept + main - spare, :] = mine[: main - spare].astype(jnp.bfloat16)
            if spare:
                both = mine[main - spare :] + shared[r * spare : (r + 1) * spare]
                out_ref[r, kept + main - spare :, :] = both.astype(jnp.bfloat16)
        send = pltpu.make_async_copy(out_ref.at[first:last], out_hbm.at[first:last], out_sems.at[number])
        send.start()
        sends.append(send)
    for send in sends:
        send.wait()


def spill_kernel(n_lists, user_dev, digits, main, base_ref, gathered_ref, items_ref, spill_ref, wide):
    items_loc, width = items_ref.shape
    spare = spill_ref.shape[1]
    wide[...] = gathered_ref[...].astype(jnp.float32)
    _, ids = unpack(wide, n_lists, user_dev, digits, width // LANES)
    index, _ = asked(ids, base_ref[0].astype(jnp.float32), items_loc, main, spare)
    rows = jnp.dot(
        picks(jnp.concatenate(index, axis=0), items_loc), items_ref[...], preferred_element_type=jnp.float32
    )
    spill_ref[...] = rows.astype(jnp.bfloat16).reshape(spill_ref.shape)


def stay_kernel(came_ref, here_ref):
    here_ref[...] = came_ref[...]


def placed(column, known_ref, slots, fetched_ref, extra_refs, out_ref):
    n_lists, block, width = fetched_ref.shape
    share = out_ref.shape[0]
    slots[...] = jnp.transpose(known_ref[...])
    start = pl.multiple_of(column * share, share)
    slot = slots[pl.ds(start, share), :][:, :1].astype(jnp.int32)
    rows = jnp.dot(
        picks(slot, n_lists * block),
        fetched_ref[...].reshape(n_lists * block, width),
        preferred_element_type=jnp.float32,
    )
    for ref in extra_refs:
        rows = rows + jnp.dot(
            picks(slot - n_lists * block, ref.shape[0]), ref[...], preferred_element_type=jnp.float32
        )
    out_ref[...] = rows.astype(jnp.bfloat16)


def place_kernel(n_users, col_ref, known_ref, fetched_ref, *refs):
    extra_refs, sent_refs, slots = refs[: -n_users], refs[-n_users:-1], refs[-1]
    for shift, ref in enumerate(sent_refs):
        placed((col_ref[0] + shift + 1) % n_users, known_ref, slots, fetched_ref, extra_refs, ref)


def attend_kernel(n_parts, *refs):
    parts, (keys_ref, values_ref, turned_ref, out_weight_ref, out_ref) = refs[:n_parts], refs[n_parts:]
    heads, events, features = keys_ref.shape
    head_dim = features - ROW_TILE
    rows = parts[0][...]
    for part in parts[1:]:
        rows = rows + part[...]
    queries = lax.dot_general(
        turned_ref[...], rows, (((1,), (1,)), ((), ())), preferred_element_type=jnp.float32
    )
    queries = (queries * head_dim ** (-0.5)).astype(jnp.bfloat16)
    feature = lax.broadcasted_iota(jnp.int32, (ROW_TILE, rows.shape[0]), 0)
    one = jnp.where(feature == 0, 1.0, 0.0).astype(jnp.bfloat16)

    def score(h):
        query = jnp.concatenate([queries[h * head_dim : (h + 1) * head_dim], one], axis=0)
        return jnp.dot(keys_ref[h], query, preferred_element_type=jnp.float32)

    ahead = [score(h) for h in range(min(2, heads))]
    mixed = []
    for h in range(heads):
        if h + 2 < heads:
            ahead.append(score(h + 2))
        exponentials = jnp.exp(ahead[h] - jnp.max(ahead[h], axis=0, keepdims=True))
        total = jnp.sum(exponentials, axis=0, keepdims=True)
        span = slice(h * head_dim, (h + 1) * head_dim)
        head = jnp.dot(values_ref[span, :], exponentials.astype(jnp.bfloat16), preferred_element_type=jnp.float32)
        mixed.append(head / total)
    attended = jnp.transpose(jnp.concatenate(mixed, axis=0)).astype(jnp.bfloat16)
    out_ref[...] = jnp.dot(attended, out_weight_ref[...], preferred_element_type=jnp.float32).astype(jnp.bfloat16)


def expand_kernel(user_dev, pieces, kept, col_ref, known_ref, fetched_ref, *refs):
    extra_refs, (out_hbm, own_ref, out_ref, slots, sems) = refs[:-5], refs[-5:]
    n_lists, _, width = fetched_ref.shape
    rows = n_lists * kept
    returned = fetched_ref[:, :kept, :].reshape(rows, width)
    count = out_ref.shape[0]
    probe = jnp.transpose(known_ref[:, :count])[:, 1:2].astype(jnp.int32)
    user = lax.broadcasted_iota(jnp.int32, (count, 1), 0) // (count // user_dev)
    sends = []
    for piece in range(pieces):
        wanted = probe * kept + piece * user_dev + user
        span = pl.ds(piece * width, width)
        out_ref[:, span] = jnp.dot(picks(wanted, rows), returned, preferred_element_type=jnp.float32).astype(
            jnp.bfloat16
        )
        sends.append(pltpu.make_async_copy(out_ref.at[:, span], out_hbm.at[:, span], sems.at[piece]))
        sends[-1].start()
    placed(col_ref[0], known_ref, slots, fetched_ref, extra_refs, own_ref)
    for send in sends:
        send.wait()


SMEM = pl.BlockSpec(memory_space=pltpu.SMEM)
VMEM = pl.BlockSpec(memory_space=pltpu.VMEM)
HBM = pl.BlockSpec(memory_space=pltpu.HBM)
PARAMS = pltpu.CompilerParams(vmem_limit_bytes=VMEM_BYTES)


def exchange(value):
    return lax.all_to_all(value, "lists", split_axis=0, concat_axis=0, tiled=True)


def shards(
    user_vectors,
    probe_lists,
    list_items,
    candidate_ids,
    history,
    history_lengths,
    query_weight,
    key_value_weight,
    out_weight,
):
    n_lists = lax.axis_size("lists")
    n_users = lax.axis_size("users")
    _, items_loc, width = list_items.shape
    user_dev, probes = probe_lists.shape
    _, cands = candidate_ids.shape
    bf16 = jnp.bfloat16
    cap = max(2, 3 * cands // (n_lists * n_users))
    cap = round_up(cap, ROW_TILE)
    kept = round_up(items_loc // width * user_dev, ROW_TILE)
    share = cands // n_users
    pieces = items_loc // width
    digits = 1
    while BASE**digits < n_lists * n_users * items_loc:
        digits += 1
    pack_rows = round_up((user_dev + digits) * (width // LANES), 8)
    line = lax.axis_index("lists").astype(jnp.int32)
    col = lax.axis_index("users").astype(jnp.int32)
    col_arg = col.reshape(1)
    line_arg = line.reshape(1)
    base_arg = ((line * n_users + col) * items_loc).reshape(1)
    other_arg = ((line * n_users + n_users - 1 - col) * items_loc).reshape(1)
    spare = 8 if n_users == 2 and cap >= 48 else 0
    main = cap - spare
    block = main + kept

    flat_items = list_items.reshape(items_loc, width)
    pack = pl.pallas_call(
        functools.partial(pack_kernel, digits),
        out_shape=jax.ShapeDtypeStruct((n_lists, pack_rows, LANES), bf16),
        in_specs=[VMEM, VMEM],
        out_specs=VMEM,
        compiler_params=pltpu.CompilerParams(vmem_limit_bytes=ALL_VMEM_BYTES),
    )(candidate_ids, user_vectors)
    gathered = exchange(pack)
    gathered = gathered.reshape(n_lists * pack_rows, LANES)

    items = pl.pallas_call(
        items_kernel,
        out_shape=jax.ShapeDtypeStruct((items_loc, width), bf16),
        in_specs=[HBM],
        out_specs=VMEM,
        scratch_shapes=[pltpu.SemaphoreType.DMA((4,))],
        compiler_params=PARAMS,
    )(flat_items)
    gathered, items = lax.optimization_barrier((gathered, items))

    siblings = []
    if spare:
        siblings.append(lax.ppermute(flat_items, "users", [(0, 1), (1, 0)]))

    known, many = pl.pallas_call(
        functools.partial(known_kernel, n_lists, items_loc, n_users, user_dev, digits, main, spare, kept),
        out_shape=(
            jax.ShapeDtypeStruct((8, cands), jnp.float32),
            jax.ShapeDtypeStruct((1,), jnp.int32),
        ),
        in_specs=[SMEM, SMEM, VMEM, VMEM, VMEM],
        out_specs=(VMEM, SMEM),
        scratch_shapes=[pltpu.VMEM((n_lists * pack_rows, LANES), jnp.float32)],
        compiler_params=PARAMS,
    )(line_arg, col_arg, candidate_ids, probe_lists, gathered)

    extras = []
    if spare:

        def spill_apart():
            spill = pl.pallas_call(
                functools.partial(spill_kernel, n_lists, user_dev, digits, main),
                out_shape=jax.ShapeDtypeStruct((n_lists, spare, width), bf16),
                in_specs=[SMEM, VMEM, VMEM],
                out_specs=VMEM,
                scratch_shapes=[pltpu.VMEM((n_lists * pack_rows, LANES), jnp.float32)],
                compiler_params=PARAMS,
            )(base_arg, gathered, flat_items)
            spill = spill[jnp.arange(n_lists, dtype=jnp.int32) ^ line]
            blocks = [spill[:1]]
            for k in range(1, n_lists):
                blocks.append(lax.ppermute(spill[k : k + 1], "lists", [(i, i ^ k) for i in range(n_lists)]))
            return jnp.concatenate(blocks, axis=0).reshape(n_lists * spare, width)

        came = lax.cond(many[0] > 0, spill_apart, lambda: jnp.zeros((n_lists * spare, width), bf16))
        extras.append(
            pl.pallas_call(
                stay_kernel,
                out_shape=jax.ShapeDtypeStruct(came.shape, bf16),
                in_specs=[VMEM],
                out_specs=VMEM,
                compiler_params=PARAMS,
            )(came)
        )

    events = history.reshape(-1, width)
    hist = [events]
    for shift in range(1, n_users):
        hist.append(lax.ppermute(events, "users", [(i, (i + shift) % n_users) for i in range(n_users)]))
    total_events = n_users * events.shape[0]
    keys, values, turned = pl.pallas_call(
        functools.partial(pairs_kernel, n_users),
        out_shape=(
            jax.ShapeDtypeStruct((HEADS, total_events, width // HEADS + ROW_TILE), bf16),
            jax.ShapeDtypeStruct((width, total_events), bf16),
            jax.ShapeDtypeStruct((width, width), bf16),
        ),
        in_specs=[SMEM, SMEM] + [VMEM] * (n_users + 2),
        out_specs=(VMEM, VMEM, VMEM),
        compiler_params=PARAMS,
    )(col_arg, history_lengths, *hist, key_value_weight, query_weight)

    step = max(1, 288 // main)
    answers = pl.pallas_call(
        functools.partial(owner_kernel, n_lists, user_dev, digits, main, spare, width ** (-0.5)),
        out_shape=jax.ShapeDtypeStruct((n_lists, block, width), bf16),
        in_specs=[SMEM, SMEM, VMEM, VMEM] + [pl.BlockSpec(memory_space=pl.ANY)] * len(siblings),
        out_specs=pl.BlockSpec(memory_space=pl.ANY),
        scratch_shapes=[
            pltpu.VMEM((n_lists * pack_rows, LANES), jnp.float32),
            pltpu.VMEM((n_lists, block, width), bf16),
            pltpu.SemaphoreType.DMA((-(-n_lists // step),)),
        ]
        + [pltpu.VMEM((items_loc, width), bf16), pltpu.SemaphoreType.DMA((4,))] * len(siblings),
        compiler_params=PARAMS,
    )(base_arg, other_arg, gathered, items, *siblings)
    fetched = exchange(answers)

    fetched, known, extras, keys, values, turned = lax.optimization_barrier(
        (fetched, known, extras, keys, values, turned)
    )

    sent = []
    if n_users > 1:
        sent = pl.pallas_call(
            functools.partial(place_kernel, n_users),
            out_shape=tuple(jax.ShapeDtypeStruct((share, width), bf16) for _ in range(n_users - 1)),
            in_specs=[SMEM, VMEM, VMEM] + [VMEM] * len(extras),
            out_specs=tuple(VMEM for _ in range(n_users - 1)),
            scratch_shapes=[pltpu.VMEM((cands, 8), jnp.float32)],
            compiler_params=PARAMS,
        )(col_arg, known, fetched, *extras)
    parts = []
    for shift in range(1, n_users):
        parts.append(
            lax.ppermute(sent[shift - 1], "users", [(i, (i + shift) % n_users) for i in range(n_users)])
        )

    list_scores, own = pl.pallas_call(
        functools.partial(expand_kernel, user_dev, pieces, kept),
        out_shape=(
            jax.ShapeDtypeStruct((user_dev * probes, items_loc), bf16),
            jax.ShapeDtypeStruct((share, width), bf16),
        ),
        in_specs=[SMEM, VMEM, VMEM] + [VMEM] * len(extras),
        out_specs=(pl.BlockSpec(memory_space=pl.ANY), VMEM),
        scratch_shapes=[
            pltpu.VMEM((user_dev * probes, items_loc), bf16),
            pltpu.VMEM((cands, 8), jnp.float32),
            pltpu.SemaphoreType.DMA((pieces,)),
        ],
        compiler_params=PARAMS,
    )(col_arg, known, fetched, *extras)
    ranked = pl.pallas_call(
        functools.partial(attend_kernel, n_users),
        out_shape=jax.ShapeDtypeStruct((share, width), bf16),
        in_specs=[VMEM] * (n_users + 4),
        out_specs=VMEM,
        compiler_params=PARAMS,
    )(own, *parts, keys, values, turned, out_weight)
    return (list_scores.reshape(user_dev, probes, items_loc), ranked.reshape(1, share, width))


def solution(mesh):
    placed = (
        P("lists", None),
        P("lists", None),
        P("lists", "users", None),
        P("lists", None),
        P("lists", "users", None),
        P("lists"),
        P(),
        P(),
        P(),
    )
    return jax.shard_map(
        shards,
        mesh=mesh,
        in_specs=placed,
        out_specs=(P("lists", None, "users"), P("lists", "users", None)),
        check_vma=False,
    )
```

```python
import functools

import jax
import jax.numpy as jnp
from jax import lax
from jax.experimental import pallas as pl
from jax.experimental.pallas import tpu as pltpu
from jax.sharding import PartitionSpec as P

HEADS = 8
BASE = 256
LANES = 128
ROW_TILE = 16
VMEM_BYTES = 28 * 1024 * 1024
ALL_VMEM_BYTES = 62 * 1024 * 1024


def round_up(value, step):
    return (value + step - 1) // step * step


def picks(index, count):
    place = lax.broadcasted_iota(jnp.int32, (index.shape[0], count), 1).astype(jnp.int16)
    one, zero = jnp.bfloat16(1.0), jnp.bfloat16(0.0)
    return jnp.where(index.astype(jnp.int16) == place, one, zero)


def pack_kernel(digits, ids_ref, vectors_ref, pack_ref):
    width = vectors_ref.shape[1]
    vectors = vectors_ref[...].astype(jnp.float32)
    ids = ids_ref[...]
    spans = [slice(start, start + LANES) for start in range(0, width, LANES)]
    rows = [vectors[:, span] for span in spans]
    for digit in range(digits):
        value = ((ids >> (8 * digit)) & (BASE - 1)).astype(jnp.float32)
        rows += [value[:, span] for span in spans]
    count = sum(row.shape[0] for row in rows)
    if pack_ref.shape[1] > count:
        rows.append(jnp.zeros((pack_ref.shape[1] - count, LANES), jnp.float32))
    pack_ref[...] = jnp.broadcast_to(jnp.concatenate(rows, axis=0).astype(jnp.bfloat16)[None], pack_ref.shape)


def earlier(count):
    row = lax.broadcasted_iota(jnp.int32, (count, count), 0)
    column = lax.broadcasted_iota(jnp.int32, (count, count), 1)
    return jnp.where(row < column, 1.0, 0.0).astype(jnp.bfloat16)


def unpack(wide, n_lists, user_dev, digits, spans):
    pack_rows = wide.shape[0] // n_lists

    def line(number):
        return wide[pl.ds(number, n_lists, stride=pack_rows), :]

    vectors = jnp.concatenate(
        [
            jnp.concatenate([line(span * user_dev + u) for span in range(spans)], axis=1)
            for u in range(user_dev)
        ],
        axis=0,
    )
    ids = []
    for span in range(spans):
        value = line(user_dev * spans + span)
        for digit in range(1, digits):
            value = value + line((user_dev + digit) * spans + span) * float(BASE**digit)
        ids.append(value)
    return vectors, ids


def asked(ids, base, items_loc, first, count):
    n_lists = ids[0].shape[0]
    local = jnp.concatenate([part - base for part in ids], axis=0)
    mine = (local >= 0.0) & (local < items_loc)
    hot = jnp.where(mine, 1.0, 0.0)
    rank = jnp.dot(hot.astype(jnp.bfloat16), earlier(LANES), preferred_element_type=jnp.float32)
    totals = jnp.sum(hot, axis=1, keepdims=True)
    before = jnp.zeros((n_lists, 1), jnp.float32)
    ranks, locals_ = [], []
    for span in range(len(ids)):
        rows = slice(span * n_lists, (span + 1) * n_lists)
        ranks.append(jnp.where(mine[rows], rank[rows] + before, -1.0))
        locals_.append(local[rows] + 1.0)
        before = before + totals[rows]
    rank, local = jnp.concatenate(ranks, axis=1), jnp.concatenate(locals_, axis=1)
    place = (lax.broadcasted_iota(jnp.int32, (count, rank.shape[1]), 0) + first).astype(jnp.float32)
    index = []
    for r in range(n_lists):
        picked = jnp.where(rank[r : r + 1] == place, local[r : r + 1], 0.0)
        index.append(jnp.sum(picked, axis=1, keepdims=True).astype(jnp.int32) - 1)
    return index, before


def items_kernel(items_hbm, items_ref, sems):
    part = items_ref.shape[0] // sems.shape[0]
    loads = []
    for p in range(sems.shape[0]):
        span = pl.ds(p * part, part)
        loads.append(pltpu.make_async_copy(items_hbm.at[span], items_ref.at[span], sems.at[p]))
        loads[-1].start()
    for load in loads:
        load.wait()


def crowded(ids, n_lists, items_loc, main, spare):
    bins = [part.astype(jnp.int32) // items_loc for part in ids]
    worst = jnp.zeros((n_lists, 1), jnp.float32)
    for owner in range(n_lists):
        count = []
        for c in range(2):
            hits = [jnp.where(part == owner * 2 + c, 1.0, 0.0) for part in bins]
            count.append(jnp.sum(sum(hits[1:], hits[0]), axis=1, keepdims=True))
        for one, other in ((0, 1), (1, 0)):
            clash = (count[one] > float(main - spare)) & (count[other] > float(main))
            worst = jnp.maximum(worst, jnp.where(clash, 1.0, 0.0))
    return jnp.max(worst)


def known_kernel(
    n_lists, items_loc, n_users, user_dev, digits, main, spare, kept, *refs
):
    line_ref, col_ref, ids_ref, probes_ref, gathered_ref, known_ref, many_ref, wide = refs
    block = kept + main
    ids = ids_ref[...]
    cands = ids.shape[1]
    bins = ids // items_loc
    mine = bins % n_users == col_ref[0]
    owner = bins // n_users
    lists = lax.broadcasted_iota(jnp.int32, (n_lists * n_users, cands), 0)
    hot = jnp.where(lists == bins, 1.0, 0.0)
    before = jnp.dot(hot.astype(jnp.bfloat16), earlier(cands), preferred_element_type=jnp.float32)
    rank = jnp.sum(before * hot, axis=0, keepdims=True)
    slot = owner.astype(jnp.float32) * block + kept + rank
    if spare:
        wide[...] = gathered_ref[...].astype(jnp.float32)
        _, asked_ids = unpack(wide, n_lists, user_dev, digits, cands // LANES)
        many = crowded(asked_ids, n_lists, items_loc, main, spare)
        many_ref[0] = many.astype(jnp.int32)
        apart = n_lists * block + (owner ^ line_ref[0]).astype(jnp.float32) * spare + rank - main
        apart = jnp.where(many > 0.5, apart, -1.0)
        there = jnp.where((rank >= float(main)) & (many < 0.5), slot - spare, -1.0)
        slot = jnp.where(mine, jnp.where(rank < float(main), slot, apart), there)
    else:
        many_ref[0] = jnp.int32(0)
        slot = jnp.where(mine, slot, -1.0)
    probes = probes_ref[...].astype(jnp.float32)
    flat = jnp.concatenate([probes[u : u + 1] for u in range(probes.shape[0])], axis=1)
    if flat.shape[1] < cands:
        flat = jnp.concatenate([flat, jnp.zeros((1, cands - flat.shape[1]), jnp.float32)], axis=1)
    row = lax.broadcasted_iota(jnp.int32, known_ref.shape, 0)
    known_ref[...] = jnp.where(row == 0, slot, flat)


def pairs_kernel(n_parts, col_ref, length_ref, *refs):
    parts, (weight_ref, query_ref, keys_ref, values_ref, turned_ref) = refs[:n_parts], refs[n_parts:]
    history = jnp.concatenate([part[...] for part in parts], axis=0)
    pairs = jnp.dot(history, weight_ref[...], preferred_element_type=jnp.float32)
    heads, events, features = keys_ref.shape
    head_dim = features - ROW_TILE
    width = heads * head_dim
    hist_dev = events // n_parts
    event = lax.broadcasted_iota(jnp.int32, (events, ROW_TILE), 0)
    feature = lax.broadcasted_iota(jnp.int32, (events, ROW_TILE), 1)
    position = (col_ref[0] - event // hist_dev + n_parts) % n_parts * hist_dev + event % hist_dev
    mask = jnp.where((position >= length_ref[0]) & (feature == 0), -1e30, 0.0)
    for h in range(heads):
        keys = pairs[:, h * head_dim : (h + 1) * head_dim]
        keys_ref[h] = jnp.concatenate([keys, mask], axis=1).astype(jnp.bfloat16)
    values_ref[...] = jnp.transpose(pairs[:, width:]).astype(jnp.bfloat16)
    turned_ref[...] = jnp.transpose(query_ref[...].astype(jnp.float32)).astype(jnp.bfloat16)


def owner_kernel(
    n_lists, user_dev, digits, main, spare, scale, base_ref, other_ref, gathered_ref, items_ref, *refs
):
    loads = []
    if spare:
        sibling_hbm, out_hbm, wide, out_ref, out_sems, sibling_ref, in_sems = refs
        part = sibling_ref.shape[0] // in_sems.shape[0]
        for p in range(in_sems.shape[0]):
            span = pl.ds(p * part, part)
            loads.append(pltpu.make_async_copy(sibling_hbm.at[span], sibling_ref.at[span], in_sems.at[p]))
            loads[-1].start()
    else:
        out_hbm, wide, out_ref, out_sems = refs
    items_loc, width = items_ref.shape
    wide[...] = gathered_ref[...].astype(jnp.float32)
    vectors, ids = unpack(wide, n_lists, user_dev, digits, width // LANES)
    index, own = asked(ids, base_ref[0].astype(jnp.float32), items_loc, 0, main)
    scores = lax.dot_general(
        vectors.astype(jnp.bfloat16),
        items_ref[...],
        (((1,), (1,)), ((), ())),
        preferred_element_type=jnp.float32,
    )
    scores = (scores * scale).astype(jnp.bfloat16)
    pieces = items_loc // width
    stacked = jnp.concatenate(
        [scores[:, piece * width : (piece + 1) * width] for piece in range(pieces)], axis=0
    )
    kept = out_ref.shape[1] - main
    entry = lax.broadcasted_iota(jnp.int32, (n_lists * kept, 1), 0)
    wanted = jnp.where(entry % kept < pieces * user_dev, entry % kept * n_lists + entry // kept, -1)
    spread = jnp.dot(
        picks(wanted, stacked.shape[0]), stacked, preferred_element_type=jnp.float32
    ).astype(jnp.bfloat16)
    out_ref[:, :kept, :] = spread.reshape(n_lists, kept, width)
    if spare:
        over, _ = asked(ids, other_ref[0].astype(jnp.float32), items_loc, main, spare)
        over = [jnp.where(own[r : r + 1] > float(main - spare), -1, over[r]) for r in range(n_lists)]
    step = max(1, 288 // main)
    chunks = [(first, min(n_lists, first + step)) for first in range(0, n_lists, step)]
    sends = []

    def finish(number):
        first, last = chunks[number]
        if spare:
            for r in range(first, last):
                out_ref[r, kept + main - spare :, :] += shared[r * spare : (r + 1) * spare]
        send = pltpu.make_async_copy(out_ref.at[first:last], out_hbm.at[first:last], out_sems.at[number])
        send.start()
        sends.append(send)

    for number, (first, last) in enumerate(chunks):
        rows = jnp.dot(
            picks(jnp.concatenate(index[first:last], axis=0), items_loc),
            items_ref[...],
            preferred_element_type=jnp.float32,
        ).astype(jnp.bfloat16)
        for r in range(first, last):
            out_ref[r, kept:, :] = rows[(r - first) * main : (r - first + 1) * main]
        if number == max(0, len(chunks) - 2):
            if spare:
                for load in loads:
                    load.wait()
                shared = jnp.dot(
                    picks(jnp.concatenate(over, axis=0), items_loc),
                    sibling_ref[...],
                    preferred_element_type=jnp.float32,
                ).astype(jnp.bfloat16)
            for done in range(number + 1):
                finish(done)
        elif number == len(chunks) - 1:
            finish(number)
    for send in sends:
        send.wait()


def spill_kernel(n_lists, user_dev, digits, main, base_ref, gathered_ref, items_ref, spill_ref, wide):
    items_loc, width = items_ref.shape
    spare = spill_ref.shape[1]
    wide[...] = gathered_ref[...].astype(jnp.float32)
    _, ids = unpack(wide, n_lists, user_dev, digits, width // LANES)
    index, _ = asked(ids, base_ref[0].astype(jnp.float32), items_loc, main, spare)
    rows = jnp.dot(
        picks(jnp.concatenate(index, axis=0), items_loc), items_ref[...], preferred_element_type=jnp.float32
    )
    spill_ref[...] = rows.astype(jnp.bfloat16).reshape(spill_ref.shape)


def stay_kernel(came_ref, here_ref):
    here_ref[...] = came_ref[...]


def placed(column, known_ref, slots, fetched_ref, extra_refs, out_ref):
    n_lists, block, width = fetched_ref.shape
    share = out_ref.shape[0]
    slots[...] = jnp.transpose(known_ref[...])
    start = pl.multiple_of(column * share, share)
    slot = slots[pl.ds(start, share), :][:, :1].astype(jnp.int32)
    rows = jnp.dot(
        picks(slot, n_lists * block),
        fetched_ref[...].reshape(n_lists * block, width),
        preferred_element_type=jnp.float32,
    )
    for ref in extra_refs:
        rows = rows + jnp.dot(
            picks(slot - n_lists * block, ref.shape[0]), ref[...], preferred_element_type=jnp.float32
        )
    out_ref[...] = rows.astype(jnp.bfloat16)


def place_kernel(n_users, col_ref, known_ref, fetched_ref, *refs):
    extra_refs, sent_refs, slots = refs[: -n_users], refs[-n_users:-1], refs[-1]
    for shift, ref in enumerate(sent_refs):
        placed((col_ref[0] + shift + 1) % n_users, known_ref, slots, fetched_ref, extra_refs, ref)


def attend_kernel(n_parts, *refs):
    parts, (keys_ref, values_ref, turned_ref, out_weight_ref, out_ref) = refs[:n_parts], refs[n_parts:]
    heads, events, features = keys_ref.shape
    head_dim = features - ROW_TILE
    rows = parts[0][...]
    for part in parts[1:]:
        rows = rows + part[...]
    queries = lax.dot_general(
        turned_ref[...], rows, (((1,), (1,)), ((), ())), preferred_element_type=jnp.float32
    )
    queries = (queries * head_dim ** (-0.5)).astype(jnp.bfloat16)
    feature = lax.broadcasted_iota(jnp.int32, (ROW_TILE, rows.shape[0]), 0)
    one = jnp.where(feature == 0, 1.0, 0.0).astype(jnp.bfloat16)

    def score(h):
        query = jnp.concatenate([queries[h * head_dim : (h + 1) * head_dim], one], axis=0)
        return jnp.dot(keys_ref[h], query, preferred_element_type=jnp.float32)

    ahead = [score(h) for h in range(min(2, heads))]
    mixed = []
    for h in range(heads):
        if h + 2 < heads:
            ahead.append(score(h + 2))
        exponentials = jnp.exp(ahead[h] - jnp.max(ahead[h], axis=0, keepdims=True))
        total = jnp.sum(exponentials, axis=0, keepdims=True)
        span = slice(h * head_dim, (h + 1) * head_dim)
        head = jnp.dot(values_ref[span, :], exponentials.astype(jnp.bfloat16), preferred_element_type=jnp.float32)
        mixed.append(head / total)
    attended = jnp.transpose(jnp.concatenate(mixed, axis=0)).astype(jnp.bfloat16)
    out_ref[...] = jnp.dot(attended, out_weight_ref[...], preferred_element_type=jnp.float32).astype(jnp.bfloat16)


def expand_kernel(user_dev, pieces, kept, col_ref, known_ref, fetched_ref, *refs):
    extra_refs, (out_hbm, own_ref, out_ref, slots, sems) = refs[:-5], refs[-5:]
    n_lists, _, width = fetched_ref.shape
    rows = n_lists * kept
    returned = fetched_ref[:, :kept, :].reshape(rows, width)
    count = out_ref.shape[0]
    probe = jnp.transpose(known_ref[:, :count])[:, 1:2].astype(jnp.int32)
    user = lax.broadcasted_iota(jnp.int32, (count, 1), 0) // (count // user_dev)
    sends = []
    for piece in range(pieces):
        wanted = probe * kept + piece * user_dev + user
        span = pl.ds(piece * width, width)
        out_ref[:, span] = jnp.dot(picks(wanted, rows), returned, preferred_element_type=jnp.float32).astype(
            jnp.bfloat16
        )
        sends.append(pltpu.make_async_copy(out_ref.at[:, span], out_hbm.at[:, span], sems.at[piece]))
        sends[-1].start()
    placed(col_ref[0], known_ref, slots, fetched_ref, extra_refs, own_ref)
    for send in sends:
        send.wait()


SMEM = pl.BlockSpec(memory_space=pltpu.SMEM)
VMEM = pl.BlockSpec(memory_space=pltpu.VMEM)
HBM = pl.BlockSpec(memory_space=pltpu.HBM)
PARAMS = pltpu.CompilerParams(vmem_limit_bytes=VMEM_BYTES)


def exchange(value):
    return lax.all_to_all(value, "lists", split_axis=0, concat_axis=0, tiled=True)


def shards(
    user_vectors,
    probe_lists,
    list_items,
    candidate_ids,
    history,
    history_lengths,
    query_weight,
    key_value_weight,
    out_weight,
):
    n_lists = lax.axis_size("lists")
    n_users = lax.axis_size("users")
    _, items_loc, width = list_items.shape
    user_dev, probes = probe_lists.shape
    _, cands = candidate_ids.shape
    bf16 = jnp.bfloat16
    cap = max(2, 3 * cands // (n_lists * n_users))
    cap = round_up(cap, ROW_TILE)
    kept = round_up(items_loc // width * user_dev, ROW_TILE)
    share = cands // n_users
    pieces = items_loc // width
    digits = 1
    while BASE**digits < n_lists * n_users * items_loc:
        digits += 1
    pack_rows = round_up((user_dev + digits) * (width // LANES), 8)
    line = lax.axis_index("lists").astype(jnp.int32)
    col = lax.axis_index("users").astype(jnp.int32)
    col_arg = col.reshape(1)
    line_arg = line.reshape(1)
    base_arg = ((line * n_users + col) * items_loc).reshape(1)
    other_arg = ((line * n_users + n_users - 1 - col) * items_loc).reshape(1)
    spare = 8 if n_users == 2 and cap >= 48 else 0
    main = cap - spare
    block = main + kept

    flat_items = list_items.reshape(items_loc, width)
    pack = pl.pallas_call(
        functools.partial(pack_kernel, digits),
        out_shape=jax.ShapeDtypeStruct((n_lists, pack_rows, LANES), bf16),
        in_specs=[VMEM, VMEM],
        out_specs=VMEM,
        compiler_params=pltpu.CompilerParams(vmem_limit_bytes=ALL_VMEM_BYTES),
    )(candidate_ids, user_vectors)
    gathered = exchange(pack)
    gathered = gathered.reshape(n_lists * pack_rows, LANES)

    items = pl.pallas_call(
        items_kernel,
        out_shape=jax.ShapeDtypeStruct((items_loc, width), bf16),
        in_specs=[HBM],
        out_specs=VMEM,
        scratch_shapes=[pltpu.SemaphoreType.DMA((4,))],
        compiler_params=PARAMS,
    )(flat_items)
    gathered, items = lax.optimization_barrier((gathered, items))

    siblings = []
    if spare:
        siblings.append(lax.ppermute(flat_items, "users", [(0, 1), (1, 0)]))

    known, many = pl.pallas_call(
        functools.partial(known_kernel, n_lists, items_loc, n_users, user_dev, digits, main, spare, kept),
        out_shape=(
            jax.ShapeDtypeStruct((8, cands), jnp.float32),
            jax.ShapeDtypeStruct((1,), jnp.int32),
        ),
        in_specs=[SMEM, SMEM, VMEM, VMEM, VMEM],
        out_specs=(VMEM, SMEM),
        scratch_shapes=[pltpu.VMEM((n_lists * pack_rows, LANES), jnp.float32)],
        compiler_params=PARAMS,
    )(line_arg, col_arg, candidate_ids, probe_lists, gathered)

    extras = []
    if spare:

        def spill_apart():
            spill = pl.pallas_call(
                functools.partial(spill_kernel, n_lists, user_dev, digits, main),
                out_shape=jax.ShapeDtypeStruct((n_lists, spare, width), bf16),
                in_specs=[SMEM, VMEM, VMEM],
                out_specs=VMEM,
                scratch_shapes=[pltpu.VMEM((n_lists * pack_rows, LANES), jnp.float32)],
                compiler_params=PARAMS,
            )(base_arg, gathered, flat_items)
            spill = spill[jnp.arange(n_lists, dtype=jnp.int32) ^ line]
            blocks = [spill[:1]]
            for k in range(1, n_lists):
                blocks.append(lax.ppermute(spill[k : k + 1], "lists", [(i, i ^ k) for i in range(n_lists)]))
            return jnp.concatenate(blocks, axis=0).reshape(n_lists * spare, width)

        came = lax.cond(many[0] > 0, spill_apart, lambda: jnp.zeros((n_lists * spare, width), bf16))
        extras.append(
            pl.pallas_call(
                stay_kernel,
                out_shape=jax.ShapeDtypeStruct(came.shape, bf16),
                in_specs=[VMEM],
                out_specs=VMEM,
                compiler_params=PARAMS,
            )(came)
        )

    events = history.reshape(-1, width)
    hist = [events]
    for shift in range(1, n_users):
        hist.append(lax.ppermute(events, "users", [(i, (i + shift) % n_users) for i in range(n_users)]))
    total_events = n_users * events.shape[0]
    keys, values, turned = pl.pallas_call(
        functools.partial(pairs_kernel, n_users),
        out_shape=(
            jax.ShapeDtypeStruct((HEADS, total_events, width // HEADS + ROW_TILE), bf16),
            jax.ShapeDtypeStruct((width, total_events), bf16),
            jax.ShapeDtypeStruct((width, width), bf16),
        ),
        in_specs=[SMEM, SMEM] + [VMEM] * (n_users + 2),
        out_specs=(VMEM, VMEM, VMEM),
        compiler_params=PARAMS,
    )(col_arg, history_lengths, *hist, key_value_weight, query_weight)

    step = max(1, 288 // main)
    answers = pl.pallas_call(
        functools.partial(owner_kernel, n_lists, user_dev, digits, main, spare, width ** (-0.5)),
        out_shape=jax.ShapeDtypeStruct((n_lists, block, width), bf16),
        in_specs=[SMEM, SMEM, VMEM, VMEM] + [pl.BlockSpec(memory_space=pl.ANY)] * len(siblings),
        out_specs=pl.BlockSpec(memory_space=pl.ANY),
        scratch_shapes=[
            pltpu.VMEM((n_lists * pack_rows, LANES), jnp.float32),
            pltpu.VMEM((n_lists, block, width), bf16),
            pltpu.SemaphoreType.DMA((-(-n_lists // step),)),
        ]
        + [pltpu.VMEM((items_loc, width), bf16), pltpu.SemaphoreType.DMA((4,))] * len(siblings),
        compiler_params=PARAMS,
    )(base_arg, other_arg, gathered, items, *siblings)
    fetched = exchange(answers)

    fetched, known, extras, keys, values, turned = lax.optimization_barrier(
        (fetched, known, extras, keys, values, turned)
    )

    sent = []
    if n_users > 1:
        sent = pl.pallas_call(
            functools.partial(place_kernel, n_users),
            out_shape=tuple(jax.ShapeDtypeStruct((share, width), bf16) for _ in range(n_users - 1)),
            in_specs=[SMEM, VMEM, VMEM] + [VMEM] * len(extras),
            out_specs=tuple(VMEM for _ in range(n_users - 1)),
            scratch_shapes=[pltpu.VMEM((cands, 8), jnp.float32)],
            compiler_params=PARAMS,
        )(col_arg, known, fetched, *extras)
    parts = []
    for shift in range(1, n_users):
        parts.append(
            lax.ppermute(sent[shift - 1], "users", [(i, (i + shift) % n_users) for i in range(n_users)])
        )

    list_scores, own = pl.pallas_call(
        functools.partial(expand_kernel, user_dev, pieces, kept),
        out_shape=(
            jax.ShapeDtypeStruct((user_dev * probes, items_loc), bf16),
            jax.ShapeDtypeStruct((share, width), bf16),
        ),
        in_specs=[SMEM, VMEM, VMEM] + [VMEM] * len(extras),
        out_specs=(pl.BlockSpec(memory_space=pl.ANY), VMEM),
        scratch_shapes=[
            pltpu.VMEM((user_dev * probes, items_loc), bf16),
            pltpu.VMEM((cands, 8), jnp.float32),
            pltpu.SemaphoreType.DMA((pieces,)),
        ],
        compiler_params=PARAMS,
    )(col_arg, known, fetched, *extras)
    ranked = pl.pallas_call(
        functools.partial(attend_kernel, n_users),
        out_shape=jax.ShapeDtypeStruct((share, width), bf16),
        in_specs=[VMEM] * (n_users + 4),
        out_specs=VMEM,
        compiler_params=PARAMS,
    )(own, *parts, keys, values, turned, out_weight)
    return (list_scores.reshape(user_dev, probes, items_loc), ranked.reshape(1, share, width))


def solution(mesh):
    placed = (
        P("lists", None),
        P("lists", None),
        P("lists", "users", None),
        P("lists", None),
        P("lists", "users", None),
        P("lists"),
        P(),
        P(),
        P(),
    )
    return jax.shard_map(
        shards,
        mesh=mesh,
        in_specs=placed,
        out_specs=(P("lists", None, "users"), P("lists", "users", None)),
        check_vma=False,
    )
```

```python
import functools

import jax
import jax.numpy as jnp
from jax import lax
from jax.experimental import pallas as pl
from jax.experimental.pallas import tpu as pltpu
from jax.sharding import PartitionSpec as P

HEADS = 8
BASE = 256
LANES = 128
ROW_TILE = 16
VMEM_BYTES = 28 * 1024 * 1024
ALL_VMEM_BYTES = 62 * 1024 * 1024


def round_up(value, step):
    return (value + step - 1) // step * step


def picks(index, count):
    place = lax.broadcasted_iota(jnp.int32, (index.shape[0], count), 1).astype(jnp.int16)
    one, zero = jnp.bfloat16(1.0), jnp.bfloat16(0.0)
    return jnp.where(index.astype(jnp.int16) == place, one, zero)


def pack_kernel(digits, ids_ref, vectors_ref, pack_ref):
    width = vectors_ref.shape[1]
    vectors = vectors_ref[...].astype(jnp.float32)
    ids = ids_ref[...]
    spans = [slice(start, start + LANES) for start in range(0, width, LANES)]
    rows = [vectors[:, span] for span in spans]
    for digit in range(digits):
        value = ((ids >> (8 * digit)) & (BASE - 1)).astype(jnp.float32)
        rows += [value[:, span] for span in spans]
    count = sum(row.shape[0] for row in rows)
    if pack_ref.shape[1] > count:
        rows.append(jnp.zeros((pack_ref.shape[1] - count, LANES), jnp.float32))
    pack_ref[...] = jnp.broadcast_to(jnp.concatenate(rows, axis=0).astype(jnp.bfloat16)[None], pack_ref.shape)


def earlier(count):
    row = lax.broadcasted_iota(jnp.int32, (count, count), 0)
    column = lax.broadcasted_iota(jnp.int32, (count, count), 1)
    return jnp.where(row < column, 1.0, 0.0).astype(jnp.bfloat16)


def unpack(wide, n_lists, user_dev, digits, spans):
    pack_rows = wide.shape[0] // n_lists

    def line(number):
        return wide[pl.ds(number, n_lists, stride=pack_rows), :]

    vectors = jnp.concatenate(
        [
            jnp.concatenate([line(span * user_dev + u) for span in range(spans)], axis=1)
            for u in range(user_dev)
        ],
        axis=0,
    )
    ids = []
    for span in range(spans):
        value = line(user_dev * spans + span)
        for digit in range(1, digits):
            value = value + line((user_dev + digit) * spans + span) * float(BASE**digit)
        ids.append(value)
    return vectors, ids


def asked(ids, base, items_loc, first, count):
    n_lists = ids[0].shape[0]
    local = jnp.concatenate([part - base for part in ids], axis=0)
    mine = (local >= 0.0) & (local < items_loc)
    hot = jnp.where(mine, 1.0, 0.0)
    rank = jnp.dot(hot.astype(jnp.bfloat16), earlier(LANES), preferred_element_type=jnp.float32)
    totals = jnp.sum(hot, axis=1, keepdims=True)
    before = jnp.zeros((n_lists, 1), jnp.float32)
    ranks, locals_ = [], []
    for span in range(len(ids)):
        rows = slice(span * n_lists, (span + 1) * n_lists)
        ranks.append(jnp.where(mine[rows], rank[rows] + before, -1.0))
        locals_.append(local[rows] + 1.0)
        before = before + totals[rows]
    rank, local = jnp.concatenate(ranks, axis=1), jnp.concatenate(locals_, axis=1)
    place = (lax.broadcasted_iota(jnp.int32, (count, rank.shape[1]), 0) + first).astype(jnp.float32)
    index = []
    for r in range(n_lists):
        picked = jnp.where(rank[r : r + 1] == place, local[r : r + 1], 0.0)
        index.append(jnp.sum(picked, axis=1, keepdims=True).astype(jnp.int32) - 1)
    return index, before


def items_kernel(items_hbm, items_ref, sems):
    part = items_ref.shape[0] // sems.shape[0]
    loads = []
    for p in range(sems.shape[0]):
        span = pl.ds(p * part, part)
        loads.append(pltpu.make_async_copy(items_hbm.at[span], items_ref.at[span], sems.at[p]))
        loads[-1].start()
    for load in loads:
        load.wait()


def crowded(ids, n_lists, items_loc, main, spare):
    bins = [part.astype(jnp.int32) // items_loc for part in ids]
    worst = jnp.zeros((n_lists, 1), jnp.float32)
    for owner in range(n_lists):
        count = []
        for c in range(2):
            hits = [jnp.where(part == owner * 2 + c, 1.0, 0.0) for part in bins]
            count.append(jnp.sum(sum(hits[1:], hits[0]), axis=1, keepdims=True))
        for one, other in ((0, 1), (1, 0)):
            clash = (count[one] > float(main - spare)) & (count[other] > float(main))
            worst = jnp.maximum(worst, jnp.where(clash, 1.0, 0.0))
    return jnp.max(worst)


def known_kernel(
    n_lists, items_loc, n_users, user_dev, digits, main, spare, kept, *refs
):
    line_ref, col_ref, ids_ref, probes_ref, gathered_ref, known_ref, many_ref, copy_ref, wide = refs
    copy_ref[...] = gathered_ref[...]
    block = kept + main
    ids = ids_ref[...]
    cands = ids.shape[1]
    bins = ids // items_loc
    mine = bins % n_users == col_ref[0]
    owner = bins // n_users
    lists = lax.broadcasted_iota(jnp.int32, (n_lists * n_users, cands), 0)
    hot = jnp.where(lists == bins, 1.0, 0.0)
    before = jnp.dot(hot.astype(jnp.bfloat16), earlier(cands), preferred_element_type=jnp.float32)
    rank = jnp.sum(before * hot, axis=0, keepdims=True)
    slot = owner.astype(jnp.float32) * block + kept + rank
    if spare:
        wide[...] = gathered_ref[...].astype(jnp.float32)
        _, asked_ids = unpack(wide, n_lists, user_dev, digits, cands // LANES)
        many = crowded(asked_ids, n_lists, items_loc, main, spare)
        many_ref[0] = many.astype(jnp.int32)
        apart = n_lists * block + (owner ^ line_ref[0]).astype(jnp.float32) * spare + rank - main
        apart = jnp.where(many > 0.5, apart, -1.0)
        there = jnp.where((rank >= float(main)) & (many < 0.5), slot - spare, -1.0)
        slot = jnp.where(mine, jnp.where(rank < float(main), slot, apart), there)
    else:
        many_ref[0] = jnp.int32(0)
        slot = jnp.where(mine, slot, -1.0)
    probes = probes_ref[...].astype(jnp.float32)
    flat = jnp.concatenate([probes[u : u + 1] for u in range(probes.shape[0])], axis=1)
    if flat.shape[1] < cands:
        flat = jnp.concatenate([flat, jnp.zeros((1, cands - flat.shape[1]), jnp.float32)], axis=1)
    row = lax.broadcasted_iota(jnp.int32, known_ref.shape, 0)
    known_ref[...] = jnp.where(row == 0, slot, flat)


def pairs_kernel(n_parts, col_ref, length_ref, *refs):
    parts, (weight_ref, query_ref, keys_ref, values_ref, turned_ref) = refs[:n_parts], refs[n_parts:]
    history = jnp.concatenate([part[...] for part in parts], axis=0)
    pairs = jnp.dot(history, weight_ref[...], preferred_element_type=jnp.float32)
    heads, events, features = keys_ref.shape
    head_dim = features - ROW_TILE
    width = heads * head_dim
    hist_dev = events // n_parts
    event = lax.broadcasted_iota(jnp.int32, (events, ROW_TILE), 0)
    feature = lax.broadcasted_iota(jnp.int32, (events, ROW_TILE), 1)
    position = (col_ref[0] - event // hist_dev + n_parts) % n_parts * hist_dev + event % hist_dev
    mask = jnp.where((position >= length_ref[0]) & (feature == 0), -1e30, 0.0)
    for h in range(heads):
        keys = pairs[:, h * head_dim : (h + 1) * head_dim]
        keys_ref[h] = jnp.concatenate([keys, mask], axis=1).astype(jnp.bfloat16)
    values_ref[...] = jnp.transpose(pairs[:, width:]).astype(jnp.bfloat16)
    turned_ref[...] = jnp.transpose(query_ref[...].astype(jnp.float32)).astype(jnp.bfloat16)


def owner_kernel(
    n_lists, user_dev, digits, main, spare, scale, base_ref, other_ref, gathered_ref, items_ref, *refs
):
    loads = []
    if spare:
        sibling_hbm, out_hbm, wide, out_ref, out_sems, sibling_ref, in_sems = refs
        part = sibling_ref.shape[0] // in_sems.shape[0]
        for p in range(in_sems.shape[0]):
            span = pl.ds(p * part, part)
            loads.append(pltpu.make_async_copy(sibling_hbm.at[span], sibling_ref.at[span], in_sems.at[p]))
            loads[-1].start()
    else:
        out_hbm, wide, out_ref, out_sems = refs
    items_loc, width = items_ref.shape
    wide[...] = gathered_ref[...].astype(jnp.float32)
    vectors, ids = unpack(wide, n_lists, user_dev, digits, width // LANES)
    index, own = asked(ids, base_ref[0].astype(jnp.float32), items_loc, 0, main)
    scores = lax.dot_general(
        vectors.astype(jnp.bfloat16),
        items_ref[...],
        (((1,), (1,)), ((), ())),
        preferred_element_type=jnp.float32,
    )
    scores = (scores * scale).astype(jnp.bfloat16)
    pieces = items_loc // width
    stacked = jnp.concatenate(
        [scores[:, piece * width : (piece + 1) * width] for piece in range(pieces)], axis=0
    )
    kept = out_ref.shape[1] - main
    entry = lax.broadcasted_iota(jnp.int32, (n_lists * kept, 1), 0)
    wanted = jnp.where(entry % kept < pieces * user_dev, entry % kept * n_lists + entry // kept, -1)
    spread = jnp.dot(
        picks(wanted, stacked.shape[0]), stacked, preferred_element_type=jnp.float32
    ).astype(jnp.bfloat16)
    out_ref[:, :kept, :] = spread.reshape(n_lists, kept, width)
    if spare:
        over, _ = asked(ids, other_ref[0].astype(jnp.float32), items_loc, main, spare)
        over = [jnp.where(own[r : r + 1] > float(main - spare), -1, over[r]) for r in range(n_lists)]
    step = max(1, 288 // main)
    sends = []
    for number, first in enumerate(range(0, n_lists, step)):
        last = min(n_lists, first + step)
        rows = jnp.dot(
            picks(jnp.concatenate(index[first:last], axis=0), items_loc),
            items_ref[...],
            preferred_element_type=jnp.float32,
        )
        if spare and first == 0:
            for load in loads:
                load.wait()
            shared = jnp.dot(
                picks(jnp.concatenate(over, axis=0), items_loc),
                sibling_ref[...],
                preferred_element_type=jnp.float32,
            )
        for r in range(first, last):
            mine = rows[(r - first) * main : (r - first + 1) * main]
            out_ref[r, kept : kept + main - spare, :] = mine[: main - spare].astype(jnp.bfloat16)
            if spare:
                both = mine[main - spare :] + shared[r * spare : (r + 1) * spare]
                out_ref[r, kept + main - spare :, :] = both.astype(jnp.bfloat16)
        send = pltpu.make_async_copy(out_ref.at[first:last], out_hbm.at[first:last], out_sems.at[number])
        send.start()
        sends.append(send)
    for send in sends:
        send.wait()


def spill_kernel(n_lists, user_dev, digits, main, base_ref, gathered_ref, items_ref, spill_ref, wide):
    items_loc, width = items_ref.shape
    spare = spill_ref.shape[1]
    wide[...] = gathered_ref[...].astype(jnp.float32)
    _, ids = unpack(wide, n_lists, user_dev, digits, width // LANES)
    index, _ = asked(ids, base_ref[0].astype(jnp.float32), items_loc, main, spare)
    rows = jnp.dot(
        picks(jnp.concatenate(index, axis=0), items_loc), items_ref[...], preferred_element_type=jnp.float32
    )
    spill_ref[...] = rows.astype(jnp.bfloat16).reshape(spill_ref.shape)


def stay_kernel(came_ref, here_ref):
    here_ref[...] = came_ref[...]


def placed(column, known_ref, slots, fetched_ref, extra_refs, out_ref):
    n_lists, block, width = fetched_ref.shape
    share = out_ref.shape[0]
    slots[...] = jnp.transpose(known_ref[...])
    start = pl.multiple_of(column * share, share)
    slot = slots[pl.ds(start, share), :][:, :1].astype(jnp.int32)
    rows = jnp.dot(
        picks(slot, n_lists * block),
        fetched_ref[...].reshape(n_lists * block, width),
        preferred_element_type=jnp.float32,
    )
    for ref in extra_refs:
        rows = rows + jnp.dot(
            picks(slot - n_lists * block, ref.shape[0]), ref[...], preferred_element_type=jnp.float32
        )
    out_ref[...] = rows.astype(jnp.bfloat16)


def place_kernel(n_users, col_ref, known_ref, fetched_ref, *refs):
    extra_refs, sent_refs, slots = refs[: -n_users], refs[-n_users:-1], refs[-1]
    for shift, ref in enumerate(sent_refs):
        placed((col_ref[0] + shift + 1) % n_users, known_ref, slots, fetched_ref, extra_refs, ref)


def attend_kernel(n_parts, *refs):
    parts, (keys_ref, values_ref, turned_ref, out_weight_ref, out_ref) = refs[:n_parts], refs[n_parts:]
    heads, events, features = keys_ref.shape
    head_dim = features - ROW_TILE
    rows = parts[0][...]
    for part in parts[1:]:
        rows = rows + part[...]
    queries = lax.dot_general(
        turned_ref[...], rows, (((1,), (1,)), ((), ())), preferred_element_type=jnp.float32
    )
    queries = (queries * head_dim ** (-0.5)).astype(jnp.bfloat16)
    feature = lax.broadcasted_iota(jnp.int32, (ROW_TILE, rows.shape[0]), 0)
    one = jnp.where(feature == 0, 1.0, 0.0).astype(jnp.bfloat16)

    def score(h):
        query = jnp.concatenate([queries[h * head_dim : (h + 1) * head_dim], one], axis=0)
        return jnp.dot(keys_ref[h], query, preferred_element_type=jnp.float32)

    ahead = [score(h) for h in range(min(2, heads))]
    mixed = []
    for h in range(heads):
        if h + 2 < heads:
            ahead.append(score(h + 2))
        exponentials = jnp.exp(ahead[h] - jnp.max(ahead[h], axis=0, keepdims=True))
        total = jnp.sum(exponentials, axis=0, keepdims=True)
        span = slice(h * head_dim, (h + 1) * head_dim)
        head = jnp.dot(values_ref[span, :], exponentials.astype(jnp.bfloat16), preferred_element_type=jnp.float32)
        mixed.append(head / total)
    attended = jnp.transpose(jnp.concatenate(mixed, axis=0)).astype(jnp.bfloat16)
    out_ref[...] = jnp.dot(attended, out_weight_ref[...], preferred_element_type=jnp.float32).astype(jnp.bfloat16)


def expand_kernel(user_dev, pieces, kept, col_ref, known_ref, fetched_ref, *refs):
    extra_refs, (out_hbm, own_ref, out_ref, slots, sems) = refs[:-5], refs[-5:]
    n_lists, _, width = fetched_ref.shape
    rows = n_lists * kept
    returned = fetched_ref[:, :kept, :].reshape(rows, width)
    count = out_ref.shape[0]
    probe = jnp.transpose(known_ref[:, :count])[:, 1:2].astype(jnp.int32)
    user = lax.broadcasted_iota(jnp.int32, (count, 1), 0) // (count // user_dev)
    sends = []
    for piece in range(pieces):
        wanted = probe * kept + piece * user_dev + user
        span = pl.ds(piece * width, width)
        out_ref[:, span] = jnp.dot(picks(wanted, rows), returned, preferred_element_type=jnp.float32).astype(
            jnp.bfloat16
        )
        sends.append(pltpu.make_async_copy(out_ref.at[:, span], out_hbm.at[:, span], sems.at[piece]))
        sends[-1].start()
    placed(col_ref[0], known_ref, slots, fetched_ref, extra_refs, own_ref)
    for send in sends:
        send.wait()


SMEM = pl.BlockSpec(memory_space=pltpu.SMEM)
VMEM = pl.BlockSpec(memory_space=pltpu.VMEM)
HBM = pl.BlockSpec(memory_space=pltpu.HBM)
PARAMS = pltpu.CompilerParams(vmem_limit_bytes=VMEM_BYTES)


def exchange(value):
    return lax.all_to_all(value, "lists", split_axis=0, concat_axis=0, tiled=True)


def shards(
    user_vectors,
    probe_lists,
    list_items,
    candidate_ids,
    history,
    history_lengths,
    query_weight,
    key_value_weight,
    out_weight,
):
    n_lists = lax.axis_size("lists")
    n_users = lax.axis_size("users")
    _, items_loc, width = list_items.shape
    user_dev, probes = probe_lists.shape
    _, cands = candidate_ids.shape
    bf16 = jnp.bfloat16
    cap = max(2, 3 * cands // (n_lists * n_users))
    cap = round_up(cap, ROW_TILE)
    kept = round_up(items_loc // width * user_dev, ROW_TILE)
    share = cands // n_users
    pieces = items_loc // width
    digits = 1
    while BASE**digits < n_lists * n_users * items_loc:
        digits += 1
    pack_rows = round_up((user_dev + digits) * (width // LANES), 8)
    line = lax.axis_index("lists").astype(jnp.int32)
    col = lax.axis_index("users").astype(jnp.int32)
    col_arg = col.reshape(1)
    line_arg = line.reshape(1)
    base_arg = ((line * n_users + col) * items_loc).reshape(1)
    other_arg = ((line * n_users + n_users - 1 - col) * items_loc).reshape(1)
    spare = 8 if n_users == 2 and cap >= 48 else 0
    main = cap - spare
    block = main + kept

    flat_items = list_items.reshape(items_loc, width)
    pack = pl.pallas_call(
        functools.partial(pack_kernel, digits),
        out_shape=jax.ShapeDtypeStruct((n_lists, pack_rows, LANES), bf16),
        in_specs=[VMEM, VMEM],
        out_specs=VMEM,
        compiler_params=pltpu.CompilerParams(vmem_limit_bytes=ALL_VMEM_BYTES),
    )(candidate_ids, user_vectors)
    gathered = exchange(pack)
    gathered = gathered.reshape(n_lists * pack_rows, LANES)

    items = pl.pallas_call(
        items_kernel,
        out_shape=jax.ShapeDtypeStruct((items_loc, width), bf16),
        in_specs=[HBM],
        out_specs=VMEM,
        scratch_shapes=[pltpu.SemaphoreType.DMA((4,))],
        compiler_params=PARAMS,
    )(flat_items)
    gathered, items = lax.optimization_barrier((gathered, items))

    siblings = []
    if spare:
        siblings.append(lax.ppermute(flat_items, "users", [(0, 1), (1, 0)]))

    known, many, gathered_copy = pl.pallas_call(
        functools.partial(known_kernel, n_lists, items_loc, n_users, user_dev, digits, main, spare, kept),
        out_shape=(
            jax.ShapeDtypeStruct((8, cands), jnp.float32),
            jax.ShapeDtypeStruct((1,), jnp.int32),
            jax.ShapeDtypeStruct(gathered.shape, bf16),
        ),
        in_specs=[SMEM, SMEM, VMEM, VMEM, VMEM],
        out_specs=(VMEM, SMEM, VMEM),
        scratch_shapes=[pltpu.VMEM((n_lists * pack_rows, LANES), jnp.float32)],
        compiler_params=PARAMS,
    )(line_arg, col_arg, candidate_ids, probe_lists, gathered)

    extras = []
    if spare:

        def spill_apart():
            spill = pl.pallas_call(
                functools.partial(spill_kernel, n_lists, user_dev, digits, main),
                out_shape=jax.ShapeDtypeStruct((n_lists, spare, width), bf16),
                in_specs=[SMEM, VMEM, VMEM],
                out_specs=VMEM,
                scratch_shapes=[pltpu.VMEM((n_lists * pack_rows, LANES), jnp.float32)],
                compiler_params=PARAMS,
            )(base_arg, gathered_copy, flat_items)
            spill = spill[jnp.arange(n_lists, dtype=jnp.int32) ^ line]
            blocks = [spill[:1]]
            for k in range(1, n_lists):
                blocks.append(lax.ppermute(spill[k : k + 1], "lists", [(i, i ^ k) for i in range(n_lists)]))
            return jnp.concatenate(blocks, axis=0).reshape(n_lists * spare, width)

        came = lax.cond(many[0] > 0, spill_apart, lambda: jnp.zeros((n_lists * spare, width), bf16))
        extras.append(
            pl.pallas_call(
                stay_kernel,
                out_shape=jax.ShapeDtypeStruct(came.shape, bf16),
                in_specs=[VMEM],
                out_specs=VMEM,
                compiler_params=PARAMS,
            )(came)
        )

    events = history.reshape(-1, width)
    hist = [events]
    for shift in range(1, n_users):
        hist.append(lax.ppermute(events, "users", [(i, (i + shift) % n_users) for i in range(n_users)]))
    total_events = n_users * events.shape[0]
    keys, values, turned = pl.pallas_call(
        functools.partial(pairs_kernel, n_users),
        out_shape=(
            jax.ShapeDtypeStruct((HEADS, total_events, width // HEADS + ROW_TILE), bf16),
            jax.ShapeDtypeStruct((width, total_events), bf16),
            jax.ShapeDtypeStruct((width, width), bf16),
        ),
        in_specs=[SMEM, SMEM] + [VMEM] * (n_users + 2),
        out_specs=(VMEM, VMEM, VMEM),
        compiler_params=PARAMS,
    )(col_arg, history_lengths, *hist, key_value_weight, query_weight)

    step = max(1, 288 // main)
    answers = pl.pallas_call(
        functools.partial(owner_kernel, n_lists, user_dev, digits, main, spare, width ** (-0.5)),
        out_shape=jax.ShapeDtypeStruct((n_lists, block, width), bf16),
        in_specs=[SMEM, SMEM, VMEM, VMEM] + [pl.BlockSpec(memory_space=pl.ANY)] * len(siblings),
        out_specs=pl.BlockSpec(memory_space=pl.ANY),
        scratch_shapes=[
            pltpu.VMEM((n_lists * pack_rows, LANES), jnp.float32),
            pltpu.VMEM((n_lists, block, width), bf16),
            pltpu.SemaphoreType.DMA((-(-n_lists // step),)),
        ]
        + [pltpu.VMEM((items_loc, width), bf16), pltpu.SemaphoreType.DMA((4,))] * len(siblings),
        compiler_params=PARAMS,
    )(base_arg, other_arg, gathered, items, *siblings)
    fetched = exchange(answers)

    fetched, known, extras, keys, values, turned = lax.optimization_barrier(
        (fetched, known, extras, keys, values, turned)
    )

    sent = []
    if n_users > 1:
        sent = pl.pallas_call(
            functools.partial(place_kernel, n_users),
            out_shape=tuple(jax.ShapeDtypeStruct((share, width), bf16) for _ in range(n_users - 1)),
            in_specs=[SMEM, VMEM, VMEM] + [VMEM] * len(extras),
            out_specs=tuple(VMEM for _ in range(n_users - 1)),
            scratch_shapes=[pltpu.VMEM((cands, 8), jnp.float32)],
            compiler_params=PARAMS,
        )(col_arg, known, fetched, *extras)
    parts = []
    for shift in range(1, n_users):
        parts.append(
            lax.ppermute(sent[shift - 1], "users", [(i, (i + shift) % n_users) for i in range(n_users)])
        )

    list_scores, own = pl.pallas_call(
        functools.partial(expand_kernel, user_dev, pieces, kept),
        out_shape=(
            jax.ShapeDtypeStruct((user_dev * probes, items_loc), bf16),
            jax.ShapeDtypeStruct((share, width), bf16),
        ),
        in_specs=[SMEM, VMEM, VMEM] + [VMEM] * len(extras),
        out_specs=(pl.BlockSpec(memory_space=pl.ANY), VMEM),
        scratch_shapes=[
            pltpu.VMEM((user_dev * probes, items_loc), bf16),
            pltpu.VMEM((cands, 8), jnp.float32),
            pltpu.SemaphoreType.DMA((pieces,)),
        ],
        compiler_params=PARAMS,
    )(col_arg, known, fetched, *extras)
    ranked = pl.pallas_call(
        functools.partial(attend_kernel, n_users),
        out_shape=jax.ShapeDtypeStruct((share, width), bf16),
        in_specs=[VMEM] * (n_users + 4),
        out_specs=VMEM,
        compiler_params=PARAMS,
    )(own, *parts, keys, values, turned, out_weight)
    return (list_scores.reshape(user_dev, probes, items_loc), ranked.reshape(1, share, width))


def solution(mesh):
    placed = (
        P("lists", None),
        P("lists", None),
        P("lists", "users", None),
        P("lists", None),
        P("lists", "users", None),
        P("lists"),
        P(),
        P(),
        P(),
    )
    return jax.shard_map(
        shards,
        mesh=mesh,
        in_specs=placed,
        out_specs=(P("lists", None, "users"), P("lists", "users", None)),
        check_vma=False,
    )
```

```python
import functools

import jax
import jax.numpy as jnp
from jax import lax
from jax.experimental import pallas as pl
from jax.experimental.pallas import tpu as pltpu
from jax.sharding import PartitionSpec as P

HEADS = 8
BASE = 256
LANES = 128
ROW_TILE = 16
VMEM_BYTES = 28 * 1024 * 1024
ALL_VMEM_BYTES = 62 * 1024 * 1024


def round_up(value, step):
    return (value + step - 1) // step * step


def picks(index, count):
    place = lax.broadcasted_iota(jnp.int32, (index.shape[0], count), 1).astype(jnp.int16)
    one, zero = jnp.bfloat16(1.0), jnp.bfloat16(0.0)
    return jnp.where(index.astype(jnp.int16) == place, one, zero)


def pack_kernel(digits, ids_ref, vectors_ref, pack_ref):
    width = vectors_ref.shape[1]
    vectors = vectors_ref[...].astype(jnp.float32)
    ids = ids_ref[...]
    spans = [slice(start, start + LANES) for start in range(0, width, LANES)]
    rows = [vectors[:, span] for span in spans]
    for digit in range(digits):
        value = ((ids >> (8 * digit)) & (BASE - 1)).astype(jnp.float32)
        rows += [value[:, span] for span in spans]
    count = sum(row.shape[0] for row in rows)
    if pack_ref.shape[1] > count:
        rows.append(jnp.zeros((pack_ref.shape[1] - count, LANES), jnp.float32))
    pack_ref[...] = jnp.broadcast_to(jnp.concatenate(rows, axis=0).astype(jnp.bfloat16)[None], pack_ref.shape)


def earlier(count):
    row = lax.broadcasted_iota(jnp.int32, (count, count), 0)
    column = lax.broadcasted_iota(jnp.int32, (count, count), 1)
    return jnp.where(row < column, 1.0, 0.0).astype(jnp.bfloat16)


def unpack(wide, n_lists, user_dev, digits, spans):
    pack_rows = wide.shape[0] // n_lists

    def line(number):
        return wide[pl.ds(number, n_lists, stride=pack_rows), :]

    vectors = jnp.concatenate(
        [
            jnp.concatenate([line(span * user_dev + u) for span in range(spans)], axis=1)
            for u in range(user_dev)
        ],
        axis=0,
    )
    ids = []
    for span in range(spans):
        value = line(user_dev * spans + span)
        for digit in range(1, digits):
            value = value + line((user_dev + digit) * spans + span) * float(BASE**digit)
        ids.append(value)
    return vectors, ids


def asked(ids, base, items_loc, first, count):
    n_lists = ids[0].shape[0]
    local = jnp.concatenate([part - base for part in ids], axis=0)
    mine = (local >= 0.0) & (local < items_loc)
    hot = jnp.where(mine, 1.0, 0.0)
    rank = jnp.dot(hot.astype(jnp.bfloat16), earlier(LANES), preferred_element_type=jnp.float32)
    totals = jnp.sum(hot, axis=1, keepdims=True)
    before = jnp.zeros((n_lists, 1), jnp.float32)
    ranks, locals_ = [], []
    for span in range(len(ids)):
        rows = slice(span * n_lists, (span + 1) * n_lists)
        ranks.append(jnp.where(mine[rows], rank[rows] + before, -1.0))
        locals_.append(local[rows] + 1.0)
        before = before + totals[rows]
    rank, local = jnp.concatenate(ranks, axis=1), jnp.concatenate(locals_, axis=1)
    place = (lax.broadcasted_iota(jnp.int32, (count, rank.shape[1]), 0) + first).astype(jnp.float32)
    index = []
    for r in range(n_lists):
        picked = jnp.where(rank[r : r + 1] == place, local[r : r + 1], 0.0)
        index.append(jnp.sum(picked, axis=1, keepdims=True).astype(jnp.int32) - 1)
    return index, before


def items_kernel(items_hbm, items_ref, sems):
    part = items_ref.shape[0] // sems.shape[0]
    loads = []
    for p in range(sems.shape[0]):
        span = pl.ds(p * part, part)
        loads.append(pltpu.make_async_copy(items_hbm.at[span], items_ref.at[span], sems.at[p]))
        loads[-1].start()
    for load in loads:
        load.wait()


def crowded(ids, n_lists, items_loc, main, spare):
    bins = [part.astype(jnp.int32) // items_loc for part in ids]
    worst = jnp.zeros((n_lists, 1), jnp.float32)
    for owner in range(n_lists):
        count = []
        for c in range(2):
            hits = [jnp.where(part == owner * 2 + c, 1.0, 0.0) for part in bins]
            count.append(jnp.sum(sum(hits[1:], hits[0]), axis=1, keepdims=True))
        for one, other in ((0, 1), (1, 0)):
            clash = (count[one] > float(main - spare)) & (count[other] > float(main))
            worst = jnp.maximum(worst, jnp.where(clash, 1.0, 0.0))
    return jnp.max(worst)


def known_kernel(
    n_lists, items_loc, n_users, user_dev, digits, main, spare, kept, *refs
):
    line_ref, col_ref, ids_ref, probes_ref, gathered_ref, known_ref, many_ref, copy_ref, wide = refs
    copy_ref[...] = gathered_ref[...]
    block = kept + main
    ids = ids_ref[...]
    cands = ids.shape[1]
    bins = ids // items_loc
    mine = bins % n_users == col_ref[0]
    owner = bins // n_users
    lists = lax.broadcasted_iota(jnp.int32, (n_lists * n_users, cands), 0)
    hot = jnp.where(lists == bins, 1.0, 0.0)
    before = jnp.dot(hot.astype(jnp.bfloat16), earlier(cands), preferred_element_type=jnp.float32)
    rank = jnp.sum(before * hot, axis=0, keepdims=True)
    slot = owner.astype(jnp.float32) * block + kept + rank
    if spare:
        wide[...] = gathered_ref[...].astype(jnp.float32)
        _, asked_ids = unpack(wide, n_lists, user_dev, digits, cands // LANES)
        many = crowded(asked_ids, n_lists, items_loc, main, spare)
        many_ref[0] = many.astype(jnp.int32)
        apart = n_lists * block + (owner ^ line_ref[0]).astype(jnp.float32) * spare + rank - main
        apart = jnp.where(many > 0.5, apart, -1.0)
        there = jnp.where((rank >= float(main)) & (many < 0.5), slot - spare, -1.0)
        slot = jnp.where(mine, jnp.where(rank < float(main), slot, apart), there)
    else:
        many_ref[0] = jnp.int32(0)
        slot = jnp.where(mine, slot, -1.0)
    probes = probes_ref[...].astype(jnp.float32)
    flat = jnp.concatenate([probes[u : u + 1] for u in range(probes.shape[0])], axis=1)
    if flat.shape[1] < cands:
        flat = jnp.concatenate([flat, jnp.zeros((1, cands - flat.shape[1]), jnp.float32)], axis=1)
    row = lax.broadcasted_iota(jnp.int32, known_ref.shape, 0)
    known_ref[...] = jnp.where(row == 0, slot, flat)


def pairs_kernel(n_parts, col_ref, length_ref, *refs):
    parts, (weight_ref, query_ref, keys_ref, values_ref, turned_ref) = refs[:n_parts], refs[n_parts:]
    history = jnp.concatenate([part[...] for part in parts], axis=0)
    pairs = jnp.dot(history, weight_ref[...], preferred_element_type=jnp.float32)
    heads, events, features = keys_ref.shape
    head_dim = features - ROW_TILE
    width = heads * head_dim
    hist_dev = events // n_parts
    event = lax.broadcasted_iota(jnp.int32, (events, ROW_TILE), 0)
    feature = lax.broadcasted_iota(jnp.int32, (events, ROW_TILE), 1)
    position = (col_ref[0] - event // hist_dev + n_parts) % n_parts * hist_dev + event % hist_dev
    mask = jnp.where((position >= length_ref[0]) & (feature == 0), -1e30, 0.0)
    for h in range(heads):
        keys = pairs[:, h * head_dim : (h + 1) * head_dim]
        keys_ref[h] = jnp.concatenate([keys, mask], axis=1).astype(jnp.bfloat16)
    values_ref[...] = jnp.transpose(pairs[:, width:]).astype(jnp.bfloat16)
    turned_ref[...] = jnp.transpose(query_ref[...].astype(jnp.float32)).astype(jnp.bfloat16)


def owner_kernel(
    n_lists, user_dev, digits, main, spare, scale, base_ref, other_ref, gathered_ref, items_ref, *refs
):
    loads = []
    if spare:
        sibling_hbm, out_hbm, wide, out_ref, out_sems, sibling_ref, in_sems = refs
        part = sibling_ref.shape[0] // in_sems.shape[0]
        for p in range(in_sems.shape[0]):
            span = pl.ds(p * part, part)
            loads.append(pltpu.make_async_copy(sibling_hbm.at[span], sibling_ref.at[span], in_sems.at[p]))
            loads[-1].start()
    else:
        out_hbm, wide, out_ref, out_sems = refs
    items_loc, width = items_ref.shape
    wide[...] = gathered_ref[...].astype(jnp.float32)
    vectors, ids = unpack(wide, n_lists, user_dev, digits, width // LANES)
    index, own = asked(ids, base_ref[0].astype(jnp.float32), items_loc, 0, main)
    scores = lax.dot_general(
        vectors.astype(jnp.bfloat16),
        items_ref[...],
        (((1,), (1,)), ((), ())),
        preferred_element_type=jnp.float32,
    )
    scores = (scores * scale).astype(jnp.bfloat16)
    pieces = items_loc // width
    stacked = jnp.concatenate(
        [scores[:, piece * width : (piece + 1) * width] for piece in range(pieces)], axis=0
    )
    kept = out_ref.shape[1] - main
    entry = lax.broadcasted_iota(jnp.int32, (n_lists * kept, 1), 0)
    wanted = jnp.where(entry % kept < pieces * user_dev, entry % kept * n_lists + entry // kept, -1)
    spread = jnp.dot(
        picks(wanted, stacked.shape[0]), stacked, preferred_element_type=jnp.float32
    ).astype(jnp.bfloat16)
    out_ref[:, :kept, :] = spread.reshape(n_lists, kept, width)
    if spare:
        over, _ = asked(ids, other_ref[0].astype(jnp.float32), items_loc, main, spare)
        over = [jnp.where(own[r : r + 1] > float(main - spare), -1, over[r]) for r in range(n_lists)]
    step = max(1, 288 // main)
    chunks = [(first, min(n_lists, first + step)) for first in range(0, n_lists, step)]
    sends = []

    def finish(number):
        first, last = chunks[number]
        if spare:
            for r in range(first, last):
                out_ref[r, kept + main - spare :, :] += shared[r * spare : (r + 1) * spare]
        send = pltpu.make_async_copy(out_ref.at[first:last], out_hbm.at[first:last], out_sems.at[number])
        send.start()
        sends.append(send)

    for number, (first, last) in enumerate(chunks):
        rows = jnp.dot(
            picks(jnp.concatenate(index[first:last], axis=0), items_loc),
            items_ref[...],
            preferred_element_type=jnp.float32,
        ).astype(jnp.bfloat16)
        for r in range(first, last):
            out_ref[r, kept:, :] = rows[(r - first) * main : (r - first + 1) * main]
        if number == max(0, len(chunks) - 2):
            if spare:
                for load in loads:
                    load.wait()
                shared = jnp.dot(
                    picks(jnp.concatenate(over, axis=0), items_loc),
                    sibling_ref[...],
                    preferred_element_type=jnp.float32,
                ).astype(jnp.bfloat16)
            for done in range(number + 1):
                finish(done)
        elif number == len(chunks) - 1:
            finish(number)
    for send in sends:
        send.wait()


def spill_kernel(n_lists, user_dev, digits, main, base_ref, gathered_ref, items_ref, spill_ref, wide):
    items_loc, width = items_ref.shape
    spare = spill_ref.shape[1]
    wide[...] = gathered_ref[...].astype(jnp.float32)
    _, ids = unpack(wide, n_lists, user_dev, digits, width // LANES)
    index, _ = asked(ids, base_ref[0].astype(jnp.float32), items_loc, main, spare)
    rows = jnp.dot(
        picks(jnp.concatenate(index, axis=0), items_loc), items_ref[...], preferred_element_type=jnp.float32
    )
    spill_ref[...] = rows.astype(jnp.bfloat16).reshape(spill_ref.shape)


def stay_kernel(came_ref, here_ref):
    here_ref[...] = came_ref[...]


def placed(column, known_ref, slots, fetched_ref, extra_refs, out_ref):
    n_lists, block, width = fetched_ref.shape
    share = out_ref.shape[0]
    slots[...] = jnp.transpose(known_ref[...])
    start = pl.multiple_of(column * share, share)
    slot = slots[pl.ds(start, share), :][:, :1].astype(jnp.int32)
    rows = jnp.dot(
        picks(slot, n_lists * block),
        fetched_ref[...].reshape(n_lists * block, width),
        preferred_element_type=jnp.float32,
    )
    for ref in extra_refs:
        rows = rows + jnp.dot(
            picks(slot - n_lists * block, ref.shape[0]), ref[...], preferred_element_type=jnp.float32
        )
    out_ref[...] = rows.astype(jnp.bfloat16)


def place_kernel(n_users, col_ref, known_ref, fetched_ref, *refs):
    extra_refs, sent_refs, slots = refs[: -n_users], refs[-n_users:-1], refs[-1]
    for shift, ref in enumerate(sent_refs):
        placed((col_ref[0] + shift + 1) % n_users, known_ref, slots, fetched_ref, extra_refs, ref)


def attend_kernel(n_parts, *refs):
    parts, (keys_ref, values_ref, turned_ref, out_weight_ref, out_ref) = refs[:n_parts], refs[n_parts:]
    heads, events, features = keys_ref.shape
    head_dim = features - ROW_TILE
    rows = parts[0][...]
    for part in parts[1:]:
        rows = rows + part[...]
    queries = lax.dot_general(
        turned_ref[...], rows, (((1,), (1,)), ((), ())), preferred_element_type=jnp.float32
    )
    queries = (queries * head_dim ** (-0.5)).astype(jnp.bfloat16)
    feature = lax.broadcasted_iota(jnp.int32, (ROW_TILE, rows.shape[0]), 0)
    one = jnp.where(feature == 0, 1.0, 0.0).astype(jnp.bfloat16)

    def score(h):
        query = jnp.concatenate([queries[h * head_dim : (h + 1) * head_dim], one], axis=0)
        return jnp.dot(keys_ref[h], query, preferred_element_type=jnp.float32)

    ahead = [score(h) for h in range(min(2, heads))]
    mixed = []
    for h in range(heads):
        if h + 2 < heads:
            ahead.append(score(h + 2))
        exponentials = jnp.exp(ahead[h] - jnp.max(ahead[h], axis=0, keepdims=True))
        total = jnp.sum(exponentials, axis=0, keepdims=True)
        span = slice(h * head_dim, (h + 1) * head_dim)
        head = jnp.dot(values_ref[span, :], exponentials.astype(jnp.bfloat16), preferred_element_type=jnp.float32)
        mixed.append(head / total)
    attended = jnp.transpose(jnp.concatenate(mixed, axis=0)).astype(jnp.bfloat16)
    out_ref[...] = jnp.dot(attended, out_weight_ref[...], preferred_element_type=jnp.float32).astype(jnp.bfloat16)


def expand_kernel(user_dev, pieces, kept, col_ref, known_ref, fetched_ref, *refs):
    extra_refs, (out_hbm, own_ref, out_ref, slots, sems) = refs[:-5], refs[-5:]
    n_lists, _, width = fetched_ref.shape
    rows = n_lists * kept
    returned = fetched_ref[:, :kept, :].reshape(rows, width)
    count = out_ref.shape[0]
    probe = jnp.transpose(known_ref[:, :count])[:, 1:2].astype(jnp.int32)
    user = lax.broadcasted_iota(jnp.int32, (count, 1), 0) // (count // user_dev)
    sends = []
    for piece in range(pieces):
        wanted = probe * kept + piece * user_dev + user
        span = pl.ds(piece * width, width)
        out_ref[:, span] = jnp.dot(picks(wanted, rows), returned, preferred_element_type=jnp.float32).astype(
            jnp.bfloat16
        )
        sends.append(pltpu.make_async_copy(out_ref.at[:, span], out_hbm.at[:, span], sems.at[piece]))
        sends[-1].start()
    placed(col_ref[0], known_ref, slots, fetched_ref, extra_refs, own_ref)
    for send in sends:
        send.wait()


SMEM = pl.BlockSpec(memory_space=pltpu.SMEM)
VMEM = pl.BlockSpec(memory_space=pltpu.VMEM)
HBM = pl.BlockSpec(memory_space=pltpu.HBM)
PARAMS = pltpu.CompilerParams(vmem_limit_bytes=VMEM_BYTES)


def exchange(value):
    return lax.all_to_all(value, "lists", split_axis=0, concat_axis=0, tiled=True)


def shards(
    user_vectors,
    probe_lists,
    list_items,
    candidate_ids,
    history,
    history_lengths,
    query_weight,
    key_value_weight,
    out_weight,
):
    n_lists = lax.axis_size("lists")
    n_users = lax.axis_size("users")
    _, items_loc, width = list_items.shape
    user_dev, probes = probe_lists.shape
    _, cands = candidate_ids.shape
    bf16 = jnp.bfloat16
    cap = max(2, 3 * cands // (n_lists * n_users))
    cap = round_up(cap, ROW_TILE)
    kept = round_up(items_loc // width * user_dev, ROW_TILE)
    share = cands // n_users
    pieces = items_loc // width
    digits = 1
    while BASE**digits < n_lists * n_users * items_loc:
        digits += 1
    pack_rows = round_up((user_dev + digits) * (width // LANES), 8)
    line = lax.axis_index("lists").astype(jnp.int32)
    col = lax.axis_index("users").astype(jnp.int32)
    col_arg = col.reshape(1)
    line_arg = line.reshape(1)
    base_arg = ((line * n_users + col) * items_loc).reshape(1)
    other_arg = ((line * n_users + n_users - 1 - col) * items_loc).reshape(1)
    spare = 8 if n_users == 2 and cap >= 48 else 0
    main = cap - spare
    block = main + kept

    flat_items = list_items.reshape(items_loc, width)
    pack = pl.pallas_call(
        functools.partial(pack_kernel, digits),
        out_shape=jax.ShapeDtypeStruct((n_lists, pack_rows, LANES), bf16),
        in_specs=[VMEM, VMEM],
        out_specs=VMEM,
        compiler_params=pltpu.CompilerParams(vmem_limit_bytes=ALL_VMEM_BYTES),
    )(candidate_ids, user_vectors)
    gathered = exchange(pack)
    gathered = gathered.reshape(n_lists * pack_rows, LANES)

    items = pl.pallas_call(
        items_kernel,
        out_shape=jax.ShapeDtypeStruct((items_loc, width), bf16),
        in_specs=[HBM],
        out_specs=VMEM,
        scratch_shapes=[pltpu.SemaphoreType.DMA((4,))],
        compiler_params=PARAMS,
    )(flat_items)
    gathered, items = lax.optimization_barrier((gathered, items))

    siblings = []
    if spare:
        siblings.append(lax.ppermute(flat_items, "users", [(0, 1), (1, 0)]))

    known, many, gathered_copy = pl.pallas_call(
        functools.partial(known_kernel, n_lists, items_loc, n_users, user_dev, digits, main, spare, kept),
        out_shape=(
            jax.ShapeDtypeStruct((8, cands), jnp.float32),
            jax.ShapeDtypeStruct((1,), jnp.int32),
            jax.ShapeDtypeStruct(gathered.shape, bf16),
        ),
        in_specs=[SMEM, SMEM, VMEM, VMEM, VMEM],
        out_specs=(VMEM, SMEM, VMEM),
        scratch_shapes=[pltpu.VMEM((n_lists * pack_rows, LANES), jnp.float32)],
        compiler_params=PARAMS,
    )(line_arg, col_arg, candidate_ids, probe_lists, gathered)

    extras = []
    if spare:

        def spill_apart():
            spill = pl.pallas_call(
                functools.partial(spill_kernel, n_lists, user_dev, digits, main),
                out_shape=jax.ShapeDtypeStruct((n_lists, spare, width), bf16),
                in_specs=[SMEM, VMEM, VMEM],
                out_specs=VMEM,
                scratch_shapes=[pltpu.VMEM((n_lists * pack_rows, LANES), jnp.float32)],
                compiler_params=PARAMS,
            )(base_arg, gathered_copy, flat_items)
            spill = spill[jnp.arange(n_lists, dtype=jnp.int32) ^ line]
            blocks = [spill[:1]]
            for k in range(1, n_lists):
                blocks.append(lax.ppermute(spill[k : k + 1], "lists", [(i, i ^ k) for i in range(n_lists)]))
            return jnp.concatenate(blocks, axis=0).reshape(n_lists * spare, width)

        came = lax.cond(many[0] > 0, spill_apart, lambda: jnp.zeros((n_lists * spare, width), bf16))
        extras.append(
            pl.pallas_call(
                stay_kernel,
                out_shape=jax.ShapeDtypeStruct(came.shape, bf16),
                in_specs=[VMEM],
                out_specs=VMEM,
                compiler_params=PARAMS,
            )(came)
        )

    events = history.reshape(-1, width)
    hist = [events]
    for shift in range(1, n_users):
        hist.append(lax.ppermute(events, "users", [(i, (i + shift) % n_users) for i in range(n_users)]))
    total_events = n_users * events.shape[0]
    keys, values, turned = pl.pallas_call(
        functools.partial(pairs_kernel, n_users),
        out_shape=(
            jax.ShapeDtypeStruct((HEADS, total_events, width // HEADS + ROW_TILE), bf16),
            jax.ShapeDtypeStruct((width, total_events), bf16),
            jax.ShapeDtypeStruct((width, width), bf16),
        ),
        in_specs=[SMEM, SMEM] + [VMEM] * (n_users + 2),
        out_specs=(VMEM, VMEM, VMEM),
        compiler_params=PARAMS,
    )(col_arg, history_lengths, *hist, key_value_weight, query_weight)

    step = max(1, 288 // main)
    answers = pl.pallas_call(
        functools.partial(owner_kernel, n_lists, user_dev, digits, main, spare, width ** (-0.5)),
        out_shape=jax.ShapeDtypeStruct((n_lists, block, width), bf16),
        in_specs=[SMEM, SMEM, VMEM, VMEM] + [pl.BlockSpec(memory_space=pl.ANY)] * len(siblings),
        out_specs=pl.BlockSpec(memory_space=pl.ANY),
        scratch_shapes=[
            pltpu.VMEM((n_lists * pack_rows, LANES), jnp.float32),
            pltpu.VMEM((n_lists, block, width), bf16),
            pltpu.SemaphoreType.DMA((-(-n_lists // step),)),
        ]
        + [pltpu.VMEM((items_loc, width), bf16), pltpu.SemaphoreType.DMA((4,))] * len(siblings),
        compiler_params=PARAMS,
    )(base_arg, other_arg, gathered, items, *siblings)
    fetched = exchange(answers)

    fetched, known, extras, keys, values, turned = lax.optimization_barrier(
        (fetched, known, extras, keys, values, turned)
    )

    sent = []
    if n_users > 1:
        sent = pl.pallas_call(
            functools.partial(place_kernel, n_users),
            out_shape=tuple(jax.ShapeDtypeStruct((share, width), bf16) for _ in range(n_users - 1)),
            in_specs=[SMEM, VMEM, VMEM] + [VMEM] * len(extras),
            out_specs=tuple(VMEM for _ in range(n_users - 1)),
            scratch_shapes=[pltpu.VMEM((cands, 8), jnp.float32)],
            compiler_params=PARAMS,
        )(col_arg, known, fetched, *extras)
    parts = []
    for shift in range(1, n_users):
        parts.append(
            lax.ppermute(sent[shift - 1], "users", [(i, (i + shift) % n_users) for i in range(n_users)])
        )

    list_scores, own = pl.pallas_call(
        functools.partial(expand_kernel, user_dev, pieces, kept),
        out_shape=(
            jax.ShapeDtypeStruct((user_dev * probes, items_loc), bf16),
            jax.ShapeDtypeStruct((share, width), bf16),
        ),
        in_specs=[SMEM, VMEM, VMEM] + [VMEM] * len(extras),
        out_specs=(pl.BlockSpec(memory_space=pl.ANY), VMEM),
        scratch_shapes=[
            pltpu.VMEM((user_dev * probes, items_loc), bf16),
            pltpu.VMEM((cands, 8), jnp.float32),
            pltpu.SemaphoreType.DMA((pieces,)),
        ],
        compiler_params=PARAMS,
    )(col_arg, known, fetched, *extras)
    ranked = pl.pallas_call(
        functools.partial(attend_kernel, n_users),
        out_shape=jax.ShapeDtypeStruct((share, width), bf16),
        in_specs=[VMEM] * (n_users + 4),
        out_specs=VMEM,
        compiler_params=PARAMS,
    )(own, *parts, keys, values, turned, out_weight)
    return (list_scores.reshape(user_dev, probes, items_loc), ranked.reshape(1, share, width))


def solution(mesh):
    placed = (
        P("lists", None),
        P("lists", None),
        P("lists", "users", None),
        P("lists", None),
        P("lists", "users", None),
        P("lists"),
        P(),
        P(),
        P(),
    )
    return jax.shard_map(
        shards,
        mesh=mesh,
        in_specs=placed,
        out_specs=(P("lists", None, "users"), P("lists", "users", None)),
        check_vma=False,
    )
```

```python
import functools

import jax
import jax.numpy as jnp
from jax import lax
from jax.experimental import pallas as pl
from jax.experimental.pallas import tpu as pltpu
from jax.sharding import PartitionSpec as P

HEADS = 8
BASE = 256
LANES = 128
ROW_TILE = 16
VMEM_BYTES = 28 * 1024 * 1024
ALL_VMEM_BYTES = 62 * 1024 * 1024


def round_up(value, step):
    return (value + step - 1) // step * step


def picks(index, count):
    place = lax.broadcasted_iota(jnp.int32, (index.shape[0], count), 1).astype(jnp.int16)
    one, zero = jnp.bfloat16(1.0), jnp.bfloat16(0.0)
    return jnp.where(index.astype(jnp.int16) == place, one, zero)


def pack_kernel(digits, ids_ref, vectors_ref, pack_ref):
    width = vectors_ref.shape[1]
    vectors = vectors_ref[...].astype(jnp.float32)
    ids = ids_ref[...]
    spans = [slice(start, start + LANES) for start in range(0, width, LANES)]
    rows = [vectors[:, span] for span in spans]
    for digit in range(digits):
        value = ((ids >> (8 * digit)) & (BASE - 1)).astype(jnp.float32)
        rows += [value[:, span] for span in spans]
    count = sum(row.shape[0] for row in rows)
    if pack_ref.shape[1] > count:
        rows.append(jnp.zeros((pack_ref.shape[1] - count, LANES), jnp.float32))
    pack_ref[...] = jnp.broadcast_to(jnp.concatenate(rows, axis=0).astype(jnp.bfloat16)[None], pack_ref.shape)


def earlier(count):
    row = lax.broadcasted_iota(jnp.int32, (count, count), 0)
    column = lax.broadcasted_iota(jnp.int32, (count, count), 1)
    return jnp.where(row < column, 1.0, 0.0).astype(jnp.bfloat16)


def unpack(wide, n_lists, user_dev, digits, spans):
    pack_rows = wide.shape[0] // n_lists

    def line(number):
        return wide[pl.ds(number, n_lists, stride=pack_rows), :]

    vectors = jnp.concatenate(
        [
            jnp.concatenate([line(span * user_dev + u) for span in range(spans)], axis=1)
            for u in range(user_dev)
        ],
        axis=0,
    )
    ids = []
    for span in range(spans):
        value = line(user_dev * spans + span)
        for digit in range(1, digits):
            value = value + line((user_dev + digit) * spans + span) * float(BASE**digit)
        ids.append(value)
    return vectors, ids


def asked(ids, base, items_loc, first, count):
    n_lists = ids[0].shape[0]
    local = jnp.concatenate([part - base for part in ids], axis=0)
    mine = (local >= 0.0) & (local < items_loc)
    hot = jnp.where(mine, 1.0, 0.0)
    rank = jnp.dot(hot.astype(jnp.bfloat16), earlier(LANES), preferred_element_type=jnp.float32)
    totals = jnp.sum(hot, axis=1, keepdims=True)
    before = jnp.zeros((n_lists, 1), jnp.float32)
    ranks, locals_ = [], []
    for span in range(len(ids)):
        rows = slice(span * n_lists, (span + 1) * n_lists)
        ranks.append(jnp.where(mine[rows], rank[rows] + before, -1.0))
        locals_.append(local[rows] + 1.0)
        before = before + totals[rows]
    rank, local = jnp.concatenate(ranks, axis=1), jnp.concatenate(locals_, axis=1)
    place = (lax.broadcasted_iota(jnp.int32, (count, rank.shape[1]), 0) + first).astype(jnp.float32)
    index = []
    for r in range(n_lists):
        picked = jnp.where(rank[r : r + 1] == place, local[r : r + 1], 0.0)
        index.append(jnp.sum(picked, axis=1, keepdims=True).astype(jnp.int32) - 1)
    return index, before


def items_kernel(items_hbm, items_ref, sems):
    part = items_ref.shape[0] // sems.shape[0]
    loads = []
    for p in range(sems.shape[0]):
        span = pl.ds(p * part, part)
        loads.append(pltpu.make_async_copy(items_hbm.at[span], items_ref.at[span], sems.at[p]))
        loads[-1].start()
    for load in loads:
        load.wait()


def crowded(ids, n_lists, items_loc, main, spare):
    bins = [part.astype(jnp.int32) // items_loc for part in ids]
    worst = jnp.zeros((n_lists, 1), jnp.float32)
    for owner in range(n_lists):
        count = []
        for c in range(2):
            hits = [jnp.where(part == owner * 2 + c, 1.0, 0.0) for part in bins]
            count.append(jnp.sum(sum(hits[1:], hits[0]), axis=1, keepdims=True))
        for one, other in ((0, 1), (1, 0)):
            clash = (count[one] > float(main - spare)) & (count[other] > float(main))
            worst = jnp.maximum(worst, jnp.where(clash, 1.0, 0.0))
    return jnp.max(worst)


def known_kernel(
    n_lists, items_loc, n_users, user_dev, digits, main, spare, kept, *refs
):
    line_ref, col_ref, ids_ref, probes_ref, gathered_ref, known_ref, many_ref, copy_ref, wide = refs
    copy_ref[...] = gathered_ref[...]
    block = kept + main
    ids = ids_ref[...]
    cands = ids.shape[1]
    bins = ids // items_loc
    mine = bins % n_users == col_ref[0]
    owner = bins // n_users
    lists = lax.broadcasted_iota(jnp.int32, (n_lists * n_users, cands), 0)
    hot = jnp.where(lists == bins, 1.0, 0.0)
    before = jnp.dot(hot.astype(jnp.bfloat16), earlier(cands), preferred_element_type=jnp.float32)
    rank = jnp.sum(before * hot, axis=0, keepdims=True)
    slot = owner.astype(jnp.float32) * block + kept + rank
    if spare:
        wide[...] = gathered_ref[...].astype(jnp.float32)
        _, asked_ids = unpack(wide, n_lists, user_dev, digits, cands // LANES)
        many = crowded(asked_ids, n_lists, items_loc, main, spare)
        many_ref[0] = many.astype(jnp.int32)
        apart = n_lists * block + (owner ^ line_ref[0]).astype(jnp.float32) * spare + rank - main
        apart = jnp.where(many > 0.5, apart, -1.0)
        there = jnp.where((rank >= float(main)) & (many < 0.5), slot - spare, -1.0)
        slot = jnp.where(mine, jnp.where(rank < float(main), slot, apart), there)
    else:
        many_ref[0] = jnp.int32(0)
        slot = jnp.where(mine, slot, -1.0)
    probes = probes_ref[...].astype(jnp.float32)
    flat = jnp.concatenate([probes[u : u + 1] for u in range(probes.shape[0])], axis=1)
    if flat.shape[1] < cands:
        flat = jnp.concatenate([flat, jnp.zeros((1, cands - flat.shape[1]), jnp.float32)], axis=1)
    row = lax.broadcasted_iota(jnp.int32, known_ref.shape, 0)
    known_ref[...] = jnp.where(row == 0, slot, flat)


def pairs_kernel(n_parts, col_ref, length_ref, *refs):
    parts, (weight_ref, query_ref, keys_ref, values_ref, turned_ref) = refs[:n_parts], refs[n_parts:]
    history = jnp.concatenate([part[...] for part in parts], axis=0)
    pairs = jnp.dot(history, weight_ref[...], preferred_element_type=jnp.float32)
    heads, events, features = keys_ref.shape
    head_dim = features - ROW_TILE
    width = heads * head_dim
    hist_dev = events // n_parts
    event = lax.broadcasted_iota(jnp.int32, (events, ROW_TILE), 0)
    feature = lax.broadcasted_iota(jnp.int32, (events, ROW_TILE), 1)
    position = (col_ref[0] - event // hist_dev + n_parts) % n_parts * hist_dev + event % hist_dev
    mask = jnp.where((position >= length_ref[0]) & (feature == 0), -1e30, 0.0)
    for h in range(heads):
        keys = pairs[:, h * head_dim : (h + 1) * head_dim]
        keys_ref[h] = jnp.concatenate([keys, mask], axis=1).astype(jnp.bfloat16)
    values_ref[...] = jnp.transpose(pairs[:, width:]).astype(jnp.bfloat16)
    turned_ref[...] = jnp.transpose(query_ref[...].astype(jnp.float32)).astype(jnp.bfloat16)


def owner_kernel(
    n_lists, user_dev, digits, main, spare, scale, base_ref, other_ref, gathered_ref, items_ref, *refs
):
    loads = []
    if spare:
        sibling_hbm, out_hbm, wide, out_ref, out_sems, sibling_ref, in_sems = refs
        part = sibling_ref.shape[0] // in_sems.shape[0]
        for p in range(in_sems.shape[0]):
            span = pl.ds(p * part, part)
            loads.append(pltpu.make_async_copy(sibling_hbm.at[span], sibling_ref.at[span], in_sems.at[p]))
            loads[-1].start()
    else:
        out_hbm, wide, out_ref, out_sems = refs
    items_loc, width = items_ref.shape
    wide[...] = gathered_ref[...].astype(jnp.float32)
    vectors, ids = unpack(wide, n_lists, user_dev, digits, width // LANES)
    index, own = asked(ids, base_ref[0].astype(jnp.float32), items_loc, 0, main)
    scores = lax.dot_general(
        vectors.astype(jnp.bfloat16),
        items_ref[...],
        (((1,), (1,)), ((), ())),
        preferred_element_type=jnp.float32,
    )
    scores = (scores * scale).astype(jnp.bfloat16)
    pieces = items_loc // width
    stacked = jnp.concatenate(
        [scores[:, piece * width : (piece + 1) * width] for piece in range(pieces)], axis=0
    )
    kept = out_ref.shape[1] - main
    entry = lax.broadcasted_iota(jnp.int32, (n_lists * kept, 1), 0)
    wanted = jnp.where(entry % kept < pieces * user_dev, entry % kept * n_lists + entry // kept, -1)
    spread = jnp.dot(
        picks(wanted, stacked.shape[0]), stacked, preferred_element_type=jnp.float32
    ).astype(jnp.bfloat16)
    out_ref[:, :kept, :] = spread.reshape(n_lists, kept, width)
    if spare:
        over, _ = asked(ids, other_ref[0].astype(jnp.float32), items_loc, main, spare)
        over = [jnp.where(own[r : r + 1] > float(main - spare), -1, over[r]) for r in range(n_lists)]
    step = max(1, 160 // main)
    chunks = [(first, min(n_lists, first + step)) for first in range(0, n_lists, step)]
    ready = max(0, len(chunks) // 2 - 1)
    sends = []

    def finish(number):
        first, last = chunks[number]
        if spare:
            for r in range(first, last):
                out_ref[r, kept + main - spare :, :] += shared[r * spare : (r + 1) * spare]
        send = pltpu.make_async_copy(out_ref.at[first:last], out_hbm.at[first:last], out_sems.at[number])
        send.start()
        sends.append(send)

    for number, (first, last) in enumerate(chunks):
        rows = jnp.dot(
            picks(jnp.concatenate(index[first:last], axis=0), items_loc),
            items_ref[...],
            preferred_element_type=jnp.float32,
        ).astype(jnp.bfloat16)
        for r in range(first, last):
            out_ref[r, kept:, :] = rows[(r - first) * main : (r - first + 1) * main]
        if number == ready:
            if spare:
                for load in loads:
                    load.wait()
                shared = jnp.dot(
                    picks(jnp.concatenate(over, axis=0), items_loc),
                    sibling_ref[...],
                    preferred_element_type=jnp.float32,
                ).astype(jnp.bfloat16)
            for done in range(number + 1):
                finish(done)
        elif number > ready:
            finish(number)
    for send in sends:
        send.wait()


def spill_kernel(n_lists, user_dev, digits, main, base_ref, gathered_ref, items_ref, spill_ref, wide):
    items_loc, width = items_ref.shape
    spare = spill_ref.shape[1]
    wide[...] = gathered_ref[...].astype(jnp.float32)
    _, ids = unpack(wide, n_lists, user_dev, digits, width // LANES)
    index, _ = asked(ids, base_ref[0].astype(jnp.float32), items_loc, main, spare)
    rows = jnp.dot(
        picks(jnp.concatenate(index, axis=0), items_loc), items_ref[...], preferred_element_type=jnp.float32
    )
    spill_ref[...] = rows.astype(jnp.bfloat16).reshape(spill_ref.shape)


def stay_kernel(came_ref, here_ref):
    here_ref[...] = came_ref[...]


def placed(column, known_ref, slots, fetched_ref, extra_refs, out_ref):
    n_lists, block, width = fetched_ref.shape
    share = out_ref.shape[0]
    slots[...] = jnp.transpose(known_ref[...])
    start = pl.multiple_of(column * share, share)
    slot = slots[pl.ds(start, share), :][:, :1].astype(jnp.int32)
    rows = jnp.dot(
        picks(slot, n_lists * block),
        fetched_ref[...].reshape(n_lists * block, width),
        preferred_element_type=jnp.float32,
    )
    for ref in extra_refs:
        rows = rows + jnp.dot(
            picks(slot - n_lists * block, ref.shape[0]), ref[...], preferred_element_type=jnp.float32
        )
    out_ref[...] = rows.astype(jnp.bfloat16)


def place_kernel(n_users, col_ref, known_ref, fetched_ref, *refs):
    extra_refs, sent_refs, slots = refs[: -n_users], refs[-n_users:-1], refs[-1]
    for shift, ref in enumerate(sent_refs):
        placed((col_ref[0] + shift + 1) % n_users, known_ref, slots, fetched_ref, extra_refs, ref)


def attend_kernel(n_parts, *refs):
    parts, (keys_ref, values_ref, turned_ref, out_weight_ref, out_ref) = refs[:n_parts], refs[n_parts:]
    heads, events, features = keys_ref.shape
    head_dim = features - ROW_TILE
    rows = parts[0][...]
    for part in parts[1:]:
        rows = rows + part[...]
    queries = lax.dot_general(
        turned_ref[...], rows, (((1,), (1,)), ((), ())), preferred_element_type=jnp.float32
    )
    queries = (queries * head_dim ** (-0.5)).astype(jnp.bfloat16)
    feature = lax.broadcasted_iota(jnp.int32, (ROW_TILE, rows.shape[0]), 0)
    one = jnp.where(feature == 0, 1.0, 0.0).astype(jnp.bfloat16)

    def score(h):
        query = jnp.concatenate([queries[h * head_dim : (h + 1) * head_dim], one], axis=0)
        return jnp.dot(keys_ref[h], query, preferred_element_type=jnp.float32)

    ahead = [score(h) for h in range(min(2, heads))]
    mixed = []
    for h in range(heads):
        if h + 2 < heads:
            ahead.append(score(h + 2))
        exponentials = jnp.exp(ahead[h] - jnp.max(ahead[h], axis=0, keepdims=True))
        total = jnp.sum(exponentials, axis=0, keepdims=True)
        span = slice(h * head_dim, (h + 1) * head_dim)
        head = jnp.dot(values_ref[span, :], exponentials.astype(jnp.bfloat16), preferred_element_type=jnp.float32)
        mixed.append(head / total)
    attended = jnp.transpose(jnp.concatenate(mixed, axis=0)).astype(jnp.bfloat16)
    out_ref[...] = jnp.dot(attended, out_weight_ref[...], preferred_element_type=jnp.float32).astype(jnp.bfloat16)


def expand_kernel(user_dev, pieces, kept, col_ref, known_ref, fetched_ref, *refs):
    extra_refs, (out_hbm, own_ref, out_ref, slots, sems) = refs[:-5], refs[-5:]
    n_lists, _, width = fetched_ref.shape
    rows = n_lists * kept
    returned = fetched_ref[:, :kept, :].reshape(rows, width)
    count = out_ref.shape[0]
    probe = jnp.transpose(known_ref[:, :count])[:, 1:2].astype(jnp.int32)
    user = lax.broadcasted_iota(jnp.int32, (count, 1), 0) // (count // user_dev)
    sends = []
    for piece in range(pieces):
        wanted = probe * kept + piece * user_dev + user
        span = pl.ds(piece * width, width)
        out_ref[:, span] = jnp.dot(picks(wanted, rows), returned, preferred_element_type=jnp.float32).astype(
            jnp.bfloat16
        )
        sends.append(pltpu.make_async_copy(out_ref.at[:, span], out_hbm.at[:, span], sems.at[piece]))
        sends[-1].start()
    placed(col_ref[0], known_ref, slots, fetched_ref, extra_refs, own_ref)
    for send in sends:
        send.wait()


SMEM = pl.BlockSpec(memory_space=pltpu.SMEM)
VMEM = pl.BlockSpec(memory_space=pltpu.VMEM)
HBM = pl.BlockSpec(memory_space=pltpu.HBM)
PARAMS = pltpu.CompilerParams(vmem_limit_bytes=VMEM_BYTES)


def exchange(value):
    return lax.all_to_all(value, "lists", split_axis=0, concat_axis=0, tiled=True)


def shards(
    user_vectors,
    probe_lists,
    list_items,
    candidate_ids,
    history,
    history_lengths,
    query_weight,
    key_value_weight,
    out_weight,
):
    n_lists = lax.axis_size("lists")
    n_users = lax.axis_size("users")
    _, items_loc, width = list_items.shape
    user_dev, probes = probe_lists.shape
    _, cands = candidate_ids.shape
    bf16 = jnp.bfloat16
    cap = max(2, 3 * cands // (n_lists * n_users))
    cap = round_up(cap, ROW_TILE)
    kept = round_up(items_loc // width * user_dev, ROW_TILE)
    share = cands // n_users
    pieces = items_loc // width
    digits = 1
    while BASE**digits < n_lists * n_users * items_loc:
        digits += 1
    pack_rows = round_up((user_dev + digits) * (width // LANES), 8)
    line = lax.axis_index("lists").astype(jnp.int32)
    col = lax.axis_index("users").astype(jnp.int32)
    col_arg = col.reshape(1)
    line_arg = line.reshape(1)
    base_arg = ((line * n_users + col) * items_loc).reshape(1)
    other_arg = ((line * n_users + n_users - 1 - col) * items_loc).reshape(1)
    spare = 8 if n_users == 2 and cap >= 48 else 0
    main = cap - spare
    block = main + kept

    flat_items = list_items.reshape(items_loc, width)
    pack = pl.pallas_call(
        functools.partial(pack_kernel, digits),
        out_shape=jax.ShapeDtypeStruct((n_lists, pack_rows, LANES), bf16),
        in_specs=[VMEM, VMEM],
        out_specs=VMEM,
        compiler_params=pltpu.CompilerParams(vmem_limit_bytes=ALL_VMEM_BYTES),
    )(candidate_ids, user_vectors)
    gathered = exchange(pack)
    gathered = gathered.reshape(n_lists * pack_rows, LANES)

    items = pl.pallas_call(
        items_kernel,
        out_shape=jax.ShapeDtypeStruct((items_loc, width), bf16),
        in_specs=[HBM],
        out_specs=VMEM,
        scratch_shapes=[pltpu.SemaphoreType.DMA((4,))],
        compiler_params=PARAMS,
    )(flat_items)
    gathered, items = lax.optimization_barrier((gathered, items))

    siblings = []
    if spare:
        siblings.append(lax.ppermute(flat_items, "users", [(0, 1), (1, 0)]))

    known, many, gathered_copy = pl.pallas_call(
        functools.partial(known_kernel, n_lists, items_loc, n_users, user_dev, digits, main, spare, kept),
        out_shape=(
            jax.ShapeDtypeStruct((8, cands), jnp.float32),
            jax.ShapeDtypeStruct((1,), jnp.int32),
            jax.ShapeDtypeStruct(gathered.shape, bf16),
        ),
        in_specs=[SMEM, SMEM, VMEM, VMEM, VMEM],
        out_specs=(VMEM, SMEM, VMEM),
        scratch_shapes=[pltpu.VMEM((n_lists * pack_rows, LANES), jnp.float32)],
        compiler_params=PARAMS,
    )(line_arg, col_arg, candidate_ids, probe_lists, gathered)

    extras = []
    if spare:

        def spill_apart():
            spill = pl.pallas_call(
                functools.partial(spill_kernel, n_lists, user_dev, digits, main),
                out_shape=jax.ShapeDtypeStruct((n_lists, spare, width), bf16),
                in_specs=[SMEM, VMEM, VMEM],
                out_specs=VMEM,
                scratch_shapes=[pltpu.VMEM((n_lists * pack_rows, LANES), jnp.float32)],
                compiler_params=PARAMS,
            )(base_arg, gathered_copy, flat_items)
            spill = spill[jnp.arange(n_lists, dtype=jnp.int32) ^ line]
            blocks = [spill[:1]]
            for k in range(1, n_lists):
                blocks.append(lax.ppermute(spill[k : k + 1], "lists", [(i, i ^ k) for i in range(n_lists)]))
            return jnp.concatenate(blocks, axis=0).reshape(n_lists * spare, width)

        came = lax.cond(many[0] > 0, spill_apart, lambda: jnp.zeros((n_lists * spare, width), bf16))
        extras.append(
            pl.pallas_call(
                stay_kernel,
                out_shape=jax.ShapeDtypeStruct(came.shape, bf16),
                in_specs=[VMEM],
                out_specs=VMEM,
                compiler_params=PARAMS,
            )(came)
        )

    events = history.reshape(-1, width)
    hist = [events]
    for shift in range(1, n_users):
        hist.append(lax.ppermute(events, "users", [(i, (i + shift) % n_users) for i in range(n_users)]))
    total_events = n_users * events.shape[0]
    keys, values, turned = pl.pallas_call(
        functools.partial(pairs_kernel, n_users),
        out_shape=(
            jax.ShapeDtypeStruct((HEADS, total_events, width // HEADS + ROW_TILE), bf16),
            jax.ShapeDtypeStruct((width, total_events), bf16),
            jax.ShapeDtypeStruct((width, width), bf16),
        ),
        in_specs=[SMEM, SMEM] + [VMEM] * (n_users + 2),
        out_specs=(VMEM, VMEM, VMEM),
        compiler_params=PARAMS,
    )(col_arg, history_lengths, *hist, key_value_weight, query_weight)

    step = max(1, 160 // main)
    answers = pl.pallas_call(
        functools.partial(owner_kernel, n_lists, user_dev, digits, main, spare, width ** (-0.5)),
        out_shape=jax.ShapeDtypeStruct((n_lists, block, width), bf16),
        in_specs=[SMEM, SMEM, VMEM, VMEM] + [pl.BlockSpec(memory_space=pl.ANY)] * len(siblings),
        out_specs=pl.BlockSpec(memory_space=pl.ANY),
        scratch_shapes=[
            pltpu.VMEM((n_lists * pack_rows, LANES), jnp.float32),
            pltpu.VMEM((n_lists, block, width), bf16),
            pltpu.SemaphoreType.DMA((-(-n_lists // step),)),
        ]
        + [pltpu.VMEM((items_loc, width), bf16), pltpu.SemaphoreType.DMA((4,))] * len(siblings),
        compiler_params=PARAMS,
    )(base_arg, other_arg, gathered, items, *siblings)
    fetched = exchange(answers)

    fetched, known, extras, keys, values, turned = lax.optimization_barrier(
        (fetched, known, extras, keys, values, turned)
    )

    sent = []
    if n_users > 1:
        sent = pl.pallas_call(
            functools.partial(place_kernel, n_users),
            out_shape=tuple(jax.ShapeDtypeStruct((share, width), bf16) for _ in range(n_users - 1)),
            in_specs=[SMEM, VMEM, VMEM] + [VMEM] * len(extras),
            out_specs=tuple(VMEM for _ in range(n_users - 1)),
            scratch_shapes=[pltpu.VMEM((cands, 8), jnp.float32)],
            compiler_params=PARAMS,
        )(col_arg, known, fetched, *extras)
    parts = []
    for shift in range(1, n_users):
        parts.append(
            lax.ppermute(sent[shift - 1], "users", [(i, (i + shift) % n_users) for i in range(n_users)])
        )

    list_scores, own = pl.pallas_call(
        functools.partial(expand_kernel, user_dev, pieces, kept),
        out_shape=(
            jax.ShapeDtypeStruct((user_dev * probes, items_loc), bf16),
            jax.ShapeDtypeStruct((share, width), bf16),
        ),
        in_specs=[SMEM, VMEM, VMEM] + [VMEM] * len(extras),
        out_specs=(pl.BlockSpec(memory_space=pl.ANY), VMEM),
        scratch_shapes=[
            pltpu.VMEM((user_dev * probes, items_loc), bf16),
            pltpu.VMEM((cands, 8), jnp.float32),
            pltpu.SemaphoreType.DMA((pieces,)),
        ],
        compiler_params=PARAMS,
    )(col_arg, known, fetched, *extras)
    ranked = pl.pallas_call(
        functools.partial(attend_kernel, n_users),
        out_shape=jax.ShapeDtypeStruct((share, width), bf16),
        in_specs=[VMEM] * (n_users + 4),
        out_specs=VMEM,
        compiler_params=PARAMS,
    )(own, *parts, keys, values, turned, out_weight)
    return (list_scores.reshape(user_dev, probes, items_loc), ranked.reshape(1, share, width))


def solution(mesh):
    placed = (
        P("lists", None),
        P("lists", None),
        P("lists", "users", None),
        P("lists", None),
        P("lists", "users", None),
        P("lists"),
        P(),
        P(),
        P(),
    )
    return jax.shard_map(
        shards,
        mesh=mesh,
        in_specs=placed,
        out_specs=(P("lists", None, "users"), P("lists", "users", None)),
        check_vma=False,
    )
```

```python
import functools

import jax
import jax.numpy as jnp
from jax import lax
from jax.experimental import pallas as pl
from jax.experimental.pallas import tpu as pltpu
from jax.sharding import PartitionSpec as P

HEADS = 8
BASE = 256
LANES = 128
ROW_TILE = 16
VMEM_BYTES = 28 * 1024 * 1024
ALL_VMEM_BYTES = 62 * 1024 * 1024


def round_up(value, step):
    return (value + step - 1) // step * step


def picks(index, count):
    place = lax.broadcasted_iota(jnp.int32, (index.shape[0], count), 1).astype(jnp.int16)
    one, zero = jnp.bfloat16(1.0), jnp.bfloat16(0.0)
    return jnp.where(index.astype(jnp.int16) == place, one, zero)


def pack_kernel(digits, ids_ref, vectors_ref, pack_ref):
    width = vectors_ref.shape[1]
    vectors = vectors_ref[...].astype(jnp.float32)
    ids = ids_ref[...]
    spans = [slice(start, start + LANES) for start in range(0, width, LANES)]
    rows = [vectors[:, span] for span in spans]
    for digit in range(digits):
        value = ((ids >> (8 * digit)) & (BASE - 1)).astype(jnp.float32)
        rows += [value[:, span] for span in spans]
    count = sum(row.shape[0] for row in rows)
    if pack_ref.shape[1] > count:
        rows.append(jnp.zeros((pack_ref.shape[1] - count, LANES), jnp.float32))
    pack_ref[...] = jnp.broadcast_to(jnp.concatenate(rows, axis=0).astype(jnp.bfloat16)[None], pack_ref.shape)


def earlier(count):
    row = lax.broadcasted_iota(jnp.int32, (count, count), 0)
    column = lax.broadcasted_iota(jnp.int32, (count, count), 1)
    return jnp.where(row < column, 1.0, 0.0).astype(jnp.bfloat16)


def unpack(wide, n_lists, user_dev, digits, spans):
    pack_rows = wide.shape[0] // n_lists

    def line(number):
        return wide[pl.ds(number, n_lists, stride=pack_rows), :]

    vectors = jnp.concatenate(
        [
            jnp.concatenate([line(span * user_dev + u) for span in range(spans)], axis=1)
            for u in range(user_dev)
        ],
        axis=0,
    )
    ids = []
    for span in range(spans):
        value = line(user_dev * spans + span)
        for digit in range(1, digits):
            value = value + line((user_dev + digit) * spans + span) * float(BASE**digit)
        ids.append(value)
    return vectors, ids


def asked(ids, base, items_loc, first, count):
    n_lists = ids[0].shape[0]
    local = jnp.concatenate([part - base for part in ids], axis=0)
    mine = (local >= 0.0) & (local < items_loc)
    hot = jnp.where(mine, 1.0, 0.0)
    rank = jnp.dot(hot.astype(jnp.bfloat16), earlier(LANES), preferred_element_type=jnp.float32)
    totals = jnp.sum(hot, axis=1, keepdims=True)
    before = jnp.zeros((n_lists, 1), jnp.float32)
    ranks, locals_ = [], []
    for span in range(len(ids)):
        rows = slice(span * n_lists, (span + 1) * n_lists)
        ranks.append(jnp.where(mine[rows], rank[rows] + before, -1.0))
        locals_.append(local[rows] + 1.0)
        before = before + totals[rows]
    rank, local = jnp.concatenate(ranks, axis=1), jnp.concatenate(locals_, axis=1)
    place = (lax.broadcasted_iota(jnp.int32, (count, rank.shape[1]), 0) + first).astype(jnp.float32)
    index = []
    for r in range(n_lists):
        picked = jnp.where(rank[r : r + 1] == place, local[r : r + 1], 0.0)
        index.append(jnp.sum(picked, axis=1, keepdims=True).astype(jnp.int32) - 1)
    return index, before


def items_kernel(items_hbm, items_ref, sems):
    part = items_ref.shape[0] // sems.shape[0]
    loads = []
    for p in range(sems.shape[0]):
        span = pl.ds(p * part, part)
        loads.append(pltpu.make_async_copy(items_hbm.at[span], items_ref.at[span], sems.at[p]))
        loads[-1].start()
    for load in loads:
        load.wait()


def crowded(ids, n_lists, items_loc, main, spare):
    bins = [part.astype(jnp.int32) // items_loc for part in ids]
    worst = jnp.zeros((n_lists, 1), jnp.float32)
    for owner in range(n_lists):
        count = []
        for c in range(2):
            hits = [jnp.where(part == owner * 2 + c, 1.0, 0.0) for part in bins]
            count.append(jnp.sum(sum(hits[1:], hits[0]), axis=1, keepdims=True))
        for one, other in ((0, 1), (1, 0)):
            clash = (count[one] > float(main - spare)) & (count[other] > float(main))
            worst = jnp.maximum(worst, jnp.where(clash, 1.0, 0.0))
    return jnp.max(worst)


def known_kernel(
    n_lists, items_loc, n_users, user_dev, digits, main, spare, kept, *refs
):
    line_ref, col_ref, ids_ref, probes_ref, gathered_ref, known_ref, many_ref, copy_ref, wide = refs
    copy_ref[...] = gathered_ref[...]
    block = kept + main
    ids = ids_ref[...]
    cands = ids.shape[1]
    bins = ids // items_loc
    mine = bins % n_users == col_ref[0]
    owner = bins // n_users
    lists = lax.broadcasted_iota(jnp.int32, (n_lists * n_users, cands), 0)
    hot = jnp.where(lists == bins, 1.0, 0.0)
    before = jnp.dot(hot.astype(jnp.bfloat16), earlier(cands), preferred_element_type=jnp.float32)
    rank = jnp.sum(before * hot, axis=0, keepdims=True)
    slot = owner.astype(jnp.float32) * block + kept + rank
    if spare:
        wide[...] = gathered_ref[...].astype(jnp.float32)
        _, asked_ids = unpack(wide, n_lists, user_dev, digits, cands // LANES)
        many = crowded(asked_ids, n_lists, items_loc, main, spare)
        many_ref[0] = many.astype(jnp.int32)
        apart = n_lists * block + (owner ^ line_ref[0]).astype(jnp.float32) * spare + rank - main
        apart = jnp.where(many > 0.5, apart, -1.0)
        there = jnp.where((rank >= float(main)) & (many < 0.5), slot - spare, -1.0)
        slot = jnp.where(mine, jnp.where(rank < float(main), slot, apart), there)
    else:
        many_ref[0] = jnp.int32(0)
        slot = jnp.where(mine, slot, -1.0)
    probes = probes_ref[...].astype(jnp.float32)
    flat = jnp.concatenate([probes[u : u + 1] for u in range(probes.shape[0])], axis=1)
    if flat.shape[1] < cands:
        flat = jnp.concatenate([flat, jnp.zeros((1, cands - flat.shape[1]), jnp.float32)], axis=1)
    row = lax.broadcasted_iota(jnp.int32, known_ref.shape, 0)
    known_ref[...] = jnp.where(row == 0, slot, flat)


def pairs_kernel(n_parts, col_ref, length_ref, *refs):
    parts, (weight_ref, query_ref, keys_ref, values_ref, turned_ref) = refs[:n_parts], refs[n_parts:]
    history = jnp.concatenate([part[...] for part in parts], axis=0)
    pairs = jnp.dot(history, weight_ref[...], preferred_element_type=jnp.float32)
    heads, events, features = keys_ref.shape
    head_dim = features - ROW_TILE
    width = heads * head_dim
    hist_dev = events // n_parts
    event = lax.broadcasted_iota(jnp.int32, (events, ROW_TILE), 0)
    feature = lax.broadcasted_iota(jnp.int32, (events, ROW_TILE), 1)
    position = (col_ref[0] - event // hist_dev + n_parts) % n_parts * hist_dev + event % hist_dev
    mask = jnp.where((position >= length_ref[0]) & (feature == 0), -1e30, 0.0)
    for h in range(heads):
        keys = pairs[:, h * head_dim : (h + 1) * head_dim]
        keys_ref[h] = jnp.concatenate([keys, mask], axis=1).astype(jnp.bfloat16)
    values_ref[...] = jnp.transpose(pairs[:, width:]).astype(jnp.bfloat16)
    turned_ref[...] = jnp.transpose(query_ref[...].astype(jnp.float32)).astype(jnp.bfloat16)


def owner_kernel(
    n_lists, user_dev, digits, main, spare, scale, base_ref, other_ref, gathered_ref, items_ref, *refs
):
    loads = []
    if spare:
        sibling_hbm, out_hbm, wide, out_ref, out_sems, sibling_ref, in_sems = refs
        part = sibling_ref.shape[0] // in_sems.shape[0]
        for p in range(in_sems.shape[0]):
            span = pl.ds(p * part, part)
            loads.append(pltpu.make_async_copy(sibling_hbm.at[span], sibling_ref.at[span], in_sems.at[p]))
            loads[-1].start()
    else:
        out_hbm, wide, out_ref, out_sems = refs
    items_loc, width = items_ref.shape
    wide[...] = gathered_ref[...].astype(jnp.float32)
    vectors, ids = unpack(wide, n_lists, user_dev, digits, width // LANES)
    index, own = asked(ids, base_ref[0].astype(jnp.float32), items_loc, 0, main)
    scores = lax.dot_general(
        vectors.astype(jnp.bfloat16),
        items_ref[...],
        (((1,), (1,)), ((), ())),
        preferred_element_type=jnp.float32,
    )
    scores = (scores * scale).astype(jnp.bfloat16)
    pieces = items_loc // width
    stacked = jnp.concatenate(
        [scores[:, piece * width : (piece + 1) * width] for piece in range(pieces)], axis=0
    )
    kept = out_ref.shape[1] - main
    entry = lax.broadcasted_iota(jnp.int32, (n_lists * kept, 1), 0)
    wanted = jnp.where(entry % kept < pieces * user_dev, entry % kept * n_lists + entry // kept, -1)
    spread = jnp.dot(
        picks(wanted, stacked.shape[0]), stacked, preferred_element_type=jnp.float32
    ).astype(jnp.bfloat16)
    out_ref[:, :kept, :] = spread.reshape(n_lists, kept, width)
    if spare:
        over, _ = asked(ids, other_ref[0].astype(jnp.float32), items_loc, main, spare)
        over = [jnp.where(own[r : r + 1] > float(main - spare), -1, over[r]) for r in range(n_lists)]
    step = max(1, 288 // main)
    chunks = [(first, min(n_lists, first + step)) for first in range(0, n_lists, step)]
    sends = []

    def finish(number):
        first, last = chunks[number]
        if spare:
            for r in range(first, last):
                out_ref[r, kept + main - spare :, :] += shared[r * spare : (r + 1) * spare]
        send = pltpu.make_async_copy(out_ref.at[first:last], out_hbm.at[first:last], out_sems.at[number])
        send.start()
        sends.append(send)

    for number, (first, last) in enumerate(chunks):
        rows = jnp.dot(
            picks(jnp.concatenate(index[first:last], axis=0), items_loc),
            items_ref[...],
            preferred_element_type=jnp.float32,
        ).astype(jnp.bfloat16)
        for r in range(first, last):
            out_ref[r, kept:, :] = rows[(r - first) * main : (r - first + 1) * main]
        if number == max(0, len(chunks) - 2):
            if spare:
                for load in loads:
                    load.wait()
                shared = jnp.dot(
                    picks(jnp.concatenate(over, axis=0), items_loc),
                    sibling_ref[...],
                    preferred_element_type=jnp.float32,
                ).astype(jnp.bfloat16)
            for done in range(number + 1):
                finish(done)
        elif number == len(chunks) - 1:
            finish(number)
    for send in sends:
        send.wait()


def spill_kernel(n_lists, user_dev, digits, main, base_ref, gathered_ref, items_ref, spill_ref, wide):
    items_loc, width = items_ref.shape
    spare = spill_ref.shape[1]
    wide[...] = gathered_ref[...].astype(jnp.float32)
    _, ids = unpack(wide, n_lists, user_dev, digits, width // LANES)
    index, _ = asked(ids, base_ref[0].astype(jnp.float32), items_loc, main, spare)
    rows = jnp.dot(
        picks(jnp.concatenate(index, axis=0), items_loc), items_ref[...], preferred_element_type=jnp.float32
    )
    spill_ref[...] = rows.astype(jnp.bfloat16).reshape(spill_ref.shape)


def stay_kernel(came_ref, here_ref):
    here_ref[...] = came_ref[...]


def placed(column, known_ref, slots, fetched_ref, extra_refs, out_ref):
    n_lists, block, width = fetched_ref.shape
    share = out_ref.shape[0]
    slots[...] = jnp.transpose(known_ref[...])
    start = pl.multiple_of(column * share, share)
    slot = slots[pl.ds(start, share), :][:, :1].astype(jnp.int32)
    rows = jnp.dot(
        picks(slot, n_lists * block),
        fetched_ref[...].reshape(n_lists * block, width),
        preferred_element_type=jnp.float32,
    )
    for ref in extra_refs:
        rows = rows + jnp.dot(
            picks(slot - n_lists * block, ref.shape[0]), ref[...], preferred_element_type=jnp.float32
        )
    out_ref[...] = rows.astype(jnp.bfloat16)


def place_kernel(n_users, col_ref, known_ref, fetched_ref, *refs):
    extra_refs, sent_refs, slots = refs[: -n_users], refs[-n_users:-1], refs[-1]
    for shift, ref in enumerate(sent_refs):
        placed((col_ref[0] + shift + 1) % n_users, known_ref, slots, fetched_ref, extra_refs, ref)


def attend_kernel(n_parts, *refs):
    parts, (keys_ref, values_ref, turned_ref, out_weight_ref, out_ref) = refs[:n_parts], refs[n_parts:]
    heads, events, features = keys_ref.shape
    head_dim = features - ROW_TILE
    rows = parts[0][...]
    for part in parts[1:]:
        rows = rows + part[...]
    queries = lax.dot_general(
        turned_ref[...], rows, (((1,), (1,)), ((), ())), preferred_element_type=jnp.float32
    )
    queries = (queries * head_dim ** (-0.5)).astype(jnp.bfloat16)
    feature = lax.broadcasted_iota(jnp.int32, (ROW_TILE, rows.shape[0]), 0)
    one = jnp.where(feature == 0, 1.0, 0.0).astype(jnp.bfloat16)

    def score(h):
        query = jnp.concatenate([queries[h * head_dim : (h + 1) * head_dim], one], axis=0)
        return jnp.dot(keys_ref[h], query, preferred_element_type=jnp.float32)

    ahead = [score(h) for h in range(min(3, heads))]
    mixed = []
    for h in range(heads):
        if h + 3 < heads:
            ahead.append(score(h + 3))
        exponentials = jnp.exp(ahead[h] - jnp.max(ahead[h], axis=0, keepdims=True))
        total = jnp.sum(exponentials, axis=0, keepdims=True)
        span = slice(h * head_dim, (h + 1) * head_dim)
        head = jnp.dot(values_ref[span, :], exponentials.astype(jnp.bfloat16), preferred_element_type=jnp.float32)
        mixed.append(head / total)
    attended = jnp.transpose(jnp.concatenate(mixed, axis=0)).astype(jnp.bfloat16)
    out_ref[...] = jnp.dot(attended, out_weight_ref[...], preferred_element_type=jnp.float32).astype(jnp.bfloat16)


def expand_kernel(user_dev, pieces, kept, col_ref, known_ref, fetched_ref, *refs):
    extra_refs, (out_hbm, own_ref, out_ref, slots, sems) = refs[:-5], refs[-5:]
    n_lists, _, width = fetched_ref.shape
    rows = n_lists * kept
    returned = fetched_ref[:, :kept, :].reshape(rows, width)
    count = out_ref.shape[0]
    probe = jnp.transpose(known_ref[:, :count])[:, 1:2].astype(jnp.int32)
    user = lax.broadcasted_iota(jnp.int32, (count, 1), 0) // (count // user_dev)
    sends = []
    for piece in range(pieces):
        wanted = probe * kept + piece * user_dev + user
        span = pl.ds(piece * width, width)
        out_ref[:, span] = jnp.dot(picks(wanted, rows), returned, preferred_element_type=jnp.float32).astype(
            jnp.bfloat16
        )
        sends.append(pltpu.make_async_copy(out_ref.at[:, span], out_hbm.at[:, span], sems.at[piece]))
        sends[-1].start()
    placed(col_ref[0], known_ref, slots, fetched_ref, extra_refs, own_ref)
    for send in sends:
        send.wait()


SMEM = pl.BlockSpec(memory_space=pltpu.SMEM)
VMEM = pl.BlockSpec(memory_space=pltpu.VMEM)
HBM = pl.BlockSpec(memory_space=pltpu.HBM)
PARAMS = pltpu.CompilerParams(vmem_limit_bytes=VMEM_BYTES)


def exchange(value):
    return lax.all_to_all(value, "lists", split_axis=0, concat_axis=0, tiled=True)


def shards(
    user_vectors,
    probe_lists,
    list_items,
    candidate_ids,
    history,
    history_lengths,
    query_weight,
    key_value_weight,
    out_weight,
):
    n_lists = lax.axis_size("lists")
    n_users = lax.axis_size("users")
    _, items_loc, width = list_items.shape
    user_dev, probes = probe_lists.shape
    _, cands = candidate_ids.shape
    bf16 = jnp.bfloat16
    cap = max(2, 3 * cands // (n_lists * n_users))
    cap = round_up(cap, ROW_TILE)
    kept = round_up(items_loc // width * user_dev, ROW_TILE)
    share = cands // n_users
    pieces = items_loc // width
    digits = 1
    while BASE**digits < n_lists * n_users * items_loc:
        digits += 1
    pack_rows = round_up((user_dev + digits) * (width // LANES), 8)
    line = lax.axis_index("lists").astype(jnp.int32)
    col = lax.axis_index("users").astype(jnp.int32)
    col_arg = col.reshape(1)
    line_arg = line.reshape(1)
    base_arg = ((line * n_users + col) * items_loc).reshape(1)
    other_arg = ((line * n_users + n_users - 1 - col) * items_loc).reshape(1)
    spare = 8 if n_users == 2 and cap >= 48 else 0
    main = cap - spare
    block = main + kept

    flat_items = list_items.reshape(items_loc, width)
    pack = pl.pallas_call(
        functools.partial(pack_kernel, digits),
        out_shape=jax.ShapeDtypeStruct((n_lists, pack_rows, LANES), bf16),
        in_specs=[VMEM, VMEM],
        out_specs=VMEM,
        compiler_params=pltpu.CompilerParams(vmem_limit_bytes=ALL_VMEM_BYTES),
    )(candidate_ids, user_vectors)
    gathered = exchange(pack)
    gathered = gathered.reshape(n_lists * pack_rows, LANES)

    items = pl.pallas_call(
        items_kernel,
        out_shape=jax.ShapeDtypeStruct((items_loc, width), bf16),
        in_specs=[HBM],
        out_specs=VMEM,
        scratch_shapes=[pltpu.SemaphoreType.DMA((4,))],
        compiler_params=PARAMS,
    )(flat_items)
    gathered, items = lax.optimization_barrier((gathered, items))

    siblings = []
    if spare:
        siblings.append(lax.ppermute(flat_items, "users", [(0, 1), (1, 0)]))

    known, many, gathered_copy = pl.pallas_call(
        functools.partial(known_kernel, n_lists, items_loc, n_users, user_dev, digits, main, spare, kept),
        out_shape=(
            jax.ShapeDtypeStruct((8, cands), jnp.float32),
            jax.ShapeDtypeStruct((1,), jnp.int32),
            jax.ShapeDtypeStruct(gathered.shape, bf16),
        ),
        in_specs=[SMEM, SMEM, VMEM, VMEM, VMEM],
        out_specs=(VMEM, SMEM, VMEM),
        scratch_shapes=[pltpu.VMEM((n_lists * pack_rows, LANES), jnp.float32)],
        compiler_params=PARAMS,
    )(line_arg, col_arg, candidate_ids, probe_lists, gathered)

    extras = []
    if spare:

        def spill_apart():
            spill = pl.pallas_call(
                functools.partial(spill_kernel, n_lists, user_dev, digits, main),
                out_shape=jax.ShapeDtypeStruct((n_lists, spare, width), bf16),
                in_specs=[SMEM, VMEM, VMEM],
                out_specs=VMEM,
                scratch_shapes=[pltpu.VMEM((n_lists * pack_rows, LANES), jnp.float32)],
                compiler_params=PARAMS,
            )(base_arg, gathered_copy, flat_items)
            spill = spill[jnp.arange(n_lists, dtype=jnp.int32) ^ line]
            blocks = [spill[:1]]
            for k in range(1, n_lists):
                blocks.append(lax.ppermute(spill[k : k + 1], "lists", [(i, i ^ k) for i in range(n_lists)]))
            return jnp.concatenate(blocks, axis=0).reshape(n_lists * spare, width)

        came = lax.cond(many[0] > 0, spill_apart, lambda: jnp.zeros((n_lists * spare, width), bf16))
        extras.append(
            pl.pallas_call(
                stay_kernel,
                out_shape=jax.ShapeDtypeStruct(came.shape, bf16),
                in_specs=[VMEM],
                out_specs=VMEM,
                compiler_params=PARAMS,
            )(came)
        )

    events = history.reshape(-1, width)
    hist = [events]
    for shift in range(1, n_users):
        hist.append(lax.ppermute(events, "users", [(i, (i + shift) % n_users) for i in range(n_users)]))
    total_events = n_users * events.shape[0]
    keys, values, turned = pl.pallas_call(
        functools.partial(pairs_kernel, n_users),
        out_shape=(
            jax.ShapeDtypeStruct((HEADS, total_events, width // HEADS + ROW_TILE), bf16),
            jax.ShapeDtypeStruct((width, total_events), bf16),
            jax.ShapeDtypeStruct((width, width), bf16),
        ),
        in_specs=[SMEM, SMEM] + [VMEM] * (n_users + 2),
        out_specs=(VMEM, VMEM, VMEM),
        compiler_params=PARAMS,
    )(col_arg, history_lengths, *hist, key_value_weight, query_weight)

    step = max(1, 288 // main)
    answers = pl.pallas_call(
        functools.partial(owner_kernel, n_lists, user_dev, digits, main, spare, width ** (-0.5)),
        out_shape=jax.ShapeDtypeStruct((n_lists, block, width), bf16),
        in_specs=[SMEM, SMEM, VMEM, VMEM] + [pl.BlockSpec(memory_space=pl.ANY)] * len(siblings),
        out_specs=pl.BlockSpec(memory_space=pl.ANY),
        scratch_shapes=[
            pltpu.VMEM((n_lists * pack_rows, LANES), jnp.float32),
            pltpu.VMEM((n_lists, block, width), bf16),
            pltpu.SemaphoreType.DMA((-(-n_lists // step),)),
        ]
        + [pltpu.VMEM((items_loc, width), bf16), pltpu.SemaphoreType.DMA((4,))] * len(siblings),
        compiler_params=PARAMS,
    )(base_arg, other_arg, gathered, items, *siblings)
    fetched = exchange(answers)

    fetched, known, extras, keys, values, turned = lax.optimization_barrier(
        (fetched, known, extras, keys, values, turned)
    )

    sent = []
    if n_users > 1:
        sent = pl.pallas_call(
            functools.partial(place_kernel, n_users),
            out_shape=tuple(jax.ShapeDtypeStruct((share, width), bf16) for _ in range(n_users - 1)),
            in_specs=[SMEM, VMEM, VMEM] + [VMEM] * len(extras),
            out_specs=tuple(VMEM for _ in range(n_users - 1)),
            scratch_shapes=[pltpu.VMEM((cands, 8), jnp.float32)],
            compiler_params=PARAMS,
        )(col_arg, known, fetched, *extras)
    parts = []
    for shift in range(1, n_users):
        parts.append(
            lax.ppermute(sent[shift - 1], "users", [(i, (i + shift) % n_users) for i in range(n_users)])
        )

    list_scores, own = pl.pallas_call(
        functools.partial(expand_kernel, user_dev, pieces, kept),
        out_shape=(
            jax.ShapeDtypeStruct((user_dev * probes, items_loc), bf16),
            jax.ShapeDtypeStruct((share, width), bf16),
        ),
        in_specs=[SMEM, VMEM, VMEM] + [VMEM] * len(extras),
        out_specs=(pl.BlockSpec(memory_space=pl.ANY), VMEM),
        scratch_shapes=[
            pltpu.VMEM((user_dev * probes, items_loc), bf16),
            pltpu.VMEM((cands, 8), jnp.float32),
            pltpu.SemaphoreType.DMA((pieces,)),
        ],
        compiler_params=PARAMS,
    )(col_arg, known, fetched, *extras)
    ranked = pl.pallas_call(
        functools.partial(attend_kernel, n_users),
        out_shape=jax.ShapeDtypeStruct((share, width), bf16),
        in_specs=[VMEM] * (n_users + 4),
        out_specs=VMEM,
        compiler_params=PARAMS,
    )(own, *parts, keys, values, turned, out_weight)
    return (list_scores.reshape(user_dev, probes, items_loc), ranked.reshape(1, share, width))


def solution(mesh):
    placed = (
        P("lists", None),
        P("lists", None),
        P("lists", "users", None),
        P("lists", None),
        P("lists", "users", None),
        P("lists"),
        P(),
        P(),
        P(),
    )
    return jax.shard_map(
        shards,
        mesh=mesh,
        in_specs=placed,
        out_specs=(P("lists", None, "users"), P("lists", "users", None)),
        check_vma=False,
    )
```
